128 devices in a mesh: dp: 16 (over x_lo, z, core), mp: 8 (over x_hi, y).
Axes of the slice: x: 4 (x_hi: 2, x_lo: 2; x = x_hi * 2 + x_lo), y: 4, z: 4, core: 2. Of those that a mesh axis runs over, the one named last changes fastest.
Arguments:
- tokens: bfloat16 [16384, 2048], P('dp'), may hold values from -6 to 6
- lengths: int32 [16, 4], P('dp'), may hold values from 0 to 1024, as said below
- ln1_gain: float32 [2048], replicated, may hold values from 0.1 to 1.9
- ln1_bias: float32 [2048], replicated, may hold values from -4 to 4
- ln2_gain: float32 [2048], replicated, may hold values from 0.1 to 1.9
- ln2_bias: float32 [2048], replicated, may hold values from -4 to 4
- qkv_master: float32 [2048, 3, 2048], P(None, None, 'mp'), may hold values from -0.125 to 0.125
- qkv_bias: float32 [3, 2048], P(None, 'mp'), may hold values from -6 to 6
- out_master: float32 [2048, 2048], P('mp'), may hold values from -0.75 to 0.75
- up_master: float32 [2048, 8192], P(None, 'mp'), may hold values from -0.125 to 0.125
- up_bias: float32 [8192], P('mp'), may hold values from -6 to 6
- down_master: float32 [8192, 2048], P('mp'), may hold values from -0.0625 to 0.0625
- branch_bias: float32 [2048], replicated, may hold values from -4 to 4
- cotangent: bfloat16 [16384, 2048], P('dp'), may hold values from -6 to 6
Outputs:
- output: bfloat16 [16384, 2048], P('dp')
- grad_tokens: bfloat16 [16384, 2048], P('dp')
- grad_ln1_gain: float32 [2048], P('mp')
- grad_ln1_bias: float32 [2048], P('mp')
- grad_ln2_gain: float32 [2048], P('mp')
- grad_ln2_bias: float32 [2048], P('mp')
- grad_qkv: float32 [2048, 3, 2048], P('dp', None, 'mp')
- grad_qkv_bias: float32 [3, 2048], P(None, 'mp')
- grad_out: float32 [2048, 2048], P('mp', 'dp')
- grad_up: float32 [2048, 8192], P('dp', 'mp')
- grad_up_bias: float32 [8192], P('mp')
- grad_down: float32 [8192, 2048], P('mp', 'dp')
- grad_branch_bias: float32 [2048], P('mp')
The draws below stay inside these ranges and needn't reach their ends.
Inputs may be any that keep to these rules, and one draw needn't show every extreme that they name: Row r of lengths describes bucket r: its sequences lie end to end from the bucket's first row in slot order and the rest of its 1024 rows are padding; a slot may be empty (length 0); each bucket's lengths sum to 512 or more; some bucket holds one sequence of exactly 1024.
All inputs are finite; a program needn't handle non-finite values.
Results may differ from the reference program's by a relative error of at most 0.012.
The reference program's roundings to bfloat16 on the way count: a program that leaves them out, or rounds other values in their place, can miss the bound.
Values may be sent and summed in bfloat16 or wider, within the bound.
A program may use at most 256 MiB of HBM per device.

```python
import math
from functools import partial
import jax
import jax.numpy as jnp
from jax import lax

D = 2048
HEADS = 8
HS = 256
ROT = 64
FF = 8192
TOK_DP = 1024
SEQS = 4
TOKENS = 16384
BUCKETS = 16


def draw_lengths(key, part):
    key = jax.random.fold_in(key, 11)
    full_key, rest_key = jax.random.split(key)
    full_row = jax.random.randint(full_key, (), 0, BUCKETS)

    def one_bucket(row_key):
        total_key, number_key, cut_key = jax.random.split(row_key, 3)
        used = jax.random.randint(total_key, (), TOK_DP // 2, TOK_DP + 1)
        number = jax.random.randint(number_key, (), 1, SEQS + 1)
        cuts = jax.random.randint(cut_key, (SEQS - 1,), 0, used + 1)
        cuts = jnp.where(jnp.arange(SEQS - 1) < number - 1, cuts, used)
        cuts = jnp.sort(cuts)
        bounds = jnp.concatenate([jnp.zeros((1,), jnp.int32), cuts.astype(jnp.int32), used[None].astype(jnp.int32)])
        return (bounds[1:] - bounds[:-1]).astype(jnp.int32)
    buckets = jax.vmap(one_bucket)(jax.random.split(rest_key, BUCKETS))
    single = jnp.zeros((SEQS,), jnp.int32).at[0].set(TOK_DP)
    return jnp.where((jnp.arange(BUCKETS) == full_row)[:, None], single[None, :], buckets).astype(jnp.int32)


def spiked(values, stream_key, source, target, parts, factor):
    owner, partner = [(jnp.arange(values.shape[dim]) // (values.shape[dim] // parts)).reshape([-1 if axis == dim else 1 for axis in range(values.ndim)]) for dim in (source, target)]
    chosen = jax.random.permutation(stream_key, parts)[partner]
    strong = (owner == chosen) | (owner == (partner + parts // 2) % parts)
    return jnp.where(strong, factor * values, values)


def block_scale(key, extent, cuts, smallest, largest):
    def one(dim, shards_of):
        steps = jax.random.uniform(jax.random.fold_in(jax.random.fold_in(key, 6), dim), (shards_of,), jnp.float32, smallest / len(cuts), largest / len(cuts))
        return jnp.repeat(jnp.exp(steps), extent[dim] // shards_of).reshape((-1,) + (1,) * (len(extent) - dim - 1))

    factor_of = one(*cuts[0])
    for cut in cuts[1:]:
        factor_of = factor_of * one(*cut)
    return factor_of


def normal_values(own_key, dims, scale, bound, shards=(), kind=jnp.bfloat16):
    loudness = block_scale(own_key, dims, shards, -0.22, 0.18) if shards else 1.0
    array = jax.random.normal(own_key, dims, jnp.float32) * scale * loudness
    return jnp.minimum(jnp.maximum(array, -bound), bound).astype(kind)


def bell_draw_with(stream_key, shape, scale, limit, shards, heavy, kind=jnp.bfloat16):
    entries = scale * jax.random.normal(stream_key, shape, jnp.float32)
    if shards:
        entries = entries * block_scale(stream_key, shape, shards, -0.22, 0.18)
    return jnp.clip(spiked(entries, jax.random.fold_in(stream_key, 3), *heavy), -limit, limit).astype(kind)


def setup_inputs(seed: int = 0) -> dict:
    key_list = jax.random.split(jax.random.key(seed), 15)
    tokens = normal_values(key_list[0], (TOKENS, D), 1.0, 6.0, ((0, 16),))
    lengths = draw_lengths(jax.random.fold_in(key_list[14], 71), 0)
    ln1_gain = jnp.clip(1.0 + 0.18 * jax.random.normal(key_list[2], (D,), jnp.float32), 0.1, 1.9)
    ln1_bias = normal_values(key_list[3], (D,), 0.3, 4.0, (), jnp.float32)
    ln2_gain = jnp.clip(1.0 + 0.18 * jax.random.normal(key_list[4], (D,), jnp.float32), 0.1, 1.9)
    ln2_bias = normal_values(key_list[5], (D,), 0.3, 4.0, (), jnp.float32)
    qkv_master = normal_values(key_list[6], (D, 3, HEADS * HS), D ** -0.5, 0.125, ((2, 8),), jnp.float32)
    qkv_bias = normal_values(key_list[7], (3, HEADS * HS), 0.5, 6.0, ((1, 8),), jnp.float32)
    out_master = normal_values(key_list[8], (HEADS * HS, D), (HEADS * HS // 32 + 2) ** -0.5, 0.75, ((0, 8),), jnp.float32)
    up_master = normal_values(key_list[9], (D, FF), D ** -0.5, 0.125, ((1, 8),), jnp.float32)
    up_bias = normal_values(key_list[10], (FF,), 0.5, 6.0, ((0, 8),), jnp.float32)
    down_master = normal_values(key_list[11], (FF, D), FF ** -0.5, 0.0625, ((0, 8),), jnp.float32)
    branch_bias = normal_values(key_list[12], (D,), 0.3, 4.0, (), jnp.float32)
    cotangent = bell_draw_with(key_list[13], (TOKENS, D), 1.0, 6.0, ((0, 16),), (0, 1, 16, 2.0))
    return {"tokens": tokens, "lengths": lengths, "ln1_gain": ln1_gain, "ln1_bias": ln1_bias, "ln2_gain": ln2_gain, "ln2_bias": ln2_bias, "qkv_master": qkv_master, "qkv_bias": qkv_bias, "out_master": out_master, "up_master": up_master, "up_bias": up_bias, "down_master": down_master, "branch_bias": branch_bias, "cotangent": cotangent}


@jax.custom_vjp
def low(v):
    return lax.optimization_barrier(v.astype(jnp.bfloat16)).astype(jnp.float32)

@jax.custom_vjp
def low_back(v):
    return v

def low_keep(v):
    return (low(v), None)

def low_pass(kept, grad):
    return (grad,)

def back_keep(v):
    return (v, None)

def back_low(kept, grad):
    return (low(grad),)
low.defvjp(low_keep, low_pass)
low_back.defvjp(back_keep, back_low)
highest = lax.Precision.HIGHEST
norm_eps = 1e-05
masked_value = -1e+30

def matmul(first_mat, second_mat):
    return jnp.dot(first_mat, second_mat, precision=highest, preferred_element_type=jnp.float32)

def layout(seq_lengths, row_count):
    seq_ends = jnp.cumsum(seq_lengths).astype(jnp.int32)
    seq_starts = (seq_ends - seq_lengths).astype(jnp.int32)
    token_index = jnp.arange(row_count, dtype=jnp.int32)
    segment = lax.optimization_barrier(jnp.sum((token_index[:, None] >= seq_ends[None, :]).astype(jnp.int32), axis=1)).astype(jnp.int32)
    slot_ids = jnp.arange(seq_lengths.shape[0], dtype=jnp.int32)
    seq_first = lax.optimization_barrier(jnp.sum(jnp.where(segment[:, None] == slot_ids[None, :], seq_starts[None, :], 0), axis=1)).astype(jnp.int32)
    return (segment, (token_index - seq_first).astype(jnp.int32))

def angles(position):
    inv_freq = jnp.exp(jnp.arange(ROT // 2, dtype=jnp.float32) * (-2.0 * math.log(10000.0) / ROT))
    phases = position.astype(jnp.float32)[:, None] * inv_freq[None, :]
    return (jnp.cos(phases)[:, None, :], jnp.sin(phases)[:, None, :])

def rotate(heads_in, cos_of, sin_of):
    half_rot = ROT // 2
    low_half = heads_in[..., :half_rot]
    high_half = heads_in[..., half_rot:ROT]
    return jnp.concatenate([low_half * cos_of - high_half * sin_of, high_half * cos_of + low_half * sin_of, heads_in[..., ROT:]], axis=-1)

def forward(segment, position, inputs, ln1_gain, ln1_bias, ln2_gain, ln2_bias, qkv_master, qkv_bias, out_master, up_master, up_bias, down_master, branch_bias):
    row_count = inputs.shape[0]
    valid_rows = (segment < SEQS).astype(jnp.float32)[:, None]
    row_mean = lax.optimization_barrier(jnp.mean(inputs, axis=-1, keepdims=True))
    centred = inputs - row_mean
    row_var = lax.optimization_barrier(jnp.mean(centred * centred, axis=-1, keepdims=True))
    normed = centred * lax.rsqrt(row_var + norm_eps)
    attn_in = low(normed * ln1_gain + ln1_bias)
    mlp_in = low(normed * ln2_gain + ln2_bias)
    projected = low_back(matmul(attn_in, low(qkv_master).reshape(D, 3 * HEADS * HS)) + qkv_bias.reshape(3 * HEADS * HS))
    projected = projected.reshape(row_count, 3, HEADS, HS)
    cos_of, sin_of = angles(position)
    query = low(rotate(projected[:, 0], cos_of, sin_of))
    keys = low(rotate(projected[:, 1], cos_of, sin_of))
    values = low(projected[:, 2])
    token_index = jnp.arange(row_count, dtype=jnp.int32)
    allowed = (segment[:, None] == segment[None, :]) & (token_index[:, None] >= token_index[None, :])
    scores = low_back(jnp.einsum('qhd,khd->hqk', query, keys, precision=highest) * (1.0 / math.sqrt(HS)))
    probs_low = low(jax.nn.softmax(jnp.where(allowed[None], scores, masked_value), axis=-1))
    mixed = low(low_back(jnp.einsum('hqk,khd->qhd', probs_low, values, precision=highest)))
    attention = matmul(mixed.reshape(row_count, HEADS * HS), low(out_master))
    up_pre = low_back(matmul(mlp_in, low(up_master)) + up_bias)
    activation = low(jax.nn.gelu(up_pre, approximate=False))
    feed = matmul(activation, low(down_master))
    return valid_rows * (inputs + attention + feed + branch_bias)

def reference(tokens, lengths, ln1_gain, ln1_bias, ln2_gain, ln2_bias, qkv_master, qkv_bias, out_master, up_master, up_bias, down_master, branch_bias, cotangent):
    parameters = (ln1_gain, ln1_bias, ln2_gain, ln2_bias, qkv_master, qkv_bias, out_master, up_master, up_bias, down_master, branch_bias)

    def one_row(totals, row_data):
        row_tokens, seq_lengths, row_cotangent = row_data
        segment, position = layout(seq_lengths.astype(jnp.int32), TOK_DP)
        result, pullback = jax.vjp(partial(forward, segment, position), row_tokens.astype(jnp.float32), *parameters)
        gradients = pullback(row_cotangent.astype(jnp.float32))
        totals = tuple((running + gradient for running, gradient in zip(totals, gradients[1:])))
        return (totals, (result.astype(jnp.bfloat16), gradients[0].astype(jnp.bfloat16)))
    zero_grads = tuple((jnp.zeros_like(parameter) for parameter in parameters))
    totals, (outputs, input_grads) = lax.scan(one_row, zero_grads, (tokens.reshape(BUCKETS, TOK_DP, D), lengths, cotangent.reshape(BUCKETS, TOK_DP, D)))
    return (outputs.reshape(TOKENS, D), input_grads.reshape(TOKENS, D), totals[0], totals[1], totals[2], totals[3], totals[4], totals[5], totals[6], totals[7], totals[8], totals[9], totals[10])
```

```python
import functools
import math

import jax
import jax.numpy as jnp
import numpy as np
from jax import lax
from jax.experimental import pallas as pl
from jax.experimental.pallas import tpu as pltpu
from jax.sharding import PartitionSpec as P

HS = 256
ROT = 64
BLK = 256
HALF = 128
SUB = 64
LEFT_COLS = 1152
MESH = pl.DeviceIdType.MESH
MIB = 2**20
norm_eps = 1e-05
masked_value = -1e30
f32 = jnp.float32
bf16 = jnp.bfloat16


def dot_nn(a, b):
    return jnp.dot(a, b, preferred_element_type=f32)


def dot_nt(a, b):
    return lax.dot_general(a, b, (((1,), (1,)), ((), ())), preferred_element_type=f32)


def dot_tn(a, b):
    return lax.dot_general(a, b, (((0,), (0,)), ((), ())), preferred_element_type=f32)


def aligned(start, size, unit=None):
    if isinstance(start, int):
        return pl.ds(start, size)
    return pl.ds(pl.multiple_of(start, unit or size), size)


class Place:
    def __init__(self):
        self.dp = lax.axis_index("dp")
        self.mp = lax.axis_index("mp")
        self.x_hi = self.mp // 4
        self.y = self.mp % 4
        self.x_lo = self.dp // 8
        self.z = (self.dp // 2) % 4
        self.core = self.dp % 2

    def y_at(self, off):
        return (self.y + off) % 4

    def z_at(self, off):
        return (self.z + off) % 4

    def to_y(self, y):
        return (self.dp, self.x_hi * 4 + y)

    def ring_y(self):
        right, left = self.y_at(1), self.y_at(3)
        return self.y, right, self.y_at(2), left, self.to_y(right), self.to_y(left)

    def ring_z(self):
        right, left = self.z_at(1), self.z_at(3)
        return self.z, right, self.z_at(2), left, self.to_z(right), self.to_z(left)

    def to_x_hi(self):
        return (self.dp, (1 - self.x_hi) * 4 + self.y)

    def to_z(self, z):
        return ((self.x_lo * 4 + z) * 2 + self.core, self.mp)

    def to_x_lo(self):
        return (((1 - self.x_lo) * 4 + self.z) * 2 + self.core, self.mp)

    def to_core(self):
        return ((self.x_lo * 4 + self.z) * 2 + 1 - self.core, self.mp)


def greet(targets):
    barrier = pltpu.get_barrier_semaphore()
    for target in targets:
        pl.semaphore_signal(barrier, inc=1, device_id=target, device_id_type=MESH)
    pl.semaphore_wait(barrier, len(targets))


class Link:
    def __init__(self, sems, number, src, dst, target):
        self.copy = pltpu.make_async_remote_copy(
            src_ref=src,
            dst_ref=dst,
            send_sem=sems.at[0, number],
            recv_sem=sems.at[1, number],
            device_id=target,
            device_id_type=MESH,
        )

    def start(self):
        self.copy.start()

    def got(self):
        self.copy.wait_recv()

    def sent(self):
        self.copy.wait_send()


class RingSum:
    def __init__(self, ring, src, rows, cols, buf, sems, base):
        self.src, self.rows, self.cols, self.buf = src, rows, cols, buf
        self.own, self.right, self.opp, self.left, to_right, to_left = ring
        part = self.part
        self.links = [
            Link(sems, base + 0, part(self.opp, 0), buf.at[0], to_right),
            Link(sems, base + 1, part(self.opp, 1), buf.at[1], to_left),
            Link(sems, base + 2, part(self.right, 0), buf.at[2], to_right),
            Link(sems, base + 3, part(self.right, 1), buf.at[3], to_right),
            Link(sems, base + 4, part(self.left, 1), buf.at[4], to_left),
            Link(sems, base + 5, part(self.left, 0), buf.at[5], to_left),
        ]

    def part(self, place, half):
        return self.src.at[self.rows(place, half), self.cols]

    def send_opp(self):
        self.links[0].start()
        self.links[1].start()

    def send_right(self):
        self.links[3].start()

    def send_left(self):
        self.links[5].start()

    def relay(self):
        for number, place, half in ((0, self.right, 0), (1, self.left, 1)):
            self.links[number].got()
            rows = self.rows(place, half)
            self.src[rows, self.cols] = (
                self.src[rows, self.cols].astype(f32) + self.buf[number].astype(f32)
            ).astype(bf16)
            self.links[2 if number == 0 else 4].start()

    def total(self, half):
        one, two = (2, 5) if half == 0 else (4, 3)
        self.links[one].got()
        self.links[two].got()
        own = self.src[self.rows(self.own, half), self.cols].astype(f32)
        return own + self.buf[one].astype(f32) + self.buf[two].astype(f32)

    def finish(self):
        for link in self.links:
            link.sent()


class BucketSum:
    LINKS = 17

    def __init__(self, here, src, buf_wide, buf_cut, buf_x, buf_far, stage, sems, width):
        self.here, self.src, self.buf_x, self.buf_far, self.stage = here, src, buf_x, buf_far, stage
        self.wide = pl.ds(0, width)
        self.cut, self.rest = pl.ds(0, LEFT_COLS), pl.ds(LEFT_COLS, width - LEFT_COLS)
        self.first_own = lambda y: y * BLK + here.x_hi * HALF
        self.first_far = lambda y: y * BLK + (1 - here.x_hi) * HALF
        halves = lambda first: lambda y, half: aligned(first(y) + half * SUB, SUB)
        self.far = RingSum(here.ring_y(), src, halves(self.first_far), self.cut, buf_cut, sems, 0)
        self.near = RingSum(here.ring_y(), src, halves(self.first_own), self.wide, buf_wide, sems, 6)
        self.across = [
            Link(
                sems,
                12 + off,
                src.at[aligned(self.first_far(here.y_at(off)), HALF), self.rest],
                buf_x.at[off],
                here.to_x_hi(),
            )
            for off in range(4)
        ]
        self.last = Link(sems, 16, stage, buf_far, here.to_x_hi())

    def add_across(self, off):
        self.across[off].got()
        rows = aligned(self.first_own(self.here.y_at(off)), HALF)
        self.src[rows, self.rest] = (
            self.src[rows, self.rest].astype(f32) + self.buf_x[off].astype(f32)
        ).astype(bf16)

    def pass_far(self):
        for half in range(2):
            self.stage[pl.ds(half * SUB, SUB), :] = self.far.total(half).astype(bf16)
        self.last.start()

    def finish(self):
        self.far.finish()
        self.near.finish()
        for link in self.across:
            link.sent()
        self.last.sent()


def gelu_parts(v):
    cdf = 0.5 * (1.0 + lax.erf(v * (1.0 / math.sqrt(2.0))))
    slope = cdf + v * (jnp.exp(-0.5 * v * v) * (1.0 / math.sqrt(2.0 * math.pi)))
    return v * cdf, slope


def row_stats(load, width):
    tiles = width // 128
    total = load(0)
    for tile in range(1, tiles):
        total = total + load(tile)
    mean = jnp.sum(total, axis=-1, keepdims=True) * (1.0 / width)
    square = jnp.zeros_like(total)
    for tile in range(tiles):
        centred = load(tile) - mean
        square = square + centred * centred
    var = jnp.sum(square, axis=-1, keepdims=True) * (1.0 / width)
    return mean, lax.rsqrt(var + norm_eps)


def front_kernel(
    lens, tok, cot, lnp, turn, freq, wq, bq, wo, wu, bu, wd, bb,
    a_o, b_o, e_o, g_o, du_o, dp_o, o_o, s_o, rows_o, vec_o,
    tok_v, a_v, b_v, e_v, wq_v, wo_v, wu_v, wd_v, st, qkv_v, dkv, o_v, do_v, tabs, mean_v, rstd_v,
    g_v, du_v, buf_wide, buf_cut, buf_x, buf_far, stage, x_own,
    in_sems, st_sems, out_sems, sems,
):
    here = Place()
    rows_all, width = tok_v.shape
    hidden = wu_v.shape[1]
    blocks = rows_all // BLK
    scale = 1.0 / math.sqrt(HS)

    def block_of(i):
        return pl.ds(i * BLK, BLK)

    tok_in = [pltpu.make_async_copy(tok.at[block_of(i)], tok_v.at[block_of(i)], in_sems.at[i]) for i in range(blocks)]
    cot_in = [pltpu.make_async_copy(cot.at[block_of(i)], e_v.at[block_of(i)], in_sems.at[blocks + i]) for i in range(blocks)]
    own_first = here.y * BLK + here.x_hi * HALF
    own_rows = aligned(own_first, HALF)
    x_in = pltpu.make_async_copy(tok.at[own_rows], x_own, in_sems.at[2 * blocks])
    q_in = [pltpu.make_async_copy(wq.at[j], st.at[j], st_sems.at[j]) for j in range(3)]
    wo_in = [
        pltpu.make_async_copy(wo.at[:, pl.ds(k * HS, HS)], st.at[0, pl.ds(k * HS, HS)], st_sems.at[3 + k])
        for k in range(width // HS)
    ]
    up_slot = (1, 2, 0, 1)
    wu_in = [
        pltpu.make_async_copy(wu.at[:, pl.ds(k * HS, HS)], st.at[up_slot[k]], st_sems.at[11 + k])
        for k in range(hidden // HS)
    ]
    down_slot = (2, 2, 0, 0, 1, 1, 2, 2)
    wd_in = [
        pltpu.make_async_copy(
            wd.at[:, pl.ds(k * HS, HS)], st.at[down_slot[k], pl.ds((k % 2) * hidden, hidden)], st_sems.at[15 + k]
        )
        for k in range(width // HS)
    ]
    tok_in[0].start()
    for copy in q_in:
        copy.start()
    for copy in tok_in[1:] + cot_in + [x_in]:
        copy.start()

    end = []
    for j in range(4):
        end.append(lens[0, j] + (end[-1] if j else 0))

    def first_of(t):
        low = jnp.zeros_like(t)
        for j in range(4):
            low = jnp.where(t >= end[j], end[j], low)
        return low

    starts = [jnp.int32(0)] + end[:3]
    lane_row = lax.broadcasted_iota(jnp.int32, (8, 128), 0)
    shift = jnp.zeros((8, 128), jnp.int32)
    for j in range(4):
        shift = jnp.where(lane_row == j, starts[j], shift)
    phase = shift.astype(f32) * freq[...]
    shift_cos, shift_sin = jnp.cos(phase), jnp.sin(phase)

    @pl.loop(0, rows_all // HALF)
    def _(i):
        rows = aligned(i * HALF, HALF)
        t = lax.broadcasted_iota(jnp.int32, (HALF, 128), 0) + i * HALF
        lane = lax.broadcasted_iota(jnp.int32, (HALF, 128), 1)
        c_of = jnp.broadcast_to(shift_cos[0:1], (HALF, 128))
        s_of = jnp.broadcast_to(shift_sin[0:1], (HALF, 128))
        for j in range(1, 4):
            c_of = jnp.where(t >= end[j - 1], shift_cos[j : j + 1], c_of)
            s_of = jnp.where(t >= end[j - 1], shift_sin[j : j + 1], s_of)
        c_of = jnp.where(t >= end[3], shift_cos[4:5], c_of)
        s_of = jnp.where(t >= end[3], shift_sin[4:5], s_of)
        t_cos, t_sin = turn[0, rows], turn[1, rows]
        cos_of = t_cos * c_of + t_sin * s_of
        sin_of = t_sin * c_of - t_cos * s_of
        tabs[0, rows] = cos_of
        tabs[1, rows] = jnp.where(lane < ROT // 2, -sin_of, 0.0)
        tabs[2, rows] = jnp.where((lane >= ROT // 2) & (lane < ROT), sin_of, 0.0)

    chunk = 64

    @pl.loop(0, blocks)
    def _(i):
        pltpu.make_async_copy(tok.at[aligned(i * BLK, BLK)], tok_v.at[aligned(i * BLK, BLK)], in_sems.at[i]).wait()

        @pl.loop(0, BLK // chunk)
        def _(c):
            rows = aligned(i * BLK + c * chunk, chunk)

            def load(tile):
                return tok_v[rows, pl.ds(tile * 128, 128)].astype(f32)

            mean, rstd = row_stats(load, width)
            mean_v[rows] = mean
            rstd_v[rows] = rstd
            for tile in range(width // 128):
                cols = pl.ds(tile * 128, 128)
                normed = (load(tile) - mean) * rstd
                a_v[rows, cols] = (normed * lnp[0:1, cols] + lnp[1:2, cols]).astype(bf16)
                b_v[rows, cols] = (normed * lnp[2:3, cols] + lnp[3:4, cols]).astype(bf16)

    a_out = pltpu.make_async_copy(a_v, a_o, out_sems.at[0])
    b_out = pltpu.make_async_copy(b_v, b_o, out_sems.at[1])
    a_out.start()
    b_out.start()

    def cast(dst, cols, slot, rows_from, rows_count, step=256):
        @pl.loop(0, rows_count // step)
        def _(i):
            dst[aligned(i * step, step), cols] = st[slot, aligned(rows_from + i * step, step), :].astype(bf16)

    for j in range(3):
        q_in[j].wait()
        cast(wq_v, pl.ds(j * HS, HS), j, 0, width)
        if j == 0:
            for copy in wo_in:
                copy.start()
        else:
            wu_in[j - 1].start()

    def turned(wide, sign, rows):
        low = wide[:, :128]
        low = low * tabs[0, rows] + sign * (
            pltpu.roll(low, 128 - ROT // 2, 1) * tabs[1, rows] + pltpu.roll(low, ROT // 2, 1) * tabs[2, rows]
        )
        return jnp.concatenate([low, wide[:, 128:]], axis=1)

    @pl.loop(0, 2)
    def _(j):
        cols = aligned(j * HS, HS)
        out = dot_nn(a_v[...], wq_v[:, cols]) + bq[:, cols]
        qkv_v[:, cols] = turned(out, 1.0, slice(None)).astype(bf16)

    qkv_v[:, 2 * HS :] = (dot_nn(a_v[...], wq_v[:, 2 * HS :]) + bq[:, 2 * HS :]).astype(bf16)

    for copy in wo_in:
        copy.wait()
    for k in range(width // HS):
        cols = pl.ds(k * HS, HS)
        wo_v[:, cols] = st[0, cols, :].astype(bf16)
    wu_in[2].start()
    esum = jnp.zeros((1, width), f32)
    for i in range(blocks):
        cot_in[i].wait()
    vec_o[...] = jnp.zeros_like(vec_o)

    @pl.loop(0, blocks)
    def _(i):
        rows = aligned(i * BLK, BLK)
        t = lax.broadcasted_iota(jnp.int32, (BLK, 1), 0) + i * BLK
        used = (t < end[3]).astype(f32)
        for tile in range(width // 512):
            cols = pl.ds(tile * 512, 512)
            kept = e_v[rows, cols].astype(f32) * used
            e_v[rows, cols] = kept.astype(bf16)
            vec_o[4:5, cols] += jnp.sum(kept, axis=0, keepdims=True)

    e_out = pltpu.make_async_copy(e_v, e_o, out_sems.at[2])
    e_out.start()
    do_v[...] = dot_nt(e_v[...], wo_v[...]).astype(bf16)

    for i in reversed(range(blocks)):
        rows, seen = pl.ds(i * BLK, BLK), (i + 1) * BLK
        query, keys, values = qkv_v[rows, :HS], qkv_v[:seen, HS : 2 * HS], qkv_v[:seen, 2 * HS :]
        t = lax.broadcasted_iota(jnp.int32, (BLK, 1), 0) + i * BLK
        key_at = lax.broadcasted_iota(jnp.int32, (BLK, seen), 1)
        scores = dot_nt(query, keys) * scale
        scores = jnp.where((key_at >= first_of(t)) & (key_at <= t), scores, masked_value)
        weights = jnp.exp(scores - jnp.max(scores, axis=-1, keepdims=True))
        probs = weights * (1.0 / jnp.sum(weights, axis=-1, keepdims=True))
        probs_low = probs.astype(bf16)
        o_v[rows, :] = dot_nn(probs_low, values).astype(bf16)
        grad_mixed = do_v[rows, :]
        grad_probs = dot_nt(grad_mixed, values)
        row_dot = jnp.sum(probs * grad_probs, axis=-1, keepdims=True)
        grad_scores = (probs * (grad_probs - row_dot)).astype(bf16)
        grad_query = dot_nn(grad_scores, keys) * scale
        grad_keys = dot_tn(grad_scores, query) * scale
        grad_values = dot_tn(probs_low, grad_mixed)
        if i == blocks - 1:
            dkv[0] = grad_keys
            dkv[1] = grad_values
        else:
            dkv[0, :seen] += grad_keys
            dkv[1, :seen] += grad_values
        qkv_v[rows, :HS] = turned(grad_query, -1.0, rows).astype(bf16)
    for i in range(blocks):
        rows = pl.ds(i * BLK, BLK)
        qkv_v[rows, HS : 2 * HS] = turned(dkv[0, rows], -1.0, rows).astype(bf16)
        qkv_v[rows, 2 * HS :] = dkv[1, rows].astype(bf16)
    for i in range(blocks):
        vec_o[5:6, : 3 * HS] += jnp.sum(qkv_v[pl.ds(i * BLK, BLK), :].astype(f32), axis=0, keepdims=True)
    o_out = pltpu.make_async_copy(o_v, o_o, out_sems.at[3])
    dp_out = pltpu.make_async_copy(qkv_v, dp_o, out_sems.at[4])
    o_out.start()
    dp_out.start()

    wu_in[0].wait()
    cast(wu_v, pl.ds(0, HS), 1, 0, width)
    wu_in[3].start()
    wu_in[1].wait()
    cast(wu_v, pl.ds(HS, HS), 2, 0, width)
    wd_in[0].start()
    wd_in[1].start()
    wu_in[2].wait()
    cast(wu_v, pl.ds(2 * HS, HS), 0, 0, width)
    wd_in[2].start()
    wd_in[3].start()
    wu_in[3].wait()
    cast(wu_v, pl.ds(3 * HS, HS), 1, 0, width)
    wd_in[4].start()
    wd_in[5].start()
    for k in range(width // HS):
        wd_in[k].wait()
        cast(wd_v, pl.ds(k * HS, HS), down_slot[k], (k % 2) * hidden, hidden)
        if k == 1:
            wd_in[6].start()
            wd_in[7].start()

    a_out.wait()
    z_v = a_v
    greet([here.to_y(here.y_at(1)), here.to_y(here.y_at(3)), here.to_x_hi()])
    branch = BucketSum(here, z_v, buf_wide, buf_cut, buf_x, buf_far, stage, sems, width)

    def feed(off):
        rows = aligned(here.y_at(off) * BLK, BLK)
        up_pre = dot_nn(b_v[rows, :], wu_v[...]) + bu[...]
        grad_act = dot_nt(e_v[rows, :], wd_v[...])
        act, slope = gelu_parts(up_pre)
        g_v[rows, :] = act.astype(bf16)
        grad_low = (grad_act * slope).astype(bf16)
        du_v[rows, :] = grad_low
        vec_o[6:7, :hidden] += jnp.sum(grad_low.astype(f32), axis=0, keepdims=True)

        @pl.loop(0, 2)
        def _(c):
            cols = aligned(c * (width // 2), width // 2)
            z_v[rows, cols] = (dot_nn(o_v[rows, :], wo_v[:, cols]) + dot_nn(g_v[rows, :], wd_v[:, cols])).astype(bf16)

        branch.across[off].start()

    def into_norms(off):
        rows = aligned(here.y_at(off) * BLK, BLK)
        mean, rstd = mean_v[rows], rstd_v[rows]

        @pl.loop(0, 4)
        def _(c):
            cols = aligned(c * (width // 4), width // 4)
            da = dot_nt(qkv_v[rows, :], wq_v[cols, :])
            db = dot_nt(du_v[rows, :], wu_v[cols, :])
            normed = (tok_v[rows, cols].astype(f32) - mean) * rstd
            vec_o[0:1, cols] += jnp.sum(da * normed, axis=0, keepdims=True)
            vec_o[1:2, cols] += jnp.sum(da, axis=0, keepdims=True)
            vec_o[2:3, cols] += jnp.sum(db * normed, axis=0, keepdims=True)
            vec_o[3:4, cols] += jnp.sum(db, axis=0, keepdims=True)
            tok_v[rows, cols] = (da * lnp[0:1, cols] + db * lnp[2:3, cols]).astype(bf16)

    feed(2)
    branch.far.send_opp()
    feed(1)
    branch.far.send_right()
    feed(3)
    branch.far.send_left()
    branch.add_across(2)
    branch.near.send_opp()
    branch.far.relay()
    feed(0)
    g_out = pltpu.make_async_copy(g_v, g_o, out_sems.at[5])
    du_out = pltpu.make_async_copy(du_v, du_o, out_sems.at[6])
    g_out.start()
    du_out.start()
    branch.add_across(1)
    branch.near.send_right()
    branch.add_across(3)
    branch.near.send_left()
    into_norms(2)
    branch.pass_far()
    branch.near.relay()
    into_norms(1)
    branch.add_across(0)
    into_norms(3)
    into_norms(0)
    s_out = pltpu.make_async_copy(tok_v, s_o, out_sems.at[7])
    s_out.start()
    x_in.wait()
    branch.last.got()
    t = lax.broadcasted_iota(jnp.int32, (SUB, 1), 0) + own_first
    for half in range(2):
        rows = pl.ds(half * SUB, SUB)
        total = branch.near.total(half)
        total = jnp.concatenate(
            [total[:, :LEFT_COLS] + buf_far[rows, :].astype(f32), total[:, LEFT_COLS:]], axis=1
        )
        used = (t + half * SUB < end[3]).astype(f32)
        rows_o[rows, :] = (used * (x_own[rows, :].astype(f32) + total + bb[...])).astype(bf16)
    branch.finish()
    for copy in (b_out, e_out, o_out, dp_out, g_out, du_out, s_out):
        copy.wait()


def any_space():
    return pl.BlockSpec(memory_space=pl.ANY)


def vmem_space():
    return pl.BlockSpec(memory_space=pltpu.VMEM)


def rotary_tables(rows):
    inverse = np.exp(np.arange(ROT // 2) * (-2.0 * math.log(10000.0) / ROT))
    angle = np.arange(rows)[:, None] * inverse[None, :]
    cos_of, sin_of = np.ones((rows, 128)), np.zeros((rows, 128))
    freq = np.zeros((8, 128))
    for first in (0, ROT // 2):
        part = slice(first, first + ROT // 2)
        cos_of[:, part], sin_of[:, part] = np.cos(angle), np.sin(angle)
        freq[:, part] = inverse
    return np.stack([cos_of, sin_of]).astype(np.float32), freq.astype(np.float32)


def front(lengths, tokens, cotangent, lnp, wq, bq, wo, wu, bu, wd, bb):
    rows, width = tokens.shape
    hidden = wu.shape[1]
    turn, freq = rotary_tables(rows)
    shape = jax.ShapeDtypeStruct
    outs = (
        shape((rows, width), bf16),
        shape((rows, width), bf16),
        shape((rows, width), bf16),
        shape((rows, hidden), bf16),
        shape((rows, hidden), bf16),
        shape((rows, 3 * HS), bf16),
        shape((rows, HS), bf16),
        shape((rows, width), bf16),
        shape((HALF, width), bf16),
        shape((8, width), f32),
    )
    v = pltpu.VMEM
    dma = pltpu.SemaphoreType.DMA
    return pl.pallas_call(
        front_kernel,
        out_shape=outs,
        in_specs=[
            pl.BlockSpec(memory_space=pltpu.SMEM), any_space(), any_space(), vmem_space(), vmem_space(), vmem_space(),
            any_space(), vmem_space(), any_space(), any_space(), vmem_space(), any_space(), vmem_space(),
        ],
        out_specs=(any_space(),) * 8 + (vmem_space(),) * 2,
        scratch_shapes=[
            v((rows, width), bf16), v((rows, width), bf16), v((rows, width), bf16), v((rows, width), bf16),
            v((width, 3 * HS), bf16), v((HS, width), bf16), v((width, hidden), bf16), v((hidden, width), bf16),
            v((3, width, HS), f32), v((rows, 3 * HS), bf16), v((2, rows, HS), f32), v((rows, HS), bf16),
            v((rows, HS), bf16), v((3, rows, 128), f32), v((rows, 1), f32), v((rows, 1), f32),
            v((rows, hidden), bf16), v((rows, hidden), bf16),
            v((6, SUB, width), bf16), v((6, SUB, LEFT_COLS), bf16), v((4, HALF, width - LEFT_COLS), bf16),
            v((HALF, LEFT_COLS), bf16), v((HALF, LEFT_COLS), bf16), v((HALF, width), bf16),
            dma((9,)), dma((23,)), dma((8,)), dma((2, BucketSum.LINKS)),
        ],
        compiler_params=pltpu.CompilerParams(
            collective_id=0, has_side_effects=True, vmem_limit_bytes=62 * MIB
        ),
        name="front",
    )(lengths, tokens, cotangent, lnp, turn, freq, wq, bq, wo, wu, bu, wd, bb)


class RingCopy:
    def __init__(self, here, own, out, first, cols, sems, base):
        self.out, self.first, self.cols = out, first, cols
        own_y, right, _, left, to_right, to_left = here.ring_y()
        part = self.part
        self.links = [
            Link(sems, base + 0, own, part(own_y), to_right),
            Link(sems, base + 1, own, part(own_y), to_left),
            Link(sems, base + 2, part(left, 0), part(left, 0), to_right),
            Link(sems, base + 3, part(right, 1), part(right, 1), to_left),
        ]

    def part(self, y, half=None, cols=None):
        if half is None:
            rows = aligned(self.first(y), HALF)
        else:
            rows = aligned(self.first(y) + half * SUB, SUB)
        return self.out.at[rows, self.cols if cols is None else cols]

    def start(self):
        self.links[0].start()
        self.links[1].start()

    def pass_on(self):
        for near, far in ((0, 2), (1, 3)):
            self.links[near].got()
            self.links[far].start()

    def finish(self):
        for link in self.links:
            link.sent()


class BucketCopy:
    LINKS = 14

    def __init__(self, here, own, out, sems, local_sem, width):
        cut, rest = pl.ds(0, LEFT_COLS), pl.ds(LEFT_COLS, width - LEFT_COLS)
        first_own = lambda y: y * BLK + here.x_hi * HALF
        first_far = lambda y: y * BLK + (1 - here.x_hi) * HALF
        self.near = RingCopy(here, own, out, first_own, pl.ds(0, width), sems, 0)
        far_own = out.at[aligned(first_far(here.y), HALF), cut]
        self.far = RingCopy(here, far_own, out, first_far, cut, sems, 4)
        part = self.near.part
        y, right, opp, left, _, _ = here.ring_y()
        moves = [(own.at[:, cut], part(y, cols=cut)), (own.at[:, rest], part(y, cols=rest))]
        for place, half in ((left, None), (right, None), (opp, 0), (opp, 1)):
            moves.append((part(place, half, rest), part(place, half, rest)))
        self.across = [Link(sems, 8 + i, src, dst, here.to_x_hi()) for i, (src, dst) in enumerate(moves)]
        self.keep = pltpu.make_async_copy(own, part(y), local_sem)

    def start(self):
        self.near.start()
        self.across[0].start()
        self.across[1].start()
        self.keep.start()

    def start_far(self):
        self.across[0].got()
        self.far.start()

    def pass_near(self):
        self.near.pass_on()
        self.across[2].start()
        self.across[3].start()

    def cross_opp(self):
        for i in range(2):
            self.near.links[2 + i].got()
            self.across[4 + i].start()

    def pass_far(self):
        self.far.pass_on()

    def finish(self):
        self.far.links[2].got()
        self.far.links[3].got()
        for link in self.across[1:]:
            link.got()
        for link in self.across:
            link.sent()
        self.near.finish()
        self.far.finish()
        self.keep.wait()


class GradSum:
    LINKS = 15

    def __init__(self, here, grads, buf_core, buf_ring, stage, buf_last, sems):
        self.here, self.grads, self.buf_core = here, grads, buf_core
        self.stage, self.buf_last = stage, buf_last
        every = pl.ds(0, grads.shape[1])

        def rows(x_lo, z, core):
            return aligned(((x_lo * 4 + z) * 2 + core) * HALF, HALF)

        self.rows = rows
        self.cores = [
            Link(
                sems,
                off * 2 + x_lo,
                grads.at[rows(x_lo, here.z_at(off), 1 - here.core)],
                buf_core.at[off * 2 + x_lo],
                here.to_core(),
            )
            for off in range(4)
            for x_lo in range(2)
        ]
        self.ring = RingSum(
            here.ring_z(), grads, lambda z, half: rows(half, z, here.core), every, buf_ring, sems, 8
        )
        self.last = Link(sems, 14, stage, buf_last, here.to_x_lo())

    def swap(self, off):
        self.cores[off * 2].start()
        self.cores[off * 2 + 1].start()

    def add_core(self, off):
        for x_lo in range(2):
            self.cores[off * 2 + x_lo].got()
            rows = self.rows(x_lo, self.here.z_at(off), self.here.core)
            self.grads[rows, :] = (
                self.grads[rows, :].astype(f32) + self.buf_core[off * 2 + x_lo].astype(f32)
            ).astype(bf16)

    def cross(self, kept):
        low, high = self.ring.total(0), self.ring.total(1)
        mine = self.here.x_lo == 0
        self.stage[...] = jnp.where(mine, high, low).astype(bf16)
        self.last.start()
        kept[...] = jnp.where(mine, low, high)

    def finish(self):
        for link in self.cores + [self.last]:
            link.sent()
        self.ring.finish()


class Total:
    def __init__(self, here, steps, bufs, sems):
        self.steps, self.bufs, self.at = steps, bufs, 0
        z_pair, y_pair = here.z + 1 - 2 * (here.z % 2), here.y + 1 - 2 * (here.y % 2)
        targets = [
            here.to_core(), here.to_z(z_pair), here.to_z(3 - here.z), here.to_x_lo(),
            here.to_y(y_pair), here.to_y(3 - here.y), here.to_x_hi(),
        ]
        self.links = [Link(sems, i, steps.at[i], bufs.at[i], target) for i, target in enumerate(targets)]

    def start(self):
        self.links[0].start()

    def step(self):
        i = self.at
        self.links[i].got()
        self.steps[i + 1] = self.steps[i] + self.bufs[i]
        self.at = i + 1
        if self.at < len(self.links):
            self.links[self.at].start()

    def finish(self):
        for link in self.links:
            link.sent()


def back_kernel(
    tok, a, b, e, g, du, dp, o, s, rows_in, vec,
    out, gt, up_o, down_o, qkv_o, out_o, gains_o, qkv_bias_o, up_bias_o, bias_o,
    a_v, b_v, e_v, g_v, du_v, dp_v, o_v, s_v, x_own, e_own, grads, buf_core, buf_ring, stage_dp, buf_dp, kept,
    buf_wide, buf_cut, buf_x, buf_far, stage, gt_own, steps, step_bufs,
    in_sems, local_sems, sum_sems, out_sems, gt_sems, dp_sems, vec_sems,
):
    here = Place()
    width = s_v.shape[1]
    hidden = g_v.shape[1]
    own_first = here.y * BLK + here.x_hi * HALF
    own_rows = aligned(own_first, HALF)

    pairs = [(s, s_v), (b, b_v), (du, du_v), (e, e_v), (g, g_v), (a, a_v), (dp, dp_v), (o, o_v)]
    pairs += [(tok.at[own_rows], x_own), (e.at[own_rows], e_own)]
    loads = [pltpu.make_async_copy(src, dst, in_sems.at[i]) for i, (src, dst) in enumerate(pairs)]
    for load in loads:
        load.start()

    ring = here.ring_y()
    ring_z = here.ring_z()
    greet([ring[4], ring[5], here.to_x_hi(), ring_z[4], ring_z[5], here.to_core(), here.to_x_lo()])

    wide = BucketSum(here, s_v, buf_wide, buf_cut, buf_x, buf_far, stage, sum_sems, width)
    gather_out = BucketCopy(here, rows_in, out, out_sems, local_sems.at[0], width)
    gather_gt = BucketCopy(here, gt_own, gt, gt_sems, local_sems.at[1], width)
    weights = GradSum(here, grads, buf_core, buf_ring, stage_dp, buf_dp, dp_sems)
    small = Total(here, steps, step_bufs, vec_sems)

    def weight_grads(off):
        @pl.loop(0, 2)
        def _(x_lo):
            m = aligned((x_lo * 4 + here.z_at(off)) * BLK, BLK)
            grads[m, :hidden] = dot_tn(b_v[:, m], du_v[...]).astype(bf16)
            grads[m, hidden : 2 * hidden] = dot_tn(e_v[:, m], g_v[...]).astype(bf16)
            grads[m, 2 * hidden : 2 * hidden + 3 * HS] = dot_tn(a_v[:, m], dp_v[...]).astype(bf16)
            grads[m, 2 * hidden + 3 * HS :] = dot_tn(e_v[:, m], o_v[...]).astype(bf16)

        weights.swap(off)

    loads[0].wait()
    for off in (2, 1, 3, 0):
        wide.across[off].start()
    wide.far.send_opp()
    wide.far.send_right()
    wide.far.send_left()
    steps[0] = vec[...]
    small.start()
    gather_out.start()
    for load in loads[1:]:
        load.wait()

    weight_grads(2)
    wide.add_across(2)
    wide.near.send_opp()
    wide.far.relay()
    small.step()
    weight_grads(1)
    weights.add_core(2)
    weights.ring.send_opp()
    wide.add_across(1)
    wide.near.send_right()
    wide.add_across(3)
    wide.near.send_left()
    wide.pass_far()
    gather_out.start_far()
    small.step()
    weight_grads(3)
    weights.add_core(1)
    weights.ring.send_right()
    wide.add_across(0)
    wide.near.relay()
    gather_out.pass_near()
    small.step()
    weight_grads(0)
    weights.add_core(3)
    weights.ring.send_left()
    weights.add_core(0)
    small.step()

    wide.last.got()
    for half in range(2):
        rows = pl.ds(half * SUB, SUB)
        total = wide.near.total(half)
        total = jnp.concatenate(
            [total[:, :LEFT_COLS] + buf_far[rows, :].astype(f32), total[:, LEFT_COLS:]], axis=1
        )
        x = x_own[rows, :].astype(f32)
        centred = x - jnp.mean(x, axis=-1, keepdims=True)
        rstd = lax.rsqrt(jnp.mean(centred * centred, axis=-1, keepdims=True) + norm_eps)
        normed = centred * rstd
        grad = rstd * (
            total - jnp.mean(total, axis=-1, keepdims=True) - normed * jnp.mean(total * normed, axis=-1, keepdims=True)
        )
        gt_own[rows, :] = (e_own[rows, :].astype(f32) + grad).astype(bf16)
    gather_gt.start()
    small.step()
    gather_out.cross_opp()
    gather_out.pass_far()
    weights.ring.relay()
    small.step()
    gather_gt.start_far()
    small.step()
    gather_gt.pass_near()
    gather_gt.cross_opp()
    gather_gt.pass_far()
    weights.cross(kept)
    gains_o[...] = steps[7, 0:4, aligned(here.mp * HS, HS)]
    bias_o[...] = steps[4, 4:5, aligned(here.mp * HS, HS)]
    qkv_bias_o[...] = steps[4, 5:6, : 3 * HS]
    up_bias_o[...] = steps[4, 6:7, :hidden]
    weights.last.got()
    up_o[...] = kept[:, :hidden] + buf_dp[:, :hidden].astype(f32)
    down_o[...] = (kept[:, hidden : 2 * hidden] + buf_dp[:, hidden : 2 * hidden].astype(f32)).T
    for j in range(3):
        cols = pl.ds(2 * hidden + j * HS, HS)
        qkv_o[j] = kept[:, cols] + buf_dp[:, cols].astype(f32)
    cols = pl.ds(2 * hidden + 3 * HS, HS)
    out_o[...] = (kept[:, cols] + buf_dp[:, cols].astype(f32)).T
    wide.finish()
    weights.finish()
    small.finish()
    gather_out.finish()
    gather_gt.finish()


def back(tokens, a, b, e, g, du, dp, o, s, rows_in, vec):
    rows, width = tokens.shape
    hidden = g.shape[1]
    all_cols = 2 * hidden + 4 * HS
    shape = jax.ShapeDtypeStruct
    outs = (
        shape((rows, width), bf16),
        shape((rows, width), bf16),
        shape((HALF, hidden), f32),
        shape((hidden, HALF), f32),
        shape((3, HALF, HS), f32),
        shape((HS, HALF), f32),
        shape((4, HS), f32),
        shape((1, 3 * HS), f32),
        shape((1, hidden), f32),
        shape((1, HS), f32),
    )
    v = pltpu.VMEM
    dma = pltpu.SemaphoreType.DMA
    return pl.pallas_call(
        back_kernel,
        out_shape=outs,
        in_specs=[any_space()] * 9 + [vmem_space()] * 2,
        out_specs=(any_space(),) * 2 + (vmem_space(),) * 8,
        scratch_shapes=[
            v((rows, width), bf16), v((rows, width), bf16), v((rows, width), bf16), v((rows, hidden), bf16),
            v((rows, hidden), bf16), v((rows, 3 * HS), bf16), v((rows, HS), bf16), v((rows, width), bf16),
            v((HALF, width), bf16), v((HALF, width), bf16),
            v((width, all_cols), bf16), v((8, HALF, all_cols), bf16), v((6, HALF, all_cols), bf16),
            v((HALF, all_cols), bf16), v((HALF, all_cols), bf16), v((HALF, all_cols), f32),
            v((6, SUB, width), bf16), v((6, SUB, LEFT_COLS), bf16), v((4, HALF, width - LEFT_COLS), bf16),
            v((HALF, LEFT_COLS), bf16), v((HALF, LEFT_COLS), bf16), v((HALF, width), bf16),
            v((8, 8, width), f32), v((7, 8, width), f32),
            dma((10,)), dma((2,)), dma((2, BucketSum.LINKS)), dma((2, BucketCopy.LINKS)),
            dma((2, BucketCopy.LINKS)), dma((2, GradSum.LINKS)), dma((2, 7)),
        ],
        compiler_params=pltpu.CompilerParams(
            collective_id=1, has_side_effects=True, vmem_limit_bytes=62 * MIB
        ),
        name="back",
    )(tokens, a, b, e, g, du, dp, o, s, rows_in, vec)


def local(
    tokens, lengths, ln1_gain, ln1_bias, ln2_gain, ln2_bias, qkv_master, qkv_bias, out_master, up_master, up_bias,
    down_master, branch_bias, cotangent,
):
    lnp = jnp.stack([ln1_gain, ln1_bias, ln2_gain, ln2_bias])
    w_qkv = jnp.transpose(qkv_master, (1, 0, 2))
    a, b, e, g, du, dp, o, s, rows, vec = front(
        lengths, tokens, cotangent, lnp, w_qkv, qkv_bias.reshape(1, -1), out_master, up_master,
        up_bias.reshape(1, -1), down_master, branch_bias.reshape(1, -1),
    )
    output, grad_tokens, up, down, qkv, out, gains, qkv_bias_sum, up_bias_sum, bias_sum = back(
        tokens, a, b, e, g, du, dp, o, s, rows, vec
    )
    return (
        output,
        grad_tokens,
        gains[0],
        gains[1],
        gains[2],
        gains[3],
        jnp.transpose(qkv, (1, 0, 2)),
        qkv_bias_sum.reshape(qkv_bias.shape),
        out,
        up,
        up_bias_sum.reshape(up_bias.shape),
        down,
        bias_sum.reshape(-1),
    )


def solution(mesh):
    placed = (
        P("dp", None),
        P("dp", None),
        P(),
        P(),
        P(),
        P(),
        P(None, None, "mp"),
        P(None, "mp"),
        P("mp", None),
        P(None, "mp"),
        P("mp"),
        P("mp", None),
        P(),
        P("dp", None),
    )
    return jax.shard_map(
        local,
        mesh=mesh,
        in_specs=placed,
        out_specs=(
            P("dp", None),
            P("dp", None),
            P("mp"),
            P("mp"),
            P("mp"),
            P("mp"),
            P("dp", None, "mp"),
            P(None, "mp"),
            P("mp", "dp"),
            P("dp", "mp"),
            P("mp"),
            P("mp", "dp"),
            P("mp"),
        ),
        check_vma=False,
    )
```

```python
import functools
import math

import jax
import jax.numpy as jnp
import numpy as np
from jax import lax
from jax.experimental import pallas as pl
from jax.experimental.pallas import tpu as pltpu
from jax.sharding import PartitionSpec as P

HS = 256
ROT = 64
BLK = 256
HALF = 128
SUB = 64
SLOTS = 2
BRANCH_CUT = 1280
NORM_CUT = 1280
OUT_CUT = 1280
GRAD_CUT = 1536
MESH = pl.DeviceIdType.MESH
MIB = 2**20
norm_eps = 1e-05
masked_value = -1e30
f32 = jnp.float32
bf16 = jnp.bfloat16


def dot_nn(a, b):
    return jnp.dot(a, b, preferred_element_type=f32)


def dot_nt(a, b):
    return lax.dot_general(a, b, (((1,), (1,)), ((), ())), preferred_element_type=f32)


def dot_tn(a, b):
    return lax.dot_general(a, b, (((0,), (0,)), ((), ())), preferred_element_type=f32)


def aligned(start, size, unit=None):
    if isinstance(start, int):
        return pl.ds(start, size)
    return pl.ds(pl.multiple_of(start, unit or size), size)


class Place:
    def __init__(self):
        self.dp = lax.axis_index("dp")
        self.mp = lax.axis_index("mp")
        self.x_hi = self.mp // 4
        self.y = self.mp % 4
        self.x_lo = self.dp // 8
        self.z = (self.dp // 2) % 4
        self.core = self.dp % 2

    def y_at(self, off):
        return (self.y + off) % 4

    def z_at(self, off):
        return (self.z + off) % 4

    def to_y(self, y):
        return (self.dp, self.x_hi * 4 + y)

    def ring_y(self):
        right, left = self.y_at(1), self.y_at(3)
        return self.y, right, self.y_at(2), left, self.to_y(right), self.to_y(left)

    def ring_z(self):
        right, left = self.z_at(1), self.z_at(3)
        return self.z, right, self.z_at(2), left, self.to_z(right), self.to_z(left)

    def to_x_hi(self):
        return (self.dp, (1 - self.x_hi) * 4 + self.y)

    def to_z(self, z):
        return ((self.x_lo * 4 + z) * 2 + self.core, self.mp)

    def to_x_lo(self):
        return (((1 - self.x_lo) * 4 + self.z) * 2 + self.core, self.mp)

    def to_core(self):
        return ((self.x_lo * 4 + self.z) * 2 + 1 - self.core, self.mp)


def greet(targets):
    for target in targets:
        pl.semaphore_signal(pltpu.get_barrier_semaphore(), inc=1, device_id=target, device_id_type=MESH)


def await_greetings(count):
    pl.semaphore_wait(pltpu.get_barrier_semaphore(), count)


class Link:
    def __init__(self, sems, number, src, dst, target):
        self.copy = pltpu.make_async_remote_copy(
            src_ref=src,
            dst_ref=dst,
            send_sem=sems.at[0, number],
            recv_sem=sems.at[1, number],
            device_id=target,
            device_id_type=MESH,
        )

    def start(self):
        self.copy.start()

    def got(self):
        self.copy.wait_recv()

    def sent(self):
        self.copy.wait_send()


class RingSum:
    def __init__(self, ring, src, at, buf, sems, base):
        self.src, self.at, self.buf = src, at, buf
        self.own, self.right, self.opp, self.left, to_right, to_left = ring
        part = lambda place, half: src.at[at(place, half)]
        self.links = [
            Link(sems, base + 0, part(self.opp, 0), buf.at[0], to_right),
            Link(sems, base + 1, part(self.opp, 1), buf.at[1], to_left),
            Link(sems, base + 2, part(self.right, 0), buf.at[2], to_right),
            Link(sems, base + 3, part(self.right, 1), buf.at[3], to_right),
            Link(sems, base + 4, part(self.left, 1), buf.at[4], to_left),
            Link(sems, base + 5, part(self.left, 0), buf.at[5], to_left),
        ]

    def send_opp(self):
        self.links[0].start()
        self.links[1].start()

    def send_right(self):
        self.links[3].start()

    def send_left(self):
        self.links[5].start()

    def relay(self):
        for number, place, half in ((0, self.right, 0), (1, self.left, 1)):
            self.links[number].got()
            at = self.at(place, half)
            self.src[at] = (self.src[at].astype(f32) + self.buf[number].astype(f32)).astype(bf16)
            self.links[2 if number == 0 else 4].start()

    def total(self, half):
        one, two = (2, 5) if half == 0 else (4, 3)
        self.links[one].got()
        self.links[two].got()
        own = self.src[self.at(self.own, half)].astype(f32)
        return own + self.buf[one].astype(f32) + self.buf[two].astype(f32)

    def finish(self):
        for link in self.links:
            link.sent()


class BucketSum:
    LINKS = 17

    def __init__(self, here, src, buf_wide, buf_cut, buf_x, buf_far, sems, width, cut):
        self.here, self.src, self.buf_x, self.buf_far, self.width, self.at_cut = here, src, buf_x, buf_far, width, cut
        self.cut, self.rest = pl.ds(0, cut), pl.ds(cut, width - cut)
        self.first_own = lambda y: y * BLK + here.x_hi * HALF
        self.first_far = lambda y: y * BLK + (1 - here.x_hi) * HALF

        def halves(first, cols):
            return lambda y, half: (aligned(first(y) + half * SUB, SUB), cols)

        self.far = RingSum(here.ring_y(), src, halves(self.first_far, self.cut), buf_cut, sems, 0)
        self.near = RingSum(here.ring_y(), src, halves(self.first_own, pl.ds(0, width)), buf_wide, sems, 6)
        self.across = [
            Link(
                sems,
                12 + off,
                src.at[aligned(self.first_far(here.y_at(off)), HALF), self.rest],
                buf_x.at[off],
                here.to_x_hi(),
            )
            for off in range(4)
        ]
        own_far = src.at[aligned(self.first_far(here.y), HALF), self.cut]
        self.last = Link(sems, 16, own_far, buf_far, here.to_x_hi())

    def add_across(self, off):
        self.across[off].got()
        rows = aligned(self.first_own(self.here.y_at(off)), HALF)
        self.src[rows, self.rest] = (
            self.src[rows, self.rest].astype(f32) + self.buf_x[off].astype(f32)
        ).astype(bf16)

    def pass_far(self):
        for half in range(2):
            self.src[self.far.at(self.here.y, half)] = self.far.total(half).astype(bf16)
        self.last.start()

    def total(self, half):
        if half == 0:
            self.last.got()
        near = self.near.total(half)
        far = self.buf_far[pl.ds(half * SUB, SUB), :].astype(f32)
        return jnp.concatenate([near[:, : self.at_cut] + far, near[:, self.at_cut :]], axis=1)

    def finish(self):
        self.far.finish()
        self.near.finish()
        for link in self.across:
            link.sent()
        self.last.sent()


class RingCopy:
    LINKS = 6

    def __init__(self, here, own, out, first, cols, sems, base):
        self.out, self.first, self.cols = out, first, cols
        own_y, right, _, left, to_right, to_left = here.ring_y()
        part = self.part
        halves = [own.at[pl.ds(half * SUB, SUB)] for half in range(2)]
        self.links = [
            Link(sems, base + 0, halves[0], part(own_y, 0), to_right),
            Link(sems, base + 1, halves[1], part(own_y, 1), to_left),
            Link(sems, base + 2, part(left, 0), part(left, 0), to_right),
            Link(sems, base + 3, part(right, 1), part(right, 1), to_left),
            Link(sems, base + 4, halves[1], part(own_y, 1), to_right),
            Link(sems, base + 5, halves[0], part(own_y, 0), to_left),
        ]

    def part(self, y, half=None, cols=None):
        if half is None:
            rows = aligned(self.first(y), HALF)
        else:
            rows = aligned(self.first(y) + half * SUB, SUB)
        return self.out.at[rows, self.cols if cols is None else cols]

    def start(self):
        for number in (0, 1, 4, 5):
            self.links[number].start()

    def pass_on(self):
        for near, far in ((0, 2), (1, 3)):
            self.links[near].got()
            self.links[far].start()

    def rest(self):
        self.links[4].got()
        self.links[5].got()

    def opposite(self):
        self.links[2].got()
        self.links[3].got()

    def finish(self):
        for link in self.links:
            link.sent()


class BucketCopy:
    LINKS = 18

    def __init__(self, here, own, out, sems, local_sem, width, cut):
        cut, rest = pl.ds(0, cut), pl.ds(cut, width - cut)
        first_own = lambda y: y * BLK + here.x_hi * HALF
        first_far = lambda y: y * BLK + (1 - here.x_hi) * HALF
        self.near = RingCopy(here, own, out, first_own, pl.ds(0, width), sems, 0)
        far_own = out.at[aligned(first_far(here.y), HALF), cut]
        self.far = RingCopy(here, far_own, out, first_far, cut, sems, RingCopy.LINKS)
        part = self.near.part
        y, right, opp, left, _, _ = here.ring_y()
        moves = [(own.at[:, cut], part(y, cols=cut)), (own.at[:, rest], part(y, cols=rest))]
        for place, half in ((left, None), (right, None), (opp, 0), (opp, 1)):
            moves.append((part(place, half, rest), part(place, half, rest)))
        self.across = [Link(sems, 2 * RingCopy.LINKS + i, src, dst, here.to_x_hi()) for i, (src, dst) in enumerate(moves)]
        self.keep = pltpu.make_async_copy(own, part(y), local_sem)

    def start(self):
        self.near.start()
        self.keep.start()

    def send_cut(self):
        self.across[0].start()

    def send_rest(self):
        self.across[1].start()

    def start_far(self):
        self.across[0].got()
        self.far.start()

    def pass_near(self):
        self.near.pass_on()

    def cross_near(self):
        self.near.rest()
        self.across[2].start()
        self.across[3].start()

    def cross_opp(self):
        for i in range(2):
            self.near.links[2 + i].got()
            self.across[4 + i].start()

    def pass_far(self):
        self.far.pass_on()

    def finish(self):
        self.far.rest()
        self.far.opposite()
        for link in self.across[1:]:
            link.got()
        for link in self.across:
            link.sent()
        self.near.finish()
        self.far.finish()
        self.keep.wait()


class GradSum:
    ORDER = (2, 1, 3, 0)
    LINKS = 15

    def __init__(self, here, grads, at, buf_core, buf_ring, buf_last, sems, free_sems):
        self.here, self.grads, self.buf_core, self.buf_last, self.free_sems = here, grads, buf_core, buf_last, free_sems
        self.at = lambda x_lo, z, core: at((x_lo * 4 + z) * 2 + core)
        self.cores = {
            off: [
                Link(
                    sems,
                    turn * 2 + x_lo,
                    grads.at[self.at(x_lo, here.z_at(off), 1 - here.core)],
                    buf_core.at[(turn % 2) * 2 + x_lo],
                    here.to_core(),
                )
                for x_lo in range(2)
            ]
            for turn, off in enumerate(self.ORDER)
        }
        self.ring = RingSum(here.ring_z(), grads, lambda z, half: self.at(half, z, here.core), buf_ring, sems, 8)
        self.other = self.at(1 - here.x_lo, here.z, here.core)
        self.last = Link(sems, 14, grads.at[self.other], buf_last, here.to_x_lo())

    def swap(self, off):
        turn = self.ORDER.index(off)
        if turn >= 2:
            pl.semaphore_wait(self.free_sems.at[turn % 2], 1)
        for link in self.cores[off]:
            link.start()

    def add_core(self, off):
        turn = self.ORDER.index(off)
        for x_lo in range(2):
            self.cores[off][x_lo].got()
            at = self.at(x_lo, self.here.z_at(off), self.here.core)
            self.grads[at] = (
                self.grads[at].astype(f32) + self.buf_core[(turn % 2) * 2 + x_lo].astype(f32)
            ).astype(bf16)
        if turn < 2:
            pl.semaphore_signal(
                self.free_sems.at[turn], inc=1, device_id=self.here.to_core(), device_id_type=MESH
            )

    def cross(self):
        low, high = self.ring.total(0), self.ring.total(1)
        mine = self.here.x_lo == 0
        self.grads[self.other] = jnp.where(mine, high, low).astype(bf16)
        self.last.start()
        return jnp.where(mine, low, high)

    def rest(self):
        self.last.got()
        return self.buf_last[...].astype(f32)

    def finish(self):
        for links in self.cores.values():
            for link in links:
                link.sent()
        self.last.sent()
        self.ring.finish()


class Total:
    def __init__(self, here, steps, bufs, sems):
        self.steps, self.bufs, self.at = steps, bufs, 0
        z_pair, y_pair = here.z + 1 - 2 * (here.z % 2), here.y + 1 - 2 * (here.y % 2)
        targets = [
            here.to_core(), here.to_z(z_pair), here.to_z(3 - here.z), here.to_x_lo(),
            here.to_y(y_pair), here.to_y(3 - here.y), here.to_x_hi(),
        ]
        self.links = [Link(sems, i, steps.at[i], bufs.at[i], target) for i, target in enumerate(targets)]

    def start(self):
        self.links[0].start()

    def step(self):
        i = self.at
        self.links[i].got()
        self.steps[i + 1] = self.steps[i] + self.bufs[i]
        self.at = i + 1
        if self.at < len(self.links):
            self.links[self.at].start()

    def finish(self):
        for link in self.links:
            link.sent()


def gelu_parts(v):
    cdf = 0.5 * (1.0 + lax.erf(v * (1.0 / math.sqrt(2.0))))
    slope = cdf + v * (jnp.exp(-0.5 * v * v) * (1.0 / math.sqrt(2.0 * math.pi)))
    return v * cdf, slope


def row_stats(load, width):
    tiles = width // 128
    total = load(0)
    for tile in range(1, tiles):
        total = total + load(tile)
    mean = jnp.sum(total, axis=-1, keepdims=True) * (1.0 / width)
    square = jnp.zeros_like(total)
    for tile in range(tiles):
        centred = load(tile) - mean
        square = square + centred * centred
    var = jnp.sum(square, axis=-1, keepdims=True) * (1.0 / width)
    return mean, lax.rsqrt(var + norm_eps)


def whole_kernel(
    lens, tok, cot, one_gain, one_bias, two_gain, two_bias, turn, freq, wq, bq, wo, wu, bu, wd, bb,
    out, gt, packed, tail, a_kept,
    tok_v, a_v, b_v, e_v, w_in, w_out, st, qkv_v, o_v, do_v, tabs, stats, g_v, du_v, rows_own, gt_own,
    z_wide, z_cut, z_x, z_far, s_wide, s_cut, s_x, s_far,
    one_core, one_ring, one_last, two_core, two_ring, two_last, steps, step_bufs,
    in_sems, st_sems, local_sems, z_sems, s_sems, out_sems, gt_sems, one_sems, two_sems, vec_sems, one_free, two_free,
):
    here = Place()
    rows_all, width = tok_v.shape
    hidden = g_v.shape[1]
    blocks = rows_all // BLK
    scale = 1.0 / math.sqrt(HS)
    qkv_first = hidden

    ring, ring_z = here.ring_y(), here.ring_z()
    greet([ring[4], ring[5], here.to_x_hi(), ring_z[4], ring_z[5], here.to_core(), here.to_x_lo()])

    def block_of(i):
        return pl.ds(i * BLK, BLK)

    def column(k):
        return pl.ds(k * HS, HS)

    tok_in = [pltpu.make_async_copy(tok.at[block_of(i)], tok_v.at[block_of(i)], in_sems.at[i]) for i in range(blocks)]
    cot_in = [pltpu.make_async_copy(cot.at[block_of(i)], e_v.at[block_of(i)], in_sems.at[blocks + i]) for i in range(blocks)]
    own_first = here.y * BLK + here.x_hi * HALF
    x_in = pltpu.make_async_copy(tok.at[aligned(own_first, HALF)], gt_own, in_sems.at[2 * blocks])
    turn_in = pltpu.make_async_copy(turn, tabs, in_sems.at[2 * blocks + 1])

    pieces = [((wq.at[j], (pl.ds(0, width),)),) for j in range(3)]
    pieces += [((wu.at[:, column(k)], (pl.ds(0, width),)),) for k in range(hidden // HS)]
    pieces += [tuple((wo.at[:, column(k)], (column(k),)) for k in range(width // HS))]
    pieces += [
        tuple((wd.at[:, column(k)], (pl.ds((k % 2) * hidden, hidden),)) for k in (2 * j, 2 * j + 1))
        for j in range(width // HS // 2)
    ]
    loads, number = [], 0
    for i, piece in enumerate(pieces):
        copies = []
        for src, (rows,) in piece:
            copies.append(pltpu.make_async_copy(src, st.at[i % SLOTS, rows], st_sems.at[number]))
            number += 1
        loads.append(copies)

    def load(i):
        if i < len(loads):
            for copy in loads[i]:
                copy.start()

    def take(i):
        for copy in loads[i]:
            copy.wait()
        slot = i % SLOTS
        if i < 7:
            first = qkv_first + i * HS if i < 3 else (i - 3) * HS

            @pl.loop(0, width // BLK)
            def _(r):
                rows = aligned(r * BLK, BLK)
                w_in[rows, pl.ds(first, HS)] = st[slot, rows, :].astype(bf16)

        elif i == 7:
            for k in range(width // HS):
                w_out[hidden:, column(k)] = st[slot, column(k), :].astype(bf16)
        else:
            for k in range(2):
                cols = column(2 * (i - 8) + k)

                @pl.loop(0, hidden // BLK)
                def _(r):
                    rows = aligned(r * BLK, BLK)
                    w_out[rows, cols] = st[slot, aligned(k * hidden + r * BLK, BLK), :].astype(bf16)

        load(i + SLOTS)

    tok_in[0].start()
    tok_in[1].start()
    for i in range(SLOTS):
        load(i)
    tok_in[2].start()
    turn_in.start()
    tok_in[3].start()

    end = []
    for j in range(4):
        end.append(lens[0, j] + (end[-1] if j else 0))

    def first_of(t):
        low = jnp.zeros_like(t)
        for j in range(4):
            low = jnp.where(t >= end[j], end[j], low)
        return low

    steps[0] = jnp.zeros(steps.shape[1:], f32)

    chunk = 64

    def norms(i):
        for c in range(BLK // chunk):
            norm_chunk(aligned(i * BLK + c * chunk, chunk))

    def norm_chunk(rows):
        def tile_of(tile):
            return tok_v[rows, pl.ds(tile * 128, 128)].astype(f32)

        mean, rstd = row_stats(tile_of, width)
        stats[rows, 0:1] = mean
        stats[rows, 1:2] = rstd
        for tile in range(width // 128):
            cols = pl.ds(tile * 128, 128)
            normed = (tile_of(tile) - mean) * rstd
            a_v[rows, cols] = (normed * one_gain[:, cols] + one_bias[:, cols]).astype(bf16)
            b_v[rows, cols] = (normed * two_gain[:, cols] + two_bias[:, cols]).astype(bf16)

    def tables():
        starts = [jnp.int32(0)] + end[:3]
        lane_row = lax.broadcasted_iota(jnp.int32, (8, 128), 0)
        shift = jnp.zeros((8, 128), jnp.int32)
        for j in range(4):
            shift = jnp.where(lane_row == j, starts[j], shift)
        phase = shift.astype(f32) * freq[...]
        shift_cos, shift_sin = jnp.cos(phase), jnp.sin(phase)
        turn_in.wait()

        @pl.loop(0, rows_all // HALF)
        def _(i):
            rows = aligned(i * HALF, HALF)
            t = lax.broadcasted_iota(jnp.int32, (HALF, 128), 0) + i * HALF
            lane = lax.broadcasted_iota(jnp.int32, (HALF, 128), 1)
            c_of = jnp.broadcast_to(shift_cos[0:1], (HALF, 128))
            s_of = jnp.broadcast_to(shift_sin[0:1], (HALF, 128))
            for j in range(4):
                c_of = jnp.where(t >= end[j], shift_cos[j + 1 : j + 2], c_of)
                s_of = jnp.where(t >= end[j], shift_sin[j + 1 : j + 2], s_of)
            t_cos, t_sin = tabs[0, rows], tabs[1, rows]
            sin_of = t_sin * c_of - t_cos * s_of
            tabs[0, rows] = t_cos * c_of + t_sin * s_of
            tabs[1, rows] = jnp.where(lane < ROT // 2, -sin_of, sin_of)

    def turned(wide, sign, rows):
        low = wide[:, :128]
        lane = lax.broadcasted_iota(jnp.int32, low.shape, 1)
        other = jnp.where(lane < ROT // 2, pltpu.roll(low, 128 - ROT // 2, 1), pltpu.roll(low, ROT // 2, 1))
        low = low * tabs[0, rows] + sign * (other * tabs[1, rows])
        return jnp.concatenate([low, wide[:, 128:]], axis=1)

    def project(i):
        rows = block_of(i)
        mixed = dot_nn(a_v[rows, :], w_in[:, qkv_first:])
        for j in range(3):
            part = mixed[:, j * HS : (j + 1) * HS] + bq[j : j + 1, :]
            qkv_v[rows, column(j)] = (turned(part, 1.0, rows) if j < 2 else part).astype(bf16)

    def norm_project(i, j):
        project(j)
        norms(i)

    def probabilities(first, seen):
        rows = aligned(first, BLK)
        t = lax.broadcasted_iota(jnp.int32, (BLK, 1), 0) + first
        key_at = lax.broadcasted_iota(jnp.int32, (BLK, seen), 1)
        scores = dot_nt(qkv_v[rows, :HS], qkv_v[:seen, HS : 2 * HS]) * scale
        scores = jnp.where((key_at >= first_of(t)) & (key_at <= t), scores, masked_value)
        weights = jnp.exp(scores - jnp.max(scores, axis=-1, keepdims=True))
        return weights * (1.0 / jnp.sum(weights, axis=-1, keepdims=True))

    def attend(off):
        first = here.y_at(off) * BLK
        probs = probabilities(first, rows_all).astype(bf16)
        o_v[aligned(first, BLK), :] = dot_nn(probs, qkv_v[:, 2 * HS :]).astype(bf16)

    def mask(i):
        cot_in[i].wait()
        rows = block_of(i)
        t = lax.broadcasted_iota(jnp.int32, (BLK, 1), 0) + i * BLK
        used = (t < end[3]).astype(f32)

        @pl.loop(0, width // 512)
        def _(c):
            cols = aligned(c * 512, 512)
            kept = e_v[rows, cols].astype(f32) * used
            e_v[rows, cols] = kept.astype(bf16)
            steps[0, 4:5, cols] += jnp.sum(kept, axis=0, keepdims=True)

    def mask_all():
        for i in range(blocks):
            mask(i)

    def mixed_back():
        do_v[...] = dot_nt(e_v[...], w_out[hidden:, :]).astype(bf16)

    def attend_back(i):
        rows, seen = block_of(i), (i + 1) * BLK
        query, keys, values = qkv_v[rows, :HS], qkv_v[:seen, HS : 2 * HS], qkv_v[:seen, 2 * HS :]
        probs = probabilities(i * BLK, seen)
        grad_mixed = do_v[rows, :]
        grad_probs = dot_nt(grad_mixed, values)
        row_dot = jnp.sum(probs * grad_probs, axis=-1, keepdims=True)
        grad_scores = (probs * (grad_probs - row_dot)).astype(bf16)
        grad_query = dot_nn(grad_scores, keys) * scale
        grad_keys = dot_tn(grad_scores, query) * scale
        grad_values = dot_tn(probs.astype(bf16), grad_mixed)
        if i == blocks - 1:
            st[0, :seen] = grad_keys
            st[0, pl.ds(rows_all, seen)] = grad_values
        else:
            st[0, :seen] += grad_keys
            st[0, pl.ds(rows_all, seen)] += grad_values
        qkv_v[rows, :HS] = turned(grad_query, -1.0, rows).astype(bf16)

    def project_back():
        for i in range(blocks):
            rows = block_of(i)
            qkv_v[rows, HS : 2 * HS] = turned(st[0, rows], -1.0, rows).astype(bf16)
            qkv_v[rows, 2 * HS :] = st[0, pl.ds(rows_all + i * BLK, BLK)].astype(bf16)
            steps[0, 5:6, : 3 * HS] += jnp.sum(qkv_v[rows, :].astype(f32), axis=0, keepdims=True)

    z_v = a_v
    branch = BucketSum(here, z_v, z_wide, z_cut, z_x, z_far, z_sems, width, BRANCH_CUT)

    def feed_up(off):
        rows = aligned(here.y_at(off) * BLK, BLK)
        act, slope = gelu_parts(dot_nn(b_v[rows, :], w_in[:, :hidden]) + bu[...])
        g_v[rows, :] = act.astype(bf16)
        du_v[rows, :] = slope.astype(bf16)

    def feed_down(off):
        rows = aligned(here.y_at(off) * BLK, BLK)

        @pl.loop(0, 2)
        def _(c):
            cols = aligned(c * (width // 2), width // 2)
            z_v[rows, cols] = (
                dot_nn(o_v[rows, :], w_out[hidden:, cols]) + dot_nn(g_v[rows, :], w_out[:hidden, cols])
            ).astype(bf16)

        branch.across[off].start()

    def out_rows():
        x_in.wait()
        t = lax.broadcasted_iota(jnp.int32, (SUB, 1), 0) + own_first
        for half in range(2):
            rows = pl.ds(half * SUB, SUB)
            used = (t + half * SUB < end[3]).astype(f32)
            rows_own[rows, :] = (used * (gt_own[rows, :].astype(f32) + branch.total(half) + bb[...])).astype(bf16)

    def attend_up(off):
        attend(off)
        feed_up(off)

    wide = BucketSum(here, tok_v, s_wide, s_cut, s_x, s_far, s_sems, width, NORM_CUT)

    def into_norms(off):
        rows = aligned(here.y_at(off) * BLK, BLK)
        grad_low = (dot_nt(e_v[rows, :], w_out[:hidden, :]) * du_v[rows, :].astype(f32)).astype(bf16)
        du_v[rows, :] = grad_low
        steps[0, 6:7, :hidden] += jnp.sum(grad_low.astype(f32), axis=0, keepdims=True)
        mean, rstd = stats[rows, 0:1], stats[rows, 1:2]

        @pl.loop(0, 4)
        def _(c):
            cols = aligned(c * (width // 4), width // 4)
            da = dot_nt(qkv_v[rows, :], w_in[cols, qkv_first:])
            db = dot_nt(du_v[rows, :], w_in[cols, :hidden])
            normed = (tok_v[rows, cols].astype(f32) - mean) * rstd
            steps[0, 0:1, cols] += jnp.sum(da * normed, axis=0, keepdims=True)
            steps[0, 1:2, cols] += jnp.sum(da, axis=0, keepdims=True)
            steps[0, 2:3, cols] += jnp.sum(db * normed, axis=0, keepdims=True)
            steps[0, 3:4, cols] += jnp.sum(db, axis=0, keepdims=True)
            tok_v[rows, cols] = (da * one_gain[:, cols] + db * two_gain[:, cols]).astype(bf16)

        wide.across[off].start()

    def gt_rows():
        for half in range(2):
            rows = pl.ds(half * SUB, SUB)
            total = wide.total(half)
            x = gt_own[rows, :].astype(f32)
            centred = x - jnp.mean(x, axis=-1, keepdims=True)
            rstd = lax.rsqrt(jnp.mean(centred * centred, axis=-1, keepdims=True) + norm_eps)
            normed = centred * rstd
            grad = rstd * (
                total - jnp.mean(total, axis=-1, keepdims=True)
                - normed * jnp.mean(total * normed, axis=-1, keepdims=True)
            )
            gt_own[rows, :] = (e_v[aligned(own_first + half * SUB, SUB), :].astype(f32) + grad).astype(bf16)

    one = GradSum(
        here, w_in, lambda block: (aligned(block * HALF, HALF), pl.ds(0, w_in.shape[1])),
        one_core, one_ring, one_last, one_sems, one_free,
    )
    two = GradSum(
        here, w_out, lambda block: (pl.ds(0, w_out.shape[0]), aligned(block * HALF, HALF)),
        two_core, two_ring, two_last, two_sems, two_free,
    )

    def grads_one(off):
        @pl.loop(0, 2)
        def _(x_lo):
            m = aligned((x_lo * 4 + here.z_at(off)) * BLK, BLK)
            w_in[m, :hidden] = dot_tn(b_v[:, m], du_v[...]).astype(bf16)
            w_in[m, qkv_first:] = dot_tn(a_v[:, m], qkv_v[...]).astype(bf16)

        one.swap(off)

    def grads_two(off):
        @pl.loop(0, 2)
        def _(x_lo):
            m = aligned((x_lo * 4 + here.z_at(off)) * BLK, BLK)
            w_out[:hidden, m] = dot_tn(g_v[...], e_v[:, m]).astype(bf16)
            w_out[hidden:, m] = dot_tn(o_v[...], e_v[:, m]).astype(bf16)

        two.swap(off)

    def pack_one(part, add):
        for j in range(w_in.shape[1] // HS):
            rows = pl.ds(j * HALF, HALF)
            tile = part[:, j * HS : (j + 1) * HS]
            st[1, rows, :] = st[1, rows, :] + tile if add else tile

    def pack_two(part, add):
        tall = w_out.shape[0] // 2
        rows = pl.ds((w_in.shape[1] // HS) * HALF, tall)
        both = jnp.concatenate([part[:tall], part[tall:]], axis=1)
        st[1, rows, :] = st[1, rows, :] + both if add else both

    gather_out = BucketCopy(here, rows_own, out, out_sems, local_sems.at[1], width, OUT_CUT)
    gather_gt = BucketCopy(here, gt_own, gt, gt_sems, local_sems.at[2], width, GRAD_CUT)
    small = Total(here, steps, step_bufs, vec_sems)
    a_in = pltpu.make_async_copy(a_kept, a_v, local_sems.at[3])

    tok_in[0].wait()
    norms(0)
    take(0)
    tok_in[1].wait()
    norms(1)
    take(1)
    take(2)
    tables()
    tok_in[2].wait()
    norm_project(2, 0)
    take(3)
    take(4)
    tok_in[3].wait()
    norm_project(3, 1)
    take(5)
    take(6)
    a_out = pltpu.make_async_copy(a_v, a_kept, local_sems.at[0])
    a_out.start()
    project(2)
    take(7)
    project(3)
    take(8)
    take(9)
    attend(2)
    take(10)
    feed_up(2)
    take(11)
    for copy in cot_in + [x_in]:
        copy.start()
    await_greetings(7)
    a_out.wait()
    feed_down(2)
    branch.far.send_opp()
    attend_up(1)
    feed_down(1)
    branch.far.send_right()
    attend_up(3)
    feed_down(3)
    branch.far.send_left()
    branch.far.relay()
    attend_up(0)
    feed_down(0)
    mask_all()
    branch.add_across(2)
    branch.near.send_opp()
    mixed_back()
    attend_back(3)
    attend_back(2)
    branch.add_across(1)
    branch.near.send_right()
    attend_back(1)
    branch.add_across(3)
    branch.near.send_left()
    branch.pass_far()
    attend_back(0)
    project_back()
    into_norms(2)
    wide.far.send_opp()
    branch.near.relay()
    into_norms(1)
    wide.far.send_right()
    branch.add_across(0)
    into_norms(3)
    wide.far.send_left()
    into_norms(0)
    wide.add_across(2)
    wide.near.send_opp()
    grads_two(2)
    small.start()
    grads_two(1)
    wide.far.relay()
    out_rows()
    branch.finish()
    a_in.start()
    gather_out.send_cut()
    small.step()
    gather_out.start()
    gather_out.send_rest()
    two.add_core(1)
    two.ring.send_right()
    a_in.wait()
    grads_one(2)
    two.add_core(2)
    two.ring.send_opp()
    grads_two(3)
    small.step()
    wide.pass_far()
    grads_one(1)
    wide.add_across(3)
    wide.near.send_left()
    wide.add_across(1)
    wide.near.send_right()
    two.add_core(3)
    two.ring.send_left()
    wide.near.relay()
    one.add_core(2)
    one.ring.send_opp()
    grads_two(0)
    grads_one(3)
    small.step()
    wide.add_across(0)
    one.add_core(3)
    one.ring.send_left()
    gather_out.pass_near()
    gather_out.cross_near()
    gt_rows()
    gather_gt.send_rest()
    small.step()
    gather_gt.start()
    two.add_core(0)
    two.ring.relay()
    gather_gt.send_cut()
    small.step()
    one.add_core(1)
    one.ring.send_right()
    gather_out.cross_opp()
    grads_one(0)
    one.ring.relay()
    gather_out.start_far()
    gather_gt.pass_near()
    gather_gt.cross_near()
    small.step()
    one.add_core(0)
    pack_two(two.cross(), False)
    gather_out.pass_far()
    small.step()
    gather_gt.start_far()
    gather_gt.cross_opp()
    pack_one(one.cross(), False)
    gather_gt.pass_far()
    pack_two(two.rest(), True)
    pack_one(one.rest(), True)
    tail[...] = jnp.zeros_like(tail)
    tail[0:4, :HS] = steps[7, 0:4, aligned(here.mp * HS, HS)]
    tail[4:5, :HS] = steps[4, 4:5, aligned(here.mp * HS, HS)]
    tail[5:6, : 3 * HS] = steps[4, 5:6, : 3 * HS]
    tail[6:7, :hidden] = steps[4, 6:7, :hidden]
    packed_out = pltpu.make_async_copy(st.at[1, pl.ds(0, packed.shape[0])], packed, local_sems.at[4])
    packed_out.start()
    wide.finish()
    one.finish()
    two.finish()
    small.finish()
    gather_out.finish()
    gather_gt.finish()
    packed_out.wait()


def any_space():
    return pl.BlockSpec(memory_space=pl.ANY)


def vmem_space():
    return pl.BlockSpec(memory_space=pltpu.VMEM)


def rotary_tables(rows):
    inverse = np.exp(np.arange(ROT // 2) * (-2.0 * math.log(10000.0) / ROT))
    angle = np.arange(rows)[:, None] * inverse[None, :]
    cos_of, sin_of = np.ones((rows, 128)), np.zeros((rows, 128))
    freq = np.zeros((8, 128))
    for first in (0, ROT // 2):
        part = slice(first, first + ROT // 2)
        cos_of[:, part], sin_of[:, part] = np.cos(angle), np.sin(angle)
        freq[:, part] = inverse
    return np.stack([cos_of, sin_of]).astype(np.float32), freq.astype(np.float32)


def whole(lengths, tokens, cotangent, norms, wq, bq, wo, wu, bu, wd, bb):
    rows, width = tokens.shape
    hidden = wu.shape[1]
    turn, freq = rotary_tables(rows)
    shape = jax.ShapeDtypeStruct
    wide_in, tall_out = hidden + 3 * HS, hidden + HS
    outs = (
        shape((rows, width), bf16),
        shape((rows, width), bf16),
        shape((wide_in // HS * HALF + tall_out // 2, HS), f32),
        shape((8, hidden), f32),
        shape((rows, width), bf16),
    )
    v = pltpu.VMEM
    dma = pltpu.SemaphoreType.DMA

    def sum_bufs(cut):
        return [v((6, SUB, width), bf16), v((6, SUB, cut), bf16), v((4, HALF, width - cut), bf16), v((HALF, cut), bf16)]

    def grad_bufs(*part):
        return [v((4, *part), bf16), v((6, *part), bf16), v(part, bf16)]

    return pl.pallas_call(
        whole_kernel,
        out_shape=outs,
        in_specs=[
            pl.BlockSpec(memory_space=pltpu.SMEM), any_space(), any_space(), *[vmem_space()] * 4, any_space(),
            vmem_space(), any_space(), vmem_space(), any_space(), any_space(), vmem_space(), any_space(), vmem_space(),
        ],
        out_specs=(any_space(),) * 3 + (vmem_space(), any_space()),
        scratch_shapes=[
            v((rows, width), bf16), v((rows, width), bf16), v((rows, width), bf16), v((rows, width), bf16),
            v((width, wide_in), bf16), v((tall_out, width), bf16), v((SLOTS, width, HS), f32), v((rows, 3 * HS), bf16),
            v((rows, HS), bf16), v((rows, HS), bf16), v((2, rows, 128), f32), v((rows, 2), f32),
            v((rows, hidden), bf16), v((rows, hidden), bf16),
            v((HALF, width), bf16), v((HALF, width), bf16),
            *sum_bufs(BRANCH_CUT), *sum_bufs(NORM_CUT), *grad_bufs(HALF, wide_in), *grad_bufs(tall_out, HALF),
            v((8, 8, width), f32), v((7, 8, width), f32),
            dma((10,)), dma((23,)), dma((5,)), dma((2, BucketSum.LINKS)), dma((2, BucketSum.LINKS)),
            dma((2, BucketCopy.LINKS)), dma((2, BucketCopy.LINKS)), dma((2, GradSum.LINKS)), dma((2, GradSum.LINKS)),
            dma((2, 7)), pltpu.SemaphoreType.REGULAR((2,)), pltpu.SemaphoreType.REGULAR((2,)),
        ],
        compiler_params=pltpu.CompilerParams(
            collective_id=0, has_side_effects=True, vmem_limit_bytes=63 * MIB + 768 * 1024
        ),
        name="whole",
    )(lengths, tokens, cotangent, *norms, turn, freq, wq, bq, wo, wu, bu, wd, bb)


def finish_kernel(
    gathered, gathered_grad, packed, tail,
    output, grad_tokens, up, down, qkv, out, one_gain, one_bias, two_gain, two_bias, qkv_bias, up_bias, bias,
    wide_v, packed_v, tail_v, in_sems, out_sems,
):
    pieces = up.shape[1] // HS
    first = (pieces + 3) * HALF
    tall = (down.shape[0] + out.shape[0]) // 2
    over = down.shape[0] - tall
    left, right = pl.ds(0, HALF), pl.ds(HALF, HALF)
    parts = gathered.shape[0] // HALF
    moves, back = [(tail, tail_v), (packed, packed_v)], []
    for slot, (src, dst) in enumerate(((gathered, output), (gathered_grad, grad_tokens))):
        for k in range(parts):
            part = pl.ds(k * HALF, HALF)
            moves.append((src.at[part], wide_v.at[slot, part]))
            back.append((wide_v.at[slot, part], dst.at[part]))
    back += [(packed_v.at[pl.ds(j * HALF, HALF)], up.at[:, pl.ds(j * HS, HS)]) for j in range(pieces)]
    back += [(packed_v.at[pl.ds((pieces + j) * HALF, HALF)], qkv.at[j]) for j in range(3)]
    back += [
        (packed_v.at[pl.ds(first, tall), left], down.at[pl.ds(0, tall)]),
        (packed_v.at[pl.ds(first, over), right], down.at[pl.ds(tall, over)]),
        (packed_v.at[pl.ds(first + over, tall - over), right], out),
    ]
    loads = [pltpu.make_async_copy(src, dst, in_sems.at[i]) for i, (src, dst) in enumerate(moves)]
    stores = [pltpu.make_async_copy(src, dst, out_sems.at[i]) for i, (src, dst) in enumerate(back)]
    for copy in loads:
        copy.start()
    loads[0].wait()
    for row, ref in enumerate((one_gain, one_bias, two_gain, two_bias, bias)):
        ref[...] = tail_v[row, :HS]
    for j in range(3):
        qkv_bias[j : j + 1, :] = tail_v[5:6, pl.ds(j * HS, HS)]
    up_bias[...] = tail_v[6, :]
    loads[1].wait()
    for store in stores[2 * parts :]:
        store.start()
    for load, store in zip(loads[2:], stores):
        load.wait()
        store.start()
    for store in stores:
        store.wait()


def finish(gathered, gathered_grad, packed, tail):
    rows, width = gathered.shape
    hidden = tail.shape[1]
    shape = jax.ShapeDtypeStruct
    dma = pltpu.SemaphoreType.DMA
    moves = 2 * rows // HALF
    return pl.pallas_call(
        finish_kernel,
        out_shape=(
            shape(gathered.shape, bf16), shape(gathered.shape, bf16),
            shape((HALF, hidden), f32), shape((hidden, HALF), f32), shape((3, HALF, HS), f32), shape((HS, HALF), f32),
            shape((HS,), f32), shape((HS,), f32), shape((HS,), f32), shape((HS,), f32),
            shape((3, HS), f32), shape((hidden,), f32), shape((HS,), f32),
        ),
        in_specs=[any_space()] * 4,
        out_specs=(any_space(),) * 6 + (vmem_space(),) * 7,
        scratch_shapes=[
            pltpu.VMEM((2, rows, width), bf16), pltpu.VMEM(packed.shape, f32), pltpu.VMEM(tail.shape, f32),
            dma((moves + 2,)), dma((moves + hidden // HS + 6,)),
        ],
        compiler_params=pltpu.CompilerParams(vmem_limit_bytes=62 * MIB),
        name="finish",
    )(gathered, gathered_grad, packed, tail)


def local(
    tokens, lengths, ln1_gain, ln1_bias, ln2_gain, ln2_bias, qkv_master, qkv_bias, out_master, up_master, up_bias,
    down_master, branch_bias, cotangent,
):
    norms = [vector.reshape(1, -1) for vector in (ln1_gain, ln1_bias, ln2_gain, ln2_bias)]
    w_qkv = jnp.transpose(qkv_master, (1, 0, 2))
    gathered, gathered_grad, packed, tail, _ = whole(
        lengths, tokens, cotangent, norms, w_qkv, qkv_bias, out_master, up_master,
        up_bias.reshape(1, -1), down_master, branch_bias.reshape(1, -1),
    )
    (
        output, grad_tokens, up, down, qkv, out, one_gain, one_bias, two_gain, two_bias,
        qkv_bias_sum, up_bias_sum, bias_sum,
    ) = finish(gathered, gathered_grad, packed, tail)
    return (
        output,
        grad_tokens,
        one_gain,
        one_bias,
        two_gain,
        two_bias,
        jnp.transpose(qkv, (1, 0, 2)),
        qkv_bias_sum,
        out,
        up,
        up_bias_sum,
        down,
        bias_sum,
    )


def solution(mesh):
    placed = (
        P("dp", None),
        P("dp", None),
        P(),
        P(),
        P(),
        P(),
        P(None, None, "mp"),
        P(None, "mp"),
        P("mp", None),
        P(None, "mp"),
        P("mp"),
        P("mp", None),
        P(),
        P("dp", None),
    )
    return jax.shard_map(
        local,
        mesh=mesh,
        in_specs=placed,
        out_specs=(
            P("dp", None),
            P("dp", None),
            P("mp"),
            P("mp"),
            P("mp"),
            P("mp"),
            P("dp", None, "mp"),
            P(None, "mp"),
            P("mp", "dp"),
            P("dp", "mp"),
            P("mp"),
            P("mp", "dp"),
            P("mp"),
        ),
        check_vma=False,
    )
```

```python
import math
from functools import partial

import jax
import jax.numpy as jnp
import numpy as np
from jax import lax
from jax.experimental import pallas as pl
from jax.experimental.pallas import tpu as pltpu
from jax.sharding import PartitionSpec as P

HS = 256
ROT = 64
BLK = 256
HALF = 128
SUB = 64
SLOTS = 2
BRANCH_CUT = 1280
NORM_CUT = 1280
OUT_CUT = 1280
GRAD_CUT = 1536
MESH = pl.DeviceIdType.MESH
MIB = 2**20
norm_eps = 1e-05
masked_value = -1e30
f32 = jnp.float32
bf16 = jnp.bfloat16


def dot_nn(a, b):
    return jnp.dot(a, b, preferred_element_type=f32)


def dot_nt(a, b):
    return lax.dot_general(a, b, (((1,), (1,)), ((), ())), preferred_element_type=f32)


def dot_tn(a, b):
    return lax.dot_general(a, b, (((0,), (0,)), ((), ())), preferred_element_type=f32)


def turn_off(k):
    return (2 + 3 * k + 3 * (k * (k - 1) // 2)) % 4


def in_turn(work, *after):
    @pl.loop(0, len(after))
    def _(k):
        work(turn_off(k))
        for i, actions in enumerate(after[:-1]):
            if actions:

                @pl.when(k == i)
                def _(actions=actions):
                    for action in actions:
                        action()

    for action in after[-1]:
        action()


def aligned(start, size, unit=None):
    if isinstance(start, int):
        return pl.ds(start, size)
    return pl.ds(pl.multiple_of(start, unit or size), size)


class Place:
    def __init__(self):
        self.dp = lax.axis_index("dp")
        self.mp = lax.axis_index("mp")
        self.x_hi = self.mp // 4
        self.y = self.mp % 4
        self.x_lo = self.dp // 8
        self.z = (self.dp // 2) % 4
        self.core = self.dp % 2

    def y_at(self, off):
        return (self.y + off) % 4

    def z_at(self, off):
        return (self.z + off) % 4

    def to_y(self, y):
        return (self.dp, self.x_hi * 4 + y)

    def ring_y(self):
        right, left = self.y_at(1), self.y_at(3)
        return self.y, right, self.y_at(2), left, self.to_y(right), self.to_y(left)

    def ring_z(self):
        right, left = self.z_at(1), self.z_at(3)
        return self.z, right, self.z_at(2), left, self.to_z(right), self.to_z(left)

    def to_x_hi(self):
        return (self.dp, (1 - self.x_hi) * 4 + self.y)

    def to_z(self, z):
        return ((self.x_lo * 4 + z) * 2 + self.core, self.mp)

    def to_x_lo(self):
        return (((1 - self.x_lo) * 4 + self.z) * 2 + self.core, self.mp)

    def to_core(self):
        return ((self.x_lo * 4 + self.z) * 2 + 1 - self.core, self.mp)


def greet(targets):
    for target in targets:
        pl.semaphore_signal(pltpu.get_barrier_semaphore(), inc=1, device_id=target, device_id_type=MESH)


def await_greetings(count):
    pl.semaphore_wait(pltpu.get_barrier_semaphore(), count)


class Link:
    def __init__(self, sems, number, src, dst, target):
        self.copy = pltpu.make_async_remote_copy(
            src_ref=src,
            dst_ref=dst,
            send_sem=sems.at[0, number],
            recv_sem=sems.at[1, number],
            device_id=target,
            device_id_type=MESH,
        )

    def start(self):
        self.copy.start()

    def got(self):
        self.copy.wait_recv()

    def sent(self):
        self.copy.wait_send()


class RingSum:
    def __init__(self, ring, src, at, buf, sems, base):
        self.src, self.at, self.buf = src, at, buf
        self.own, self.right, self.opp, self.left, to_right, to_left = ring
        part = lambda place, half: src.at[at(place, half)]
        self.links = [
            Link(sems, base + 0, part(self.opp, 0), buf.at[0], to_right),
            Link(sems, base + 1, part(self.opp, 1), buf.at[1], to_left),
            Link(sems, base + 2, part(self.right, 0), buf.at[2], to_right),
            Link(sems, base + 3, part(self.right, 1), buf.at[3], to_right),
            Link(sems, base + 4, part(self.left, 1), buf.at[4], to_left),
            Link(sems, base + 5, part(self.left, 0), buf.at[5], to_left),
        ]

    def send_opp(self):
        self.links[0].start()
        self.links[1].start()

    def send_right(self):
        self.links[3].start()

    def send_left(self):
        self.links[5].start()

    def relay(self):
        for number, place, half in ((0, self.right, 0), (1, self.left, 1)):
            self.links[number].got()
            at = self.at(place, half)
            self.src[at] = (self.src[at].astype(f32) + self.buf[number].astype(f32)).astype(bf16)
            self.links[2 if number == 0 else 4].start()

    def total(self, half):
        one, two = (2, 5) if half == 0 else (4, 3)
        self.links[one].got()
        self.links[two].got()
        own = self.src[self.at(self.own, half)].astype(f32)
        return own + self.buf[one].astype(f32) + self.buf[two].astype(f32)

    def finish(self):
        for link in self.links:
            link.sent()


class BucketSum:
    LINKS = 17

    def __init__(self, here, src, buf_wide, buf_cut, buf_x, buf_far, sems, width, cut):
        self.here, self.src, self.buf_x, self.buf_far, self.width, self.at_cut = here, src, buf_x, buf_far, width, cut
        self.cut, self.rest = pl.ds(0, cut), pl.ds(cut, width - cut)
        self.first_own = lambda y: y * BLK + here.x_hi * HALF
        self.first_far = lambda y: y * BLK + (1 - here.x_hi) * HALF

        def halves(first, cols):
            return lambda y, half: (aligned(first(y) + half * SUB, SUB), cols)

        self.far = RingSum(here.ring_y(), src, halves(self.first_far, self.cut), buf_cut, sems, 0)
        self.near = RingSum(here.ring_y(), src, halves(self.first_own, pl.ds(0, width)), buf_wide, sems, 6)
        self.across = [
            Link(
                sems,
                12 + off,
                src.at[aligned(self.first_far(here.y_at(off)), HALF), self.rest],
                buf_x.at[off],
                here.to_x_hi(),
            )
            for off in range(4)
        ]
        own_far = src.at[aligned(self.first_far(here.y), HALF), self.cut]
        self.last = Link(sems, 16, own_far, buf_far, here.to_x_hi())

    def add_across(self, off):
        self.across[off].got()
        rows = aligned(self.first_own(self.here.y_at(off)), HALF)
        self.src[rows, self.rest] = (
            self.src[rows, self.rest].astype(f32) + self.buf_x[off].astype(f32)
        ).astype(bf16)

    def pass_far(self):
        for half in range(2):
            self.src[self.far.at(self.here.y, half)] = self.far.total(half).astype(bf16)
        self.last.start()

    def total(self, half):
        if half == 0:
            self.last.got()
        near = self.near.total(half)
        far = self.buf_far[pl.ds(half * SUB, SUB), :].astype(f32)
        return jnp.concatenate([near[:, : self.at_cut] + far, near[:, self.at_cut :]], axis=1)

    def finish(self):
        self.far.finish()
        self.near.finish()
        for link in self.across:
            link.sent()
        self.last.sent()


class RingCopy:
    LINKS = 6

    def __init__(self, here, own, out, first, cols, sems, base):
        self.out, self.first, self.cols = out, first, cols
        own_y, right, _, left, to_right, to_left = here.ring_y()
        part = self.part
        halves = [own.at[pl.ds(half * SUB, SUB)] for half in range(2)]
        self.links = [
            Link(sems, base + 0, halves[0], part(own_y, 0), to_right),
            Link(sems, base + 1, halves[1], part(own_y, 1), to_left),
            Link(sems, base + 2, part(left, 0), part(left, 0), to_right),
            Link(sems, base + 3, part(right, 1), part(right, 1), to_left),
            Link(sems, base + 4, halves[1], part(own_y, 1), to_right),
            Link(sems, base + 5, halves[0], part(own_y, 0), to_left),
        ]

    def part(self, y, half=None, cols=None):
        if half is None:
            rows = aligned(self.first(y), HALF)
        else:
            rows = aligned(self.first(y) + half * SUB, SUB)
        return self.out.at[rows, self.cols if cols is None else cols]

    def start(self):
        for number in (0, 1, 4, 5):
            self.links[number].start()

    def pass_on(self):
        for near, far in ((0, 2), (1, 3)):
            self.links[near].got()
            self.links[far].start()

    def rest(self):
        self.links[4].got()
        self.links[5].got()

    def opposite(self):
        self.links[2].got()
        self.links[3].got()

    def finish(self):
        for link in self.links:
            link.sent()


class BucketCopy:
    LINKS = 18

    def __init__(self, here, own, out, sems, local_sem, width, cut):
        cut, rest = pl.ds(0, cut), pl.ds(cut, width - cut)
        first_own = lambda y: y * BLK + here.x_hi * HALF
        first_far = lambda y: y * BLK + (1 - here.x_hi) * HALF
        self.near = RingCopy(here, own, out, first_own, pl.ds(0, width), sems, 0)
        far_own = out.at[aligned(first_far(here.y), HALF), cut]
        self.far = RingCopy(here, far_own, out, first_far, cut, sems, RingCopy.LINKS)
        part = self.near.part
        y, right, opp, left, _, _ = here.ring_y()
        moves = [(own.at[:, cut], part(y, cols=cut)), (own.at[:, rest], part(y, cols=rest))]
        for place, half in ((left, None), (right, None), (opp, 0), (opp, 1)):
            moves.append((part(place, half, rest), part(place, half, rest)))
        self.across = [Link(sems, 2 * RingCopy.LINKS + i, src, dst, here.to_x_hi()) for i, (src, dst) in enumerate(moves)]
        self.keep = pltpu.make_async_copy(own, part(y), local_sem)

    def start(self):
        self.near.start()
        self.keep.start()

    def send_cut(self):
        self.across[0].start()

    def send_rest(self):
        self.across[1].start()

    def start_far(self):
        self.across[0].got()
        self.far.start()

    def pass_near(self):
        self.near.pass_on()

    def cross_near(self):
        self.near.rest()
        self.across[2].start()
        self.across[3].start()

    def cross_opp(self):
        for i in range(2):
            self.near.links[2 + i].got()
            self.across[4 + i].start()

    def pass_far(self):
        self.far.pass_on()

    def finish(self):
        self.far.rest()
        self.far.opposite()
        for link in self.across[1:]:
            link.got()
        for link in self.across:
            link.sent()
        self.near.finish()
        self.far.finish()
        self.keep.wait()


class GradSum:
    ORDER = (2, 1, 3, 0)
    LINKS = 15

    def __init__(self, here, grads, at, buf_core, buf_ring, buf_last, sems, free_sems):
        self.here, self.grads, self.buf_core, self.buf_last, self.free_sems = here, grads, buf_core, buf_last, free_sems
        self.at = lambda x_lo, z, core: at((x_lo * 4 + z) * 2 + core)
        self.cores = {
            off: [
                Link(
                    sems,
                    turn * 2 + x_lo,
                    grads.at[self.at(x_lo, here.z_at(off), 1 - here.core)],
                    buf_core.at[(turn % 2) * 2 + x_lo],
                    here.to_core(),
                )
                for x_lo in range(2)
            ]
            for turn, off in enumerate(self.ORDER)
        }
        self.ring = RingSum(here.ring_z(), grads, lambda z, half: self.at(half, z, here.core), buf_ring, sems, 8)
        self.other = self.at(1 - here.x_lo, here.z, here.core)
        self.last = Link(sems, 14, grads.at[self.other], buf_last, here.to_x_lo())

    def swap(self, off):
        turn = self.ORDER.index(off)
        if turn >= 2:
            pl.semaphore_wait(self.free_sems.at[turn % 2], 1)
        for link in self.cores[off]:
            link.start()

    def add_core(self, off):
        turn = self.ORDER.index(off)
        for x_lo in range(2):
            self.cores[off][x_lo].got()
            at = self.at(x_lo, self.here.z_at(off), self.here.core)
            self.grads[at] = (
                self.grads[at].astype(f32) + self.buf_core[(turn % 2) * 2 + x_lo].astype(f32)
            ).astype(bf16)
        if turn < 2:
            pl.semaphore_signal(
                self.free_sems.at[turn], inc=1, device_id=self.here.to_core(), device_id_type=MESH
            )

    def cross(self):
        low, high = self.ring.total(0), self.ring.total(1)
        mine = self.here.x_lo == 0
        self.grads[self.other] = jnp.where(mine, high, low).astype(bf16)
        self.last.start()
        return jnp.where(mine, low, high)

    def rest(self):
        self.last.got()
        return self.buf_last[...].astype(f32)

    def finish(self):
        for links in self.cores.values():
            for link in links:
                link.sent()
        self.last.sent()
        self.ring.finish()


class Total:
    def __init__(self, here, steps, bufs, sems):
        self.steps, self.bufs, self.at = steps, bufs, 0
        z_pair, y_pair = here.z + 1 - 2 * (here.z % 2), here.y + 1 - 2 * (here.y % 2)
        targets = [
            here.to_core(), here.to_z(z_pair), here.to_z(3 - here.z), here.to_x_lo(),
            here.to_y(y_pair), here.to_y(3 - here.y), here.to_x_hi(),
        ]
        self.links = [Link(sems, i, steps.at[i], bufs.at[i], target) for i, target in enumerate(targets)]

    def start(self):
        self.links[0].start()

    def step(self):
        i = self.at
        self.links[i].got()
        self.steps[i + 1] = self.steps[i] + self.bufs[i]
        self.at = i + 1
        if self.at < len(self.links):
            self.links[self.at].start()

    def finish(self):
        for link in self.links:
            link.sent()


def gelu_parts(v):
    cdf = 0.5 * (1.0 + lax.erf(v * (1.0 / math.sqrt(2.0))))
    slope = cdf + v * (jnp.exp(-0.5 * v * v) * (1.0 / math.sqrt(2.0 * math.pi)))
    return v * cdf, slope


def row_stats(load, width):
    tiles = width // 128
    total = load(0)
    for tile in range(1, tiles):
        total = total + load(tile)
    mean = jnp.sum(total, axis=-1, keepdims=True) * (1.0 / width)
    square = jnp.zeros_like(total)
    for tile in range(tiles):
        centred = load(tile) - mean
        square = square + centred * centred
    var = jnp.sum(square, axis=-1, keepdims=True) * (1.0 / width)
    return mean, lax.rsqrt(var + norm_eps)


def whole_kernel(
    lens, tok, cot, one_gain, one_bias, two_gain, two_bias, turn, freq, wq, bq, wo, wu, bu, wd, bb,
    out, gt, packed, tail, a_kept,
    tok_v, a_v, b_v, e_v, w_in, w_out, st, qkv_v, o_v, do_v, tabs, stats, g_v, du_v, rows_own, gt_own,
    z_wide, z_cut, z_x, z_far, s_wide, s_cut, s_x, s_far,
    one_core, one_ring, one_last, two_core, two_ring, two_last, steps, step_bufs,
    in_sems, st_sems, local_sems, z_sems, s_sems, out_sems, gt_sems, one_sems, two_sems, vec_sems, one_free, two_free,
):
    here = Place()
    rows_all, width = tok_v.shape
    hidden = g_v.shape[1]
    blocks = rows_all // BLK
    scale = 1.0 / math.sqrt(HS)
    qkv_first = hidden

    ring, ring_z = here.ring_y(), here.ring_z()
    greet([ring[4], ring[5], here.to_x_hi(), ring_z[4], ring_z[5], here.to_core(), here.to_x_lo()])

    def block_of(i):
        return pl.ds(i * BLK, BLK)

    def column(k):
        return pl.ds(k * HS, HS)

    tok_in = [pltpu.make_async_copy(tok.at[block_of(i)], tok_v.at[block_of(i)], in_sems.at[i]) for i in range(blocks)]
    cot_in = [pltpu.make_async_copy(cot.at[block_of(i)], e_v.at[block_of(i)], in_sems.at[blocks + i]) for i in range(blocks)]
    own_first = here.y * BLK + here.x_hi * HALF
    x_in = pltpu.make_async_copy(tok.at[aligned(own_first, HALF)], gt_own, in_sems.at[2 * blocks])
    turn_in = pltpu.make_async_copy(turn, tabs, in_sems.at[2 * blocks + 1])

    pieces = [((wq.at[j], (pl.ds(0, width),)),) for j in range(3)]
    pieces += [((wu.at[:, column(k)], (pl.ds(0, width),)),) for k in range(hidden // HS)]
    pieces += [tuple((wo.at[:, column(k)], (column(k),)) for k in range(width // HS))]
    pieces += [
        tuple((wd.at[:, column(k)], (pl.ds((k % 2) * hidden, hidden),)) for k in (2 * j, 2 * j + 1))
        for j in range(width // HS // 2)
    ]
    loads, number = [], 0
    for i, piece in enumerate(pieces):
        copies = []
        for src, (rows,) in piece:
            copies.append(pltpu.make_async_copy(src, st.at[i % SLOTS, rows], st_sems.at[number]))
            number += 1
        loads.append(copies)

    def load(i):
        if i < len(loads):
            for copy in loads[i]:
                copy.start()

    def take(i):
        for copy in loads[i]:
            copy.wait()
        slot = i % SLOTS
        if i < 7:
            first = qkv_first + i * HS if i < 3 else (i - 3) * HS

            @pl.loop(0, width // BLK)
            def _(r):
                rows = aligned(r * BLK, BLK)
                w_in[rows, pl.ds(first, HS)] = st[slot, rows, :].astype(bf16)

        elif i == 7:
            for k in range(width // HS):
                w_out[hidden:, column(k)] = st[slot, column(k), :].astype(bf16)
        else:
            for k in range(2):
                cols = column(2 * (i - 8) + k)

                @pl.loop(0, hidden // BLK)
                def _(r):
                    rows = aligned(r * BLK, BLK)
                    w_out[rows, cols] = st[slot, aligned(k * hidden + r * BLK, BLK), :].astype(bf16)

        load(i + SLOTS)

    tok_in[0].start()
    tok_in[1].start()
    for i in range(SLOTS):
        load(i)
    tok_in[2].start()
    turn_in.start()
    tok_in[3].start()

    end = []
    for j in range(4):
        end.append(lens[0, j] + (end[-1] if j else 0))

    def first_of(t):
        low = jnp.zeros_like(t)
        for j in range(4):
            low = jnp.where(t >= end[j], end[j], low)
        return low

    steps[0] = jnp.zeros(steps.shape[1:], f32)

    chunk = 64

    def norms(i):
        @pl.loop(0, BLK // chunk)
        def _(c):
            norm_chunk(aligned(i * BLK + c * chunk, chunk))

    def norm_chunk(rows):
        def tile_of(tile):
            return tok_v[rows, pl.ds(tile * 128, 128)].astype(f32)

        mean, rstd = row_stats(tile_of, width)
        stats[rows, 0:1] = mean
        stats[rows, 1:2] = rstd
        for tile in range(width // 128):
            cols = pl.ds(tile * 128, 128)
            normed = (tile_of(tile) - mean) * rstd
            a_v[rows, cols] = (normed * one_gain[:, cols] + one_bias[:, cols]).astype(bf16)
            b_v[rows, cols] = (normed * two_gain[:, cols] + two_bias[:, cols]).astype(bf16)

    def tables():
        starts = [jnp.int32(0)] + end[:3]
        lane_row = lax.broadcasted_iota(jnp.int32, (8, 128), 0)
        shift = jnp.zeros((8, 128), jnp.int32)
        for j in range(4):
            shift = jnp.where(lane_row == j, starts[j], shift)
        phase = shift.astype(f32) * freq[...]
        shift_cos, shift_sin = jnp.cos(phase), jnp.sin(phase)
        turn_in.wait()

        @pl.loop(0, rows_all // HALF)
        def _(i):
            rows = aligned(i * HALF, HALF)
            t = lax.broadcasted_iota(jnp.int32, (HALF, 128), 0) + i * HALF
            lane = lax.broadcasted_iota(jnp.int32, (HALF, 128), 1)
            c_of = jnp.broadcast_to(shift_cos[0:1], (HALF, 128))
            s_of = jnp.broadcast_to(shift_sin[0:1], (HALF, 128))
            for j in range(4):
                c_of = jnp.where(t >= end[j], shift_cos[j + 1 : j + 2], c_of)
                s_of = jnp.where(t >= end[j], shift_sin[j + 1 : j + 2], s_of)
            t_cos, t_sin = tabs[0, rows], tabs[1, rows]
            sin_of = t_sin * c_of - t_cos * s_of
            tabs[0, rows] = t_cos * c_of + t_sin * s_of
            tabs[1, rows] = jnp.where(lane < ROT // 2, -sin_of, sin_of)

    def turned(wide, sign, rows):
        low = wide[:, :128]
        lane = lax.broadcasted_iota(jnp.int32, low.shape, 1)
        other = jnp.where(lane < ROT // 2, pltpu.roll(low, 128 - ROT // 2, 1), pltpu.roll(low, ROT // 2, 1))
        low = low * tabs[0, rows] + sign * (other * tabs[1, rows])
        return jnp.concatenate([low, wide[:, 128:]], axis=1)

    def project(i):
        rows = aligned(i * BLK, BLK)
        mixed = dot_nn(a_v[rows, :], w_in[:, qkv_first:])
        for j in range(3):
            part = mixed[:, j * HS : (j + 1) * HS] + bq[j : j + 1, :]
            qkv_v[rows, column(j)] = (turned(part, 1.0, rows) if j < 2 else part).astype(bf16)

    def probabilities(first, seen):
        rows = aligned(first, BLK)
        t = lax.broadcasted_iota(jnp.int32, (BLK, 1), 0) + first
        key_at = lax.broadcasted_iota(jnp.int32, (BLK, seen), 1)
        scores = dot_nt(qkv_v[rows, :HS], qkv_v[:seen, HS : 2 * HS]) * scale
        scores = jnp.where((key_at >= first_of(t)) & (key_at <= t), scores, masked_value)
        weights = jnp.exp(scores - jnp.max(scores, axis=-1, keepdims=True))
        return weights * (1.0 / jnp.sum(weights, axis=-1, keepdims=True))

    def attend(off):
        first = here.y_at(off) * BLK
        probs = probabilities(first, rows_all).astype(bf16)
        o_v[aligned(first, BLK), :] = dot_nn(probs, qkv_v[:, 2 * HS :]).astype(bf16)

    def mask(i):
        rows = aligned(i * BLK, BLK)
        t = lax.broadcasted_iota(jnp.int32, (BLK, 1), 0) + i * BLK
        used = (t < end[3]).astype(f32)

        @pl.loop(0, width // 512)
        def _(c):
            cols = aligned(c * 512, 512)
            kept = e_v[rows, cols].astype(f32) * used
            e_v[rows, cols] = kept.astype(bf16)
            steps[0, 4:5, cols] += jnp.sum(kept, axis=0, keepdims=True)

    def mask_all():
        for copy in cot_in:
            copy.wait()
        pl.loop(0, blocks)(mask)

    def mixed_back():
        do_v[...] = dot_nt(e_v[...], w_out[hidden:, :]).astype(bf16)

    def attend_back(i):
        rows, seen = block_of(i), (i + 1) * BLK
        query, keys, values = qkv_v[rows, :HS], qkv_v[:seen, HS : 2 * HS], qkv_v[:seen, 2 * HS :]
        probs = probabilities(i * BLK, seen)
        grad_mixed = do_v[rows, :]
        grad_probs = dot_nt(grad_mixed, values)
        row_dot = jnp.sum(probs * grad_probs, axis=-1, keepdims=True)
        grad_scores = (probs * (grad_probs - row_dot)).astype(bf16)
        grad_query = dot_nn(grad_scores, keys) * scale
        grad_keys = dot_tn(grad_scores, query) * scale
        grad_values = dot_tn(probs.astype(bf16), grad_mixed)
        if i == blocks - 1:
            st[0, :seen] = grad_keys
            st[0, pl.ds(rows_all, seen)] = grad_values
        else:
            st[0, :seen] += grad_keys
            st[0, pl.ds(rows_all, seen)] += grad_values
        qkv_v[rows, :HS] = turned(grad_query, -1.0, rows).astype(bf16)

    def project_back():
        for i in range(blocks):
            rows = block_of(i)
            qkv_v[rows, HS : 2 * HS] = turned(st[0, rows], -1.0, rows).astype(bf16)
            qkv_v[rows, 2 * HS :] = st[0, pl.ds(rows_all + i * BLK, BLK)].astype(bf16)
            steps[0, 5:6, : 3 * HS] += jnp.sum(qkv_v[rows, :].astype(f32), axis=0, keepdims=True)

    z_v = a_v
    branch = BucketSum(here, z_v, z_wide, z_cut, z_x, z_far, z_sems, width, BRANCH_CUT)

    def feed_up(off):
        rows = aligned(here.y_at(off) * BLK, BLK)
        act, slope = gelu_parts(dot_nn(b_v[rows, :], w_in[:, :hidden]) + bu[...])
        g_v[rows, :] = act.astype(bf16)
        du_v[rows, :] = slope.astype(bf16)

    def feed_down(off):
        rows = aligned(here.y_at(off) * BLK, BLK)

        @pl.loop(0, 2)
        def _(c):
            cols = aligned(c * (width // 2), width // 2)
            z_v[rows, cols] = (
                dot_nn(o_v[rows, :], w_out[hidden:, cols]) + dot_nn(g_v[rows, :], w_out[:hidden, cols])
            ).astype(bf16)

    def out_rows():
        x_in.wait()
        t = lax.broadcasted_iota(jnp.int32, (SUB, 1), 0) + own_first
        for half in range(2):
            rows = pl.ds(half * SUB, SUB)
            used = (t + half * SUB < end[3]).astype(f32)
            rows_own[rows, :] = (used * (gt_own[rows, :].astype(f32) + branch.total(half) + bb[...])).astype(bf16)

    def attend_up(off):
        attend(off)
        feed_up(off)

    wide = BucketSum(here, tok_v, s_wide, s_cut, s_x, s_far, s_sems, width, NORM_CUT)

    def into_norms(off):
        rows = aligned(here.y_at(off) * BLK, BLK)
        grad_low = (dot_nt(e_v[rows, :], w_out[:hidden, :]) * du_v[rows, :].astype(f32)).astype(bf16)
        du_v[rows, :] = grad_low
        steps[0, 6:7, :hidden] += jnp.sum(grad_low.astype(f32), axis=0, keepdims=True)
        mean, rstd = stats[rows, 0:1], stats[rows, 1:2]

        @pl.loop(0, 4)
        def _(c):
            cols = aligned(c * (width // 4), width // 4)
            da = dot_nt(qkv_v[rows, :], w_in[cols, qkv_first:])
            db = dot_nt(du_v[rows, :], w_in[cols, :hidden])
            normed = (tok_v[rows, cols].astype(f32) - mean) * rstd
            steps[0, 0:1, cols] += jnp.sum(da * normed, axis=0, keepdims=True)
            steps[0, 1:2, cols] += jnp.sum(da, axis=0, keepdims=True)
            steps[0, 2:3, cols] += jnp.sum(db * normed, axis=0, keepdims=True)
            steps[0, 3:4, cols] += jnp.sum(db, axis=0, keepdims=True)
            tok_v[rows, cols] = (da * one_gain[:, cols] + db * two_gain[:, cols]).astype(bf16)

    def gt_rows():
        for half in range(2):
            rows = pl.ds(half * SUB, SUB)
            total = wide.total(half)
            x = gt_own[rows, :].astype(f32)
            centred = x - jnp.mean(x, axis=-1, keepdims=True)
            rstd = lax.rsqrt(jnp.mean(centred * centred, axis=-1, keepdims=True) + norm_eps)
            normed = centred * rstd
            grad = rstd * (
                total - jnp.mean(total, axis=-1, keepdims=True)
                - normed * jnp.mean(total * normed, axis=-1, keepdims=True)
            )
            gt_own[rows, :] = (e_v[aligned(own_first + half * SUB, SUB), :].astype(f32) + grad).astype(bf16)

    one = GradSum(
        here, w_in, lambda block: (aligned(block * HALF, HALF), pl.ds(0, w_in.shape[1])),
        one_core, one_ring, one_last, one_sems, one_free,
    )
    two = GradSum(
        here, w_out, lambda block: (pl.ds(0, w_out.shape[0]), aligned(block * HALF, HALF)),
        two_core, two_ring, two_last, two_sems, two_free,
    )

    def grads_one(off):
        @pl.loop(0, 2)
        def _(x_lo):
            m = aligned((x_lo * 4 + here.z_at(off)) * BLK, BLK)
            w_in[m, :hidden] = dot_tn(b_v[:, m], du_v[...]).astype(bf16)
            w_in[m, qkv_first:] = dot_tn(a_v[:, m], qkv_v[...]).astype(bf16)

    def grads_two(off):
        @pl.loop(0, 2)
        def _(x_lo):
            m = aligned((x_lo * 4 + here.z_at(off)) * BLK, BLK)
            w_out[:hidden, m] = dot_tn(g_v[...], e_v[:, m]).astype(bf16)
            w_out[hidden:, m] = dot_tn(o_v[...], e_v[:, m]).astype(bf16)

    def pack_one(part, add):
        for j in range(w_in.shape[1] // HS):
            rows = pl.ds(j * HALF, HALF)
            tile = part[:, j * HS : (j + 1) * HS]
            st[1, rows, :] = st[1, rows, :] + tile if add else tile

    def pack_two(part, add):
        tall = w_out.shape[0] // 2
        rows = pl.ds((w_in.shape[1] // HS) * HALF, tall)
        both = jnp.concatenate([part[:tall], part[tall:]], axis=1)
        st[1, rows, :] = st[1, rows, :] + both if add else both

    def cross_one():
        pack_one(one.cross(), False)

    def rest_one():
        pack_one(one.rest(), True)

    def cross_two():
        pack_two(two.cross(), False)

    def rest_two():
        pack_two(two.rest(), True)

    gather_out = BucketCopy(here, rows_own, out, out_sems, local_sems.at[1], width, OUT_CUT)
    gather_gt = BucketCopy(here, gt_own, gt, gt_sems, local_sems.at[2], width, GRAD_CUT)
    small = Total(here, steps, step_bufs, vec_sems)
    a_in = pltpu.make_async_copy(a_kept, a_v, local_sems.at[3])

    tok_in[0].wait()
    norms(0)
    take(0)
    tok_in[1].wait()
    norms(1)
    take(1)
    take(2)
    tables()
    tok_in[2].wait()
    norms(2)
    take(3)
    take(4)
    tok_in[3].wait()
    norms(3)
    take(5)
    take(6)
    a_out = pltpu.make_async_copy(a_v, a_kept, local_sems.at[0])
    a_out.start()

    @pl.loop(0, blocks)
    def _(i):
        project(i)

        @pl.when(i == 0)
        def _():
            take(7)

        @pl.when(i == 1)
        def _():
            take(8)

        @pl.when(i == 2)
        def _():
            take(9)

    def first_feed():
        take(11)
        for copy in cot_in + [x_in]:
            copy.start()
        await_greetings(7)
        a_out.wait()

    def feed(off):
        attend_up(off)
        pl.when(off == 2)(first_feed)
        feed_down(off)

    take(10)
    in_turn(
        feed,
        [branch.across[2].start, branch.far.send_opp],
        [branch.across[1].start, branch.far.send_right],
        [branch.across[3].start, branch.far.send_left, branch.far.relay],
        [branch.across[0].start],
    )
    mask_all()
    branch.add_across(2)
    branch.near.send_opp()
    mixed_back()
    attend_back(3)
    branch.add_across(1)
    branch.near.send_right()
    attend_back(2)
    branch.add_across(3)
    branch.near.send_left()
    attend_back(1)
    attend_back(0)
    project_back()
    branch.pass_far()
    in_turn(
        into_norms,
        [wide.across[2].start, wide.far.send_opp, branch.near.relay],
        [wide.across[1].start, wide.far.send_right],
        [wide.across[3].start, wide.far.send_left, partial(branch.add_across, 0)],
        [wide.across[0].start],
    )
    wide.far.relay()
    in_turn(
        grads_two,
        [partial(two.swap, 2), partial(wide.add_across, 2), wide.near.send_opp, small.start],
        [partial(two.swap, 1), out_rows, small.step, partial(two.add_core, 2), two.ring.send_opp, partial(two.add_core, 1), two.ring.send_right, gather_out.start, branch.finish, a_in.start, gather_out.send_rest, partial(wide.add_across, 1), wide.near.send_right, wide.pass_far, small.step],
        [partial(two.swap, 3), partial(wide.add_across, 3), wide.near.send_left, gather_out.send_cut, partial(two.add_core, 3), two.ring.send_left, small.step],
        [partial(two.swap, 0)],
    )
    two.ring.relay()
    wide.near.relay()
    a_in.wait()
    in_turn(
        grads_one,
        [partial(one.swap, 2), gather_out.pass_near, gather_out.cross_near],
        [partial(one.swap, 1), partial(wide.add_across, 0), small.step, partial(one.add_core, 2), one.ring.send_opp],
        [partial(one.swap, 3), gt_rows, gather_gt.send_cut, gather_gt.start, partial(one.add_core, 1), one.ring.send_right, partial(one.add_core, 3), one.ring.send_left, gather_out.cross_opp, partial(two.add_core, 0), small.step, cross_two, one.ring.relay, gather_out.start_far],
        [partial(one.swap, 0)],
    )
    gather_gt.pass_near()
    one.add_core(0)
    small.step()
    gather_gt.cross_near()
    gather_gt.start_far()
    gather_gt.send_rest()
    cross_one()
    gather_out.pass_far()
    gather_gt.pass_far()
    gather_gt.cross_opp()
    small.step()
    rest_two()
    rest_one()
    tail[...] = jnp.zeros_like(tail)
    tail[0:4, :HS] = steps[7, 0:4, aligned(here.mp * HS, HS)]
    tail[4:5, :HS] = steps[4, 4:5, aligned(here.mp * HS, HS)]
    tail[5:6, : 3 * HS] = steps[4, 5:6, : 3 * HS]
    tail[6:7, :hidden] = steps[4, 6:7, :hidden]
    packed_out = pltpu.make_async_copy(st.at[1, pl.ds(0, packed.shape[0])], packed, local_sems.at[4])
    packed_out.start()
    wide.finish()
    one.finish()
    two.finish()
    small.finish()
    gather_out.finish()
    gather_gt.finish()
    packed_out.wait()


def any_space():
    return pl.BlockSpec(memory_space=pl.ANY)


def vmem_space():
    return pl.BlockSpec(memory_space=pltpu.VMEM)


def rotary_tables(rows):
    inverse = np.exp(np.arange(ROT // 2) * (-2.0 * math.log(10000.0) / ROT))
    angle = np.arange(rows)[:, None] * inverse[None, :]
    cos_of, sin_of = np.ones((rows, 128)), np.zeros((rows, 128))
    freq = np.zeros((8, 128))
    for first in (0, ROT // 2):
        part = slice(first, first + ROT // 2)
        cos_of[:, part], sin_of[:, part] = np.cos(angle), np.sin(angle)
        freq[:, part] = inverse
    return np.stack([cos_of, sin_of]).astype(np.float32), freq.astype(np.float32)


def whole(lengths, tokens, cotangent, norms, wq, bq, wo, wu, bu, wd, bb):
    rows, width = tokens.shape
    hidden = wu.shape[1]
    turn, freq = rotary_tables(rows)
    shape = jax.ShapeDtypeStruct
    wide_in, tall_out = hidden + 3 * HS, hidden + HS
    outs = (
        shape((rows, width), bf16),
        shape((rows, width), bf16),
        shape((wide_in // HS * HALF + tall_out // 2, HS), f32),
        shape((8, hidden), f32),
        shape((rows, width), bf16),
    )
    v = pltpu.VMEM
    dma = pltpu.SemaphoreType.DMA

    def sum_bufs(cut):
        return [v((6, SUB, width), bf16), v((6, SUB, cut), bf16), v((4, HALF, width - cut), bf16), v((HALF, cut), bf16)]

    def grad_bufs(*part):
        return [v((4, *part), bf16), v((6, *part), bf16), v(part, bf16)]

    return pl.pallas_call(
        whole_kernel,
        out_shape=outs,
        in_specs=[
            pl.BlockSpec(memory_space=pltpu.SMEM), any_space(), any_space(), *[vmem_space()] * 4, any_space(),
            vmem_space(), any_space(), vmem_space(), any_space(), any_space(), vmem_space(), any_space(), vmem_space(),
        ],
        out_specs=(any_space(),) * 3 + (vmem_space(), any_space()),
        scratch_shapes=[
            v((rows, width), bf16), v((rows, width), bf16), v((rows, width), bf16), v((rows, width), bf16),
            v((width, wide_in), bf16), v((tall_out, width), bf16), v((SLOTS, width, HS), f32), v((rows, 3 * HS), bf16),
            v((rows, HS), bf16), v((rows, HS), bf16), v((2, rows, 128), f32), v((rows, 2), f32),
            v((rows, hidden), bf16), v((rows, hidden), bf16),
            v((HALF, width), bf16), v((HALF, width), bf16),
            *sum_bufs(BRANCH_CUT), *sum_bufs(NORM_CUT), *grad_bufs(HALF, wide_in), *grad_bufs(tall_out, HALF),
            v((8, 8, width), f32), v((7, 8, width), f32),
            dma((10,)), dma((23,)), dma((5,)), dma((2, BucketSum.LINKS)), dma((2, BucketSum.LINKS)),
            dma((2, BucketCopy.LINKS)), dma((2, BucketCopy.LINKS)), dma((2, GradSum.LINKS)), dma((2, GradSum.LINKS)),
            dma((2, 7)), pltpu.SemaphoreType.REGULAR((2,)), pltpu.SemaphoreType.REGULAR((2,)),
        ],
        compiler_params=pltpu.CompilerParams(
            collective_id=0, has_side_effects=True, vmem_limit_bytes=63 * MIB + 768 * 1024
        ),
        name="whole",
    )(lengths, tokens, cotangent, *norms, turn, freq, wq, bq, wo, wu, bu, wd, bb)


def finish_kernel(
    gathered, gathered_grad, packed, tail,
    output, grad_tokens, up, down, qkv, out, one_gain, one_bias, two_gain, two_bias, qkv_bias, up_bias, bias,
    wide_v, packed_v, tail_v, in_sems, out_sems,
):
    pieces = up.shape[1] // HS
    first = (pieces + 3) * HALF
    tall = (down.shape[0] + out.shape[0]) // 2
    over = down.shape[0] - tall
    left, right = pl.ds(0, HALF), pl.ds(HALF, HALF)
    parts = gathered.shape[0] // HALF
    moves, back = [(tail, tail_v), (packed, packed_v)], []
    for slot, (src, dst) in enumerate(((gathered, output), (gathered_grad, grad_tokens))):
        for k in range(parts):
            part = pl.ds(k * HALF, HALF)
            moves.append((src.at[part], wide_v.at[slot, part]))
            back.append((wide_v.at[slot, part], dst.at[part]))
    back += [(packed_v.at[pl.ds(j * HALF, HALF)], up.at[:, pl.ds(j * HS, HS)]) for j in range(pieces)]
    back += [(packed_v.at[pl.ds((pieces + j) * HALF, HALF)], qkv.at[j]) for j in range(3)]
    back += [
        (packed_v.at[pl.ds(first, tall), left], down.at[pl.ds(0, tall)]),
        (packed_v.at[pl.ds(first, over), right], down.at[pl.ds(tall, over)]),
        (packed_v.at[pl.ds(first + over, tall - over), right], out),
    ]
    loads = [pltpu.make_async_copy(src, dst, in_sems.at[i]) for i, (src, dst) in enumerate(moves)]
    stores = [pltpu.make_async_copy(src, dst, out_sems.at[i]) for i, (src, dst) in enumerate(back)]
    for copy in loads:
        copy.start()
    loads[0].wait()
    for row, ref in enumerate((one_gain, one_bias, two_gain, two_bias, bias)):
        ref[...] = tail_v[row, :HS]
    for j in range(3):
        qkv_bias[j : j + 1, :] = tail_v[5:6, pl.ds(j * HS, HS)]
    up_bias[...] = tail_v[6, :]
    loads[1].wait()
    for store in stores[2 * parts :]:
        store.start()
    for load, store in zip(loads[2:], stores):
        load.wait()
        store.start()
    for store in stores:
        store.wait()


def finish(gathered, gathered_grad, packed, tail):
    rows, width = gathered.shape
    hidden = tail.shape[1]
    shape = jax.ShapeDtypeStruct
    dma = pltpu.SemaphoreType.DMA
    moves = 2 * rows // HALF
    return pl.pallas_call(
        finish_kernel,
        out_shape=(
            shape(gathered.shape, bf16), shape(gathered.shape, bf16),
            shape((HALF, hidden), f32), shape((hidden, HALF), f32), shape((3, HALF, HS), f32), shape((HS, HALF), f32),
            shape((HS,), f32), shape((HS,), f32), shape((HS,), f32), shape((HS,), f32),
            shape((3, HS), f32), shape((hidden,), f32), shape((HS,), f32),
        ),
        in_specs=[any_space()] * 4,
        out_specs=(any_space(),) * 6 + (vmem_space(),) * 7,
        scratch_shapes=[
            pltpu.VMEM((2, rows, width), bf16), pltpu.VMEM(packed.shape, f32), pltpu.VMEM(tail.shape, f32),
            dma((moves + 2,)), dma((moves + hidden // HS + 6,)),
        ],
        compiler_params=pltpu.CompilerParams(vmem_limit_bytes=62 * MIB),
        name="finish",
    )(gathered, gathered_grad, packed, tail)


def local(
    tokens, lengths, ln1_gain, ln1_bias, ln2_gain, ln2_bias, qkv_master, qkv_bias, out_master, up_master, up_bias,
    down_master, branch_bias, cotangent,
):
    norms = [vector.reshape(1, -1) for vector in (ln1_gain, ln1_bias, ln2_gain, ln2_bias)]
    w_qkv = jnp.transpose(qkv_master, (1, 0, 2))
    gathered, gathered_grad, packed, tail, _ = whole(
        lengths, tokens, cotangent, norms, w_qkv, qkv_bias, out_master, up_master,
        up_bias.reshape(1, -1), down_master, branch_bias.reshape(1, -1),
    )
    (
        output, grad_tokens, up, down, qkv, out, one_gain, one_bias, two_gain, two_bias,
        qkv_bias_sum, up_bias_sum, bias_sum,
    ) = finish(gathered, gathered_grad, packed, tail)
    return (
        output,
        grad_tokens,
        one_gain,
        one_bias,
        two_gain,
        two_bias,
        jnp.transpose(qkv, (1, 0, 2)),
        qkv_bias_sum,
        out,
        up,
        up_bias_sum,
        down,
        bias_sum,
    )


def solution(mesh):
    placed = (
        P("dp", None),
        P("dp", None),
        P(),
        P(),
        P(),
        P(),
        P(None, None, "mp"),
        P(None, "mp"),
        P("mp", None),
        P(None, "mp"),
        P("mp"),
        P("mp", None),
        P(),
        P("dp", None),
    )
    return jax.shard_map(
        local,
        mesh=mesh,
        in_specs=placed,
        out_specs=(
            P("dp", None),
            P("dp", None),
            P("mp"),
            P("mp"),
            P("mp"),
            P("mp"),
            P("dp", None, "mp"),
            P(None, "mp"),
            P("mp", "dp"),
            P("dp", "mp"),
            P("mp"),
            P("mp", "dp"),
            P("mp"),
        ),
        check_vma=False,
    )
```

```python
import math
from functools import partial

import jax
import jax.numpy as jnp
import numpy as np
from jax import lax
from jax.experimental import pallas as pl
from jax.experimental.pallas import tpu as pltpu
from jax.sharding import PartitionSpec as P

HS = 256
ROT = 64
BLK = 256
HALF = 128
SUB = 64
SLOTS = 2
BRANCH_CUT = 1280
NORM_CUT = 1280
OUT_CUT = 1280
GRAD_CUT = 1536
MESH = pl.DeviceIdType.MESH
MIB = 2**20
norm_eps = 1e-05
masked_value = -1e30
f32 = jnp.float32
bf16 = jnp.bfloat16


def dot_nn(a, b):
    return jnp.dot(a, b, preferred_element_type=f32)


def dot_nt(a, b):
    return lax.dot_general(a, b, (((1,), (1,)), ((), ())), preferred_element_type=f32)


def dot_tn(a, b):
    return lax.dot_general(a, b, (((0,), (0,)), ((), ())), preferred_element_type=f32)


def turn_off(k):
    return (2 + 3 * k + 3 * (k * (k - 1) // 2)) % 4


def in_turn(work, *after):
    @pl.loop(0, len(after))
    def _(k):
        work(turn_off(k))
        for i, actions in enumerate(after[:-1]):
            if actions:

                @pl.when(k == i)
                def _(actions=actions):
                    for action in actions:
                        action()

    for action in after[-1]:
        action()


def aligned(start, size, unit=None):
    if isinstance(start, int):
        return pl.ds(start, size)
    return pl.ds(pl.multiple_of(start, unit or size), size)


class Place:
    def __init__(self):
        self.dp = lax.axis_index("dp")
        self.mp = lax.axis_index("mp")
        self.x_hi = self.mp // 4
        self.y = self.mp % 4
        self.x_lo = self.dp // 8
        self.z = (self.dp // 2) % 4
        self.core = self.dp % 2

    def y_at(self, off):
        return (self.y + off) % 4

    def z_at(self, off):
        return (self.z + off) % 4

    def to_y(self, y):
        return (self.dp, self.x_hi * 4 + y)

    def ring_y(self):
        right, left = self.y_at(1), self.y_at(3)
        return self.y, right, self.y_at(2), left, self.to_y(right), self.to_y(left)

    def ring_z(self):
        right, left = self.z_at(1), self.z_at(3)
        return self.z, right, self.z_at(2), left, self.to_z(right), self.to_z(left)

    def to_x_hi(self):
        return (self.dp, (1 - self.x_hi) * 4 + self.y)

    def to_z(self, z):
        return ((self.x_lo * 4 + z) * 2 + self.core, self.mp)

    def to_x_lo(self):
        return (((1 - self.x_lo) * 4 + self.z) * 2 + self.core, self.mp)

    def to_core(self):
        return ((self.x_lo * 4 + self.z) * 2 + 1 - self.core, self.mp)


def greet(targets):
    for target in targets:
        pl.semaphore_signal(pltpu.get_barrier_semaphore(), inc=1, device_id=target, device_id_type=MESH)


def await_greetings(count):
    pl.semaphore_wait(pltpu.get_barrier_semaphore(), count)


class Link:
    def __init__(self, sems, number, src, dst, target):
        self.copy = pltpu.make_async_remote_copy(
            src_ref=src,
            dst_ref=dst,
            send_sem=sems.at[0, number],
            recv_sem=sems.at[1, number],
            device_id=target,
            device_id_type=MESH,
        )

    def start(self):
        self.copy.start()

    def got(self):
        self.copy.wait_recv()

    def sent(self):
        self.copy.wait_send()


class RingSum:
    def __init__(self, ring, src, at, buf, sems, base):
        self.src, self.at, self.buf = src, at, buf
        self.own, self.right, self.opp, self.left, to_right, to_left = ring
        part = lambda place, half: src.at[at(place, half)]
        self.links = [
            Link(sems, base + 0, part(self.opp, 0), buf.at[0], to_right),
            Link(sems, base + 1, part(self.opp, 1), buf.at[1], to_left),
            Link(sems, base + 2, part(self.right, 0), buf.at[2], to_right),
            Link(sems, base + 3, part(self.right, 1), buf.at[3], to_right),
            Link(sems, base + 4, part(self.left, 1), buf.at[4], to_left),
            Link(sems, base + 5, part(self.left, 0), buf.at[5], to_left),
        ]

    def send_opp(self):
        self.links[0].start()
        self.links[1].start()

    def send_right(self):
        self.links[3].start()

    def send_left(self):
        self.links[5].start()

    def relay(self):
        for number, place, half in ((0, self.right, 0), (1, self.left, 1)):
            self.links[number].got()
            at = self.at(place, half)
            self.src[at] = (self.src[at].astype(f32) + self.buf[number].astype(f32)).astype(bf16)
            self.links[2 if number == 0 else 4].start()

    def total(self, half):
        one, two = (2, 5) if half == 0 else (4, 3)
        self.links[one].got()
        self.links[two].got()
        own = self.src[self.at(self.own, half)].astype(f32)
        return own + self.buf[one].astype(f32) + self.buf[two].astype(f32)

    def finish(self):
        for link in self.links:
            link.sent()


class BucketSum:
    LINKS = 17

    def __init__(self, here, src, buf_wide, buf_cut, buf_x, buf_far, sems, width, cut):
        self.here, self.src, self.buf_x, self.buf_far, self.width, self.at_cut = here, src, buf_x, buf_far, width, cut
        self.cut, self.rest = pl.ds(0, cut), pl.ds(cut, width - cut)
        self.first_own = lambda y: y * BLK + here.x_hi * HALF
        self.first_far = lambda y: y * BLK + (1 - here.x_hi) * HALF

        def halves(first, cols):
            return lambda y, half: (aligned(first(y) + half * SUB, SUB), cols)

        self.far = RingSum(here.ring_y(), src, halves(self.first_far, self.cut), buf_cut, sems, 0)
        self.near = RingSum(here.ring_y(), src, halves(self.first_own, pl.ds(0, width)), buf_wide, sems, 6)
        self.across = [
            Link(
                sems,
                12 + off,
                src.at[aligned(self.first_far(here.y_at(off)), HALF), self.rest],
                buf_x.at[off],
                here.to_x_hi(),
            )
            for off in range(4)
        ]
        own_far = src.at[aligned(self.first_far(here.y), HALF), self.cut]
        self.last = Link(sems, 16, own_far, buf_far, here.to_x_hi())

    def add_across(self, off):
        self.across[off].got()
        rows = aligned(self.first_own(self.here.y_at(off)), HALF)
        self.src[rows, self.rest] = (
            self.src[rows, self.rest].astype(f32) + self.buf_x[off].astype(f32)
        ).astype(bf16)

    def pass_far(self):
        for half in range(2):
            self.src[self.far.at(self.here.y, half)] = self.far.total(half).astype(bf16)
        self.last.start()

    def total(self, half):
        if half == 0:
            self.last.got()
        near = self.near.total(half)
        far = self.buf_far[pl.ds(half * SUB, SUB), :].astype(f32)
        return jnp.concatenate([near[:, : self.at_cut] + far, near[:, self.at_cut :]], axis=1)

    def finish(self):
        self.far.finish()
        self.near.finish()
        for link in self.across:
            link.sent()
        self.last.sent()


class RingCopy:
    LINKS = 6

    def __init__(self, here, own, out, first, cols, sems, base):
        self.out, self.first, self.cols = out, first, cols
        own_y, right, _, left, to_right, to_left = here.ring_y()
        part = self.part
        halves = [own.at[pl.ds(half * SUB, SUB)] for half in range(2)]
        self.links = [
            Link(sems, base + 0, halves[0], part(own_y, 0), to_right),
            Link(sems, base + 1, halves[1], part(own_y, 1), to_left),
            Link(sems, base + 2, part(left, 0), part(left, 0), to_right),
            Link(sems, base + 3, part(right, 1), part(right, 1), to_left),
            Link(sems, base + 4, halves[1], part(own_y, 1), to_right),
            Link(sems, base + 5, halves[0], part(own_y, 0), to_left),
        ]

    def part(self, y, half=None, cols=None):
        if half is None:
            rows = aligned(self.first(y), HALF)
        else:
            rows = aligned(self.first(y) + half * SUB, SUB)
        return self.out.at[rows, self.cols if cols is None else cols]

    def start(self):
        for number in (0, 1, 4, 5):
            self.links[number].start()

    def pass_on(self):
        for near, far in ((0, 2), (1, 3)):
            self.links[near].got()
            self.links[far].start()

    def rest(self):
        self.links[4].got()
        self.links[5].got()

    def opposite(self):
        self.links[2].got()
        self.links[3].got()

    def finish(self):
        for link in self.links:
            link.sent()


class BucketCopy:
    LINKS = 18

    def __init__(self, here, own, out, sems, local_sem, width, cut):
        cut, rest = pl.ds(0, cut), pl.ds(cut, width - cut)
        first_own = lambda y: y * BLK + here.x_hi * HALF
        first_far = lambda y: y * BLK + (1 - here.x_hi) * HALF
        self.near = RingCopy(here, own, out, first_own, pl.ds(0, width), sems, 0)
        far_own = out.at[aligned(first_far(here.y), HALF), cut]
        self.far = RingCopy(here, far_own, out, first_far, cut, sems, RingCopy.LINKS)
        part = self.near.part
        y, right, opp, left, _, _ = here.ring_y()
        moves = [(own.at[:, cut], part(y, cols=cut)), (own.at[:, rest], part(y, cols=rest))]
        for place, half in ((left, None), (right, None), (opp, 0), (opp, 1)):
            moves.append((part(place, half, rest), part(place, half, rest)))
        self.across = [Link(sems, 2 * RingCopy.LINKS + i, src, dst, here.to_x_hi()) for i, (src, dst) in enumerate(moves)]
        self.keep = pltpu.make_async_copy(own, part(y), local_sem)

    def start(self):
        self.near.start()
        self.keep.start()

    def send_cut(self):
        self.across[0].start()

    def send_rest(self):
        self.across[1].start()

    def start_far(self):
        self.across[0].got()
        self.far.start()

    def pass_near(self):
        self.near.pass_on()

    def cross_near(self):
        self.near.rest()
        self.across[2].start()
        self.across[3].start()

    def cross_opp(self):
        for i in range(2):
            self.near.links[2 + i].got()
            self.across[4 + i].start()

    def pass_far(self):
        self.far.pass_on()

    def finish(self):
        self.far.rest()
        self.far.opposite()
        for link in self.across[1:]:
            link.got()
        for link in self.across:
            link.sent()
        self.near.finish()
        self.far.finish()


class GradSum:
    ORDER = (2, 1, 3, 0)
    LINKS = 15

    def __init__(self, here, grads, at, buf_core, buf_ring, buf_last, sems, free_sems):
        self.here, self.grads, self.buf_core, self.buf_last, self.free_sems = here, grads, buf_core, buf_last, free_sems
        self.at = lambda x_lo, z, core: at((x_lo * 4 + z) * 2 + core)
        self.cores = {
            off: [
                Link(
                    sems,
                    turn * 2 + x_lo,
                    grads.at[self.at(x_lo, here.z_at(off), 1 - here.core)],
                    buf_core.at[(turn % 2) * 2 + x_lo],
                    here.to_core(),
                )
                for x_lo in range(2)
            ]
            for turn, off in enumerate(self.ORDER)
        }
        self.ring = RingSum(here.ring_z(), grads, lambda z, half: self.at(half, z, here.core), buf_ring, sems, 8)
        self.other = self.at(1 - here.x_lo, here.z, here.core)
        self.last = Link(sems, 14, grads.at[self.other], buf_last, here.to_x_lo())

    def swap(self, off):
        turn = self.ORDER.index(off)
        if turn >= 2:
            pl.semaphore_wait(self.free_sems.at[turn % 2], 1)
        for link in self.cores[off]:
            link.start()

    def add_core(self, off):
        turn = self.ORDER.index(off)
        for x_lo in range(2):
            self.cores[off][x_lo].got()
            at = self.at(x_lo, self.here.z_at(off), self.here.core)
            self.grads[at] = (
                self.grads[at].astype(f32) + self.buf_core[(turn % 2) * 2 + x_lo].astype(f32)
            ).astype(bf16)
        if turn < 2:
            pl.semaphore_signal(
                self.free_sems.at[turn], inc=1, device_id=self.here.to_core(), device_id_type=MESH
            )

    def cross(self):
        low, high = self.ring.total(0), self.ring.total(1)
        mine = self.here.x_lo == 0
        self.grads[self.other] = jnp.where(mine, high, low).astype(bf16)
        self.last.start()
        return jnp.where(mine, low, high)

    def rest(self):
        self.last.got()
        return self.buf_last[...].astype(f32)

    def finish(self):
        for links in self.cores.values():
            for link in links:
                link.sent()
        self.last.sent()
        self.ring.finish()


class Total:
    def __init__(self, here, steps, bufs, sems):
        self.steps, self.bufs, self.at = steps, bufs, 0
        z_pair, y_pair = here.z + 1 - 2 * (here.z % 2), here.y + 1 - 2 * (here.y % 2)
        targets = [
            here.to_core(), here.to_z(z_pair), here.to_z(3 - here.z), here.to_x_lo(),
            here.to_y(y_pair), here.to_y(3 - here.y), here.to_x_hi(),
        ]
        self.links = [Link(sems, i, steps.at[i], bufs.at[i], target) for i, target in enumerate(targets)]

    def start(self):
        self.links[0].start()

    def step(self):
        i = self.at
        self.links[i].got()
        self.steps[i + 1] = self.steps[i] + self.bufs[i]
        self.at = i + 1
        if self.at < len(self.links):
            self.links[self.at].start()

    def finish(self):
        for link in self.links:
            link.sent()


def gelu_parts(v):
    cdf = 0.5 * (1.0 + lax.erf(v * (1.0 / math.sqrt(2.0))))
    slope = cdf + v * (jnp.exp(-0.5 * v * v) * (1.0 / math.sqrt(2.0 * math.pi)))
    return v * cdf, slope


def row_stats(load, width):
    tiles = width // 128
    total = load(0)
    for tile in range(1, tiles):
        total = total + load(tile)
    mean = jnp.sum(total, axis=-1, keepdims=True) * (1.0 / width)
    square = jnp.zeros_like(total)
    for tile in range(tiles):
        centred = load(tile) - mean
        square = square + centred * centred
    var = jnp.sum(square, axis=-1, keepdims=True) * (1.0 / width)
    return mean, lax.rsqrt(var + norm_eps)


def whole_kernel(
    lens, tok, cot, one_gain_h, one_bias_h, two_gain_h, two_bias_h, turn, freq_h, wq, bq_h, wo, wu, bu_h, wd, bb_h,
    out, gt, packed, tail, b_v, e_v,
    tail_v, tok_v, a_v, w_in, w_out, st, qkv_v, o_v, do_v, tabs, stats, g_v, du_v, rows_own, gt_own,
    z_wide, z_cut, z_x, z_far, s_wide, s_cut, s_x, s_far,
    one_core, one_ring, one_last, two_core, two_ring, two_last, steps, step_bufs,
    one_gain, one_bias, two_gain, two_bias, freq, bq, bu, bb,
    in_sems, st_sems, local_sems, z_sems, s_sems, out_sems, gt_sems, one_sems, two_sems, vec_sems, one_free, two_free,
):
    here = Place()
    rows_all, width = tok_v.shape
    hidden = g_v.shape[1]
    blocks = rows_all // BLK
    scale = 1.0 / math.sqrt(HS)
    qkv_first = hidden

    ring, ring_z = here.ring_y(), here.ring_z()
    greet([ring[4], ring[5], here.to_x_hi(), ring_z[4], ring_z[5], here.to_core(), here.to_x_lo()])

    def block_of(i):
        return pl.ds(i * BLK, BLK)

    def column(k):
        return pl.ds(k * HS, HS)

    tok_in = [pltpu.make_async_copy(tok.at[block_of(i)], tok_v.at[block_of(i)], in_sems.at[i]) for i in range(blocks)]
    cot_in = [pltpu.make_async_copy(cot.at[block_of(i)], e_v.at[block_of(i)], in_sems.at[blocks + i]) for i in range(blocks)]
    own_first = here.y * BLK + here.x_hi * HALF
    x_in = pltpu.make_async_copy(tok.at[aligned(own_first, HALF)], gt_own, in_sems.at[2 * blocks])
    turn_in = pltpu.make_async_copy(turn, tabs, in_sems.at[2 * blocks + 1])

    pieces = [((wq.at[j], (pl.ds(0, width),)),) for j in range(3)]
    pieces += [((wu.at[:, column(k)], (pl.ds(0, width),)),) for k in range(hidden // HS)]
    pieces += [tuple((wo.at[:, column(k)], (column(k),)) for k in range(width // HS))]
    pieces += [
        tuple((wd.at[:, column(k)], (pl.ds((k % 2) * hidden, hidden),)) for k in (2 * j, 2 * j + 1))
        for j in range(width // HS // 2)
    ]
    loads, number = [], 0
    for i, piece in enumerate(pieces):
        copies = []
        for src, (rows,) in piece:
            copies.append(pltpu.make_async_copy(src, st.at[i % SLOTS, rows], st_sems.at[number]))
            number += 1
        loads.append(copies)

    def load(i):
        if i < len(loads):
            for copy in loads[i]:
                copy.start()

    def take(i):
        for copy in loads[i]:
            copy.wait()
        slot = i % SLOTS
        if i < 7:
            first = qkv_first + i * HS if i < 3 else (i - 3) * HS

            @pl.loop(0, width // BLK)
            def _(r):
                rows = aligned(r * BLK, BLK)
                w_in[rows, pl.ds(first, HS)] = st[slot, rows, :].astype(bf16)

        elif i == 7:
            for k in range(width // HS):
                w_out[hidden:, column(k)] = st[slot, column(k), :].astype(bf16)
        else:
            for k in range(2):
                cols = column(2 * (i - 8) + k)

                @pl.loop(0, hidden // BLK)
                def _(r):
                    rows = aligned(r * BLK, BLK)
                    w_out[rows, cols] = st[slot, aligned(k * hidden + r * BLK, BLK), :].astype(bf16)

        load(i + SLOTS)

    small_pairs = [
        (one_gain_h, one_gain), (one_bias_h, one_bias), (two_gain_h, two_gain), (two_bias_h, two_bias),
        (freq_h, freq), (bq_h, bq), (bu_h, bu), (bb_h, bb),
    ]
    small_in = [
        pltpu.make_async_copy(src, dst, in_sems.at[2 * blocks + 2 + i]) for i, (src, dst) in enumerate(small_pairs)
    ]
    tok_in[0].start()
    for copy in small_in:
        copy.start()
    tok_in[1].start()
    for i in range(SLOTS):
        load(i)
    tok_in[2].start()
    turn_in.start()
    tok_in[3].start()

    end = []
    for j in range(4):
        end.append(lens[0, j] + (end[-1] if j else 0))

    def first_of(t):
        low = jnp.zeros_like(t)
        for j in range(4):
            low = jnp.where(t >= end[j], end[j], low)
        return low

    steps[0] = jnp.zeros(steps.shape[1:], f32)

    chunk = 64

    def norms(i):
        rows = aligned(i * BLK, BLK)
        pltpu.make_async_copy(tok.at[rows], tok_v.at[rows], in_sems.at[i]).wait()
        for c in range(BLK // chunk):
            norm_chunk(aligned(i * BLK + c * chunk, chunk))

    def norm_chunk(rows):
        def tile_of(tile):
            return tok_v[rows, pl.ds(tile * 128, 128)].astype(f32)

        mean, rstd = row_stats(tile_of, width)
        stats[rows, 0:1] = mean
        stats[rows, 1:2] = rstd
        for tile in range(width // 128):
            cols = pl.ds(tile * 128, 128)
            normed = (tile_of(tile) - mean) * rstd
            a_v[rows, cols] = (normed * one_gain[:, cols] + one_bias[:, cols]).astype(bf16)
            b_v[rows, cols] = (normed * two_gain[:, cols] + two_bias[:, cols]).astype(bf16)

    def tables():
        starts = [jnp.int32(0)] + end[:3]
        lane_row = lax.broadcasted_iota(jnp.int32, (8, 128), 0)
        shift = jnp.zeros((8, 128), jnp.int32)
        for j in range(4):
            shift = jnp.where(lane_row == j, starts[j], shift)
        phase = shift.astype(f32) * freq[...]
        shift_cos, shift_sin = jnp.cos(phase), jnp.sin(phase)
        turn_in.wait()

        @pl.loop(0, rows_all // HALF)
        def _(i):
            rows = aligned(i * HALF, HALF)
            t = lax.broadcasted_iota(jnp.int32, (HALF, 128), 0) + i * HALF
            lane = lax.broadcasted_iota(jnp.int32, (HALF, 128), 1)
            c_of = jnp.broadcast_to(shift_cos[0:1], (HALF, 128))
            s_of = jnp.broadcast_to(shift_sin[0:1], (HALF, 128))
            for j in range(4):
                c_of = jnp.where(t >= end[j], shift_cos[j + 1 : j + 2], c_of)
                s_of = jnp.where(t >= end[j], shift_sin[j + 1 : j + 2], s_of)
            t_cos, t_sin = tabs[0, rows], tabs[1, rows]
            sin_of = t_sin * c_of - t_cos * s_of
            tabs[0, rows] = t_cos * c_of + t_sin * s_of
            tabs[1, rows] = jnp.where(lane < ROT // 2, -sin_of, sin_of)

    def turned(wide, sign, rows):
        low = wide[:, :128]
        lane = lax.broadcasted_iota(jnp.int32, low.shape, 1)
        other = jnp.where(lane < ROT // 2, pltpu.roll(low, 128 - ROT // 2, 1), pltpu.roll(low, ROT // 2, 1))
        low = low * tabs[0, rows] + sign * (other * tabs[1, rows])
        return jnp.concatenate([low, wide[:, 128:]], axis=1)

    def project(i):
        rows = aligned(i * BLK, BLK)
        mixed = dot_nn(a_v[rows, :], w_in[:, qkv_first:])
        for j in range(3):
            part = mixed[:, j * HS : (j + 1) * HS] + bq[j : j + 1, :]
            qkv_v[rows, column(j)] = (turned(part, 1.0, rows) if j < 2 else part).astype(bf16)

    def probabilities(first, seen):
        rows = aligned(first, BLK)
        t = lax.broadcasted_iota(jnp.int32, (BLK, 1), 0) + first
        key_at = lax.broadcasted_iota(jnp.int32, (BLK, seen), 1)
        scores = dot_nt(qkv_v[rows, :HS], qkv_v[:seen, HS : 2 * HS]) * scale
        scores = jnp.where((key_at >= first_of(t)) & (key_at <= t), scores, masked_value)
        weights = jnp.exp(scores - jnp.max(scores, axis=-1, keepdims=True))
        return weights * (1.0 / jnp.sum(weights, axis=-1, keepdims=True))

    def attend(off):
        first = here.y_at(off) * BLK
        probs = probabilities(first, rows_all).astype(bf16)
        o_v[aligned(first, BLK), :] = dot_nn(probs, qkv_v[:, 2 * HS :]).astype(bf16)

    def mask(i):
        rows = aligned(i * BLK, BLK)
        t = lax.broadcasted_iota(jnp.int32, (BLK, 1), 0) + i * BLK
        used = (t < end[3]).astype(f32)

        @pl.loop(0, width // 512)
        def _(c):
            cols = aligned(c * 512, 512)
            kept = e_v[rows, cols].astype(f32) * used
            e_v[rows, cols] = kept.astype(bf16)
            steps[0, 4:5, cols] += jnp.sum(kept, axis=0, keepdims=True)

    def mask_all():
        for copy in cot_in:
            copy.wait()
        pl.loop(0, blocks)(mask)

    def mixed_back():
        do_v[...] = dot_nt(e_v[...], w_out[hidden:, :]).astype(bf16)

    def attend_back(i):
        rows, seen = block_of(i), (i + 1) * BLK
        query, keys, values = qkv_v[rows, :HS], qkv_v[:seen, HS : 2 * HS], qkv_v[:seen, 2 * HS :]
        probs = probabilities(i * BLK, seen)
        grad_mixed = do_v[rows, :]
        grad_probs = dot_nt(grad_mixed, values)
        row_dot = jnp.sum(probs * grad_probs, axis=-1, keepdims=True)
        grad_scores = (probs * (grad_probs - row_dot)).astype(bf16)
        grad_query = dot_nn(grad_scores, keys) * scale
        grad_keys = dot_tn(grad_scores, query) * scale
        grad_values = dot_tn(probs.astype(bf16), grad_mixed)
        if i == blocks - 1:
            st[0, :seen] = grad_keys
            st[0, pl.ds(rows_all, seen)] = grad_values
        else:
            st[0, :seen] += grad_keys
            st[0, pl.ds(rows_all, seen)] += grad_values
        qkv_v[rows, :HS] = turned(grad_query, -1.0, rows).astype(bf16)

    def project_back():
        for i in range(blocks):
            rows = block_of(i)
            qkv_v[rows, HS : 2 * HS] = turned(st[0, rows], -1.0, rows).astype(bf16)
            qkv_v[rows, 2 * HS :] = st[0, pl.ds(rows_all + i * BLK, BLK)].astype(bf16)
            steps[0, 5:6, : 3 * HS] += jnp.sum(qkv_v[rows, :].astype(f32), axis=0, keepdims=True)

    z_v = a_v
    branch = BucketSum(here, z_v, z_wide, z_cut, z_x, z_far, z_sems, width, BRANCH_CUT)

    def feed_up(off):
        rows = aligned(here.y_at(off) * BLK, BLK)
        act, slope = gelu_parts(dot_nn(b_v[rows, :], w_in[:, :hidden]) + bu[...])
        g_v[rows, :] = act.astype(bf16)
        du_v[rows, :] = slope.astype(bf16)

    def feed_down(off):
        rows = aligned(here.y_at(off) * BLK, BLK)

        @pl.loop(0, 2)
        def _(c):
            cols = aligned(c * (width // 2), width // 2)
            z_v[rows, cols] = (
                dot_nn(o_v[rows, :], w_out[hidden:, cols]) + dot_nn(g_v[rows, :], w_out[:hidden, cols])
            ).astype(bf16)

    def out_rows():
        x_in.wait()
        t = lax.broadcasted_iota(jnp.int32, (SUB, 1), 0) + own_first
        for half in range(2):
            rows = pl.ds(half * SUB, SUB)
            used = (t + half * SUB < end[3]).astype(f32)
            rows_own[rows, :] = (used * (gt_own[rows, :].astype(f32) + branch.total(half) + bb[...])).astype(bf16)

    def attend_up(off):
        attend(off)
        feed_up(off)

    wide = BucketSum(here, tok_v, s_wide, s_cut, s_x, s_far, s_sems, width, NORM_CUT)

    def into_norms(off):
        rows = aligned(here.y_at(off) * BLK, BLK)
        grad_low = (dot_nt(e_v[rows, :], w_out[:hidden, :]) * du_v[rows, :].astype(f32)).astype(bf16)
        du_v[rows, :] = grad_low
        steps[0, 6:7, :hidden] += jnp.sum(grad_low.astype(f32), axis=0, keepdims=True)
        mean, rstd = stats[rows, 0:1], stats[rows, 1:2]

        @pl.loop(0, 4)
        def _(c):
            cols = aligned(c * (width // 4), width // 4)
            da = dot_nt(qkv_v[rows, :], w_in[cols, qkv_first:])
            db = dot_nt(du_v[rows, :], w_in[cols, :hidden])
            normed = (tok_v[rows, cols].astype(f32) - mean) * rstd
            steps[0, 0:1, cols] += jnp.sum(da * normed, axis=0, keepdims=True)
            steps[0, 1:2, cols] += jnp.sum(da, axis=0, keepdims=True)
            steps[0, 2:3, cols] += jnp.sum(db * normed, axis=0, keepdims=True)
            steps[0, 3:4, cols] += jnp.sum(db, axis=0, keepdims=True)
            tok_v[rows, cols] = (da * one_gain[:, cols] + db * two_gain[:, cols]).astype(bf16)

    def gt_rows():
        for half in range(2):
            rows = pl.ds(half * SUB, SUB)
            total = wide.total(half)
            x = gt_own[rows, :].astype(f32)
            centred = x - jnp.mean(x, axis=-1, keepdims=True)
            rstd = lax.rsqrt(jnp.mean(centred * centred, axis=-1, keepdims=True) + norm_eps)
            normed = centred * rstd
            grad = rstd * (
                total - jnp.mean(total, axis=-1, keepdims=True)
                - normed * jnp.mean(total * normed, axis=-1, keepdims=True)
            )
            gt_own[rows, :] = (e_v[aligned(own_first + half * SUB, SUB), :].astype(f32) + grad).astype(bf16)

    one = GradSum(
        here, w_in, lambda block: (aligned(block * HALF, HALF), pl.ds(0, w_in.shape[1])),
        one_core, one_ring, one_last, one_sems, one_free,
    )
    two = GradSum(
        here, w_out, lambda block: (pl.ds(0, w_out.shape[0]), aligned(block * HALF, HALF)),
        two_core, two_ring, two_last, two_sems, two_free,
    )

    def grads_one(off):
        @pl.loop(0, 2)
        def _(x_lo):
            m = aligned((x_lo * 4 + here.z_at(off)) * BLK, BLK)
            w_in[m, :hidden] = dot_tn(b_v[:, m], du_v[...]).astype(bf16)
            w_in[m, qkv_first:] = dot_tn(a_v[:, m], qkv_v[...]).astype(bf16)

    def grads_two(off):
        @pl.loop(0, 2)
        def _(x_lo):
            m = aligned((x_lo * 4 + here.z_at(off)) * BLK, BLK)
            w_out[:hidden, m] = dot_tn(g_v[...], e_v[:, m]).astype(bf16)
            w_out[hidden:, m] = dot_tn(o_v[...], e_v[:, m]).astype(bf16)

    def pack_one(part, add):
        for j in range(w_in.shape[1] // HS):
            rows = pl.ds(j * HALF, HALF)
            tile = part[:, j * HS : (j + 1) * HS]
            st[1, rows, :] = st[1, rows, :] + tile if add else tile

    def pack_two(part, add):
        tall = w_out.shape[0] // 2
        rows = pl.ds((w_in.shape[1] // HS) * HALF, tall)
        both = jnp.concatenate([part[:tall], part[tall:]], axis=1)
        st[1, rows, :] = st[1, rows, :] + both if add else both

    def cross_one():
        pack_one(one.cross(), False)

    def rest_one():
        pack_one(one.rest(), True)

    def cross_two():
        pack_two(two.cross(), False)

    def rest_two():
        pack_two(two.rest(), True)

    gather_out = BucketCopy(here, rows_own, out, out_sems, local_sems.at[1], width, OUT_CUT)
    gather_gt = BucketCopy(here, gt_own, gt, gt_sems, local_sems.at[2], width, GRAD_CUT)
    small = Total(here, steps, step_bufs, vec_sems)
    a_in = pltpu.make_async_copy(tok, a_v, local_sems.at[3])

    def renew():
        a_in.wait()

        @pl.loop(0, rows_all // chunk)
        def _(c):
            rows = aligned(c * chunk, chunk)
            mean, rstd = stats[rows, 0:1], stats[rows, 1:2]
            for tile in range(width // 128):
                cols = pl.ds(tile * 128, 128)
                normed = (a_v[rows, cols].astype(f32) - mean) * rstd
                a_v[rows, cols] = (normed * one_gain[:, cols] + one_bias[:, cols]).astype(bf16)

    for copy in small_in:
        copy.wait()

    def after_norms(i):
        if i == 1:
            tables()
        for k in ((0,), (1, 2), (3, 4), (5, 6))[i]:
            take(k)

    @pl.loop(0, blocks)
    def _(i):
        norms(i)
        for k in range(blocks):
            pl.when(i == k)(partial(after_norms, k))


    @pl.loop(0, blocks)
    def _(i):
        project(i)
        for k in range(3):
            pl.when(i == k)(partial(take, 7 + k))

    def first_feed():
        take(11)
        for copy in cot_in + [x_in]:
            copy.start()
        await_greetings(7)

    def feed(off):
        attend_up(off)
        pl.when(off == 2)(first_feed)
        feed_down(off)

    take(10)
    out_done = pltpu.make_async_copy(out, e_v, local_sems.at[5])

    def gt_copies(x_hi, first_sem):
        parts = [aligned(y * BLK + x_hi * HALF, HALF) for y in range(4)]
        return [pltpu.make_async_copy(gt.at[part], b_v.at[part], local_sems.at[first_sem + i]) for i, part in enumerate(parts)]

    gt_near, gt_far = gt_copies(here.x_hi, 6), gt_copies(1 - here.x_hi, 10)

    def finish_out():
        gather_out.finish()
        gather_out.keep.wait()
        out_done.start()

    def near_done():
        gather_gt.keep.wait()
        for copy in gt_near:
            copy.start()

    in_turn(
        feed,
        [branch.across[2].start, branch.far.send_opp],
        [branch.across[1].start, branch.far.send_right],
        [branch.across[3].start, branch.far.send_left, branch.far.relay],
        [branch.across[0].start],
    )
    branch.add_across(2)
    branch.near.send_opp()
    mask_all()
    mixed_back()
    attend_back(3)
    branch.add_across(1)
    branch.near.send_right()
    attend_back(2)
    branch.add_across(3)
    branch.near.send_left()
    attend_back(1)
    attend_back(0)
    project_back()
    branch.pass_far()
    in_turn(
        into_norms,
        [wide.across[2].start, wide.far.send_opp, partial(branch.add_across, 0), branch.near.relay],
        [wide.across[1].start, wide.far.send_right],
        [wide.across[3].start, wide.far.send_left],
        [wide.across[0].start],
    )
    small.start()
    wide.add_across(2)
    wide.near.send_opp()
    wide.far.relay()
    in_turn(
        grads_two,
        [partial(two.swap, 2), out_rows, small.step],
        [partial(two.swap, 1), gather_out.start, gather_out.send_cut, branch.finish, a_in.start, partial(two.add_core, 2), two.ring.send_opp, partial(wide.add_across, 1), wide.near.send_right],
        [partial(two.swap, 3), partial(two.add_core, 1), two.ring.send_right, partial(wide.add_across, 3), wide.near.send_left, renew],
        [partial(two.swap, 0)],
    )
    wide.add_across(0)
    small.step()
    two.add_core(3)
    two.ring.send_left()
    wide.pass_far()
    in_turn(
        grads_one,
        [partial(one.swap, 2)],
        [partial(one.swap, 1), gather_out.send_rest, partial(one.add_core, 2), one.ring.send_opp, wide.near.relay, small.step, gather_out.pass_near, gather_out.cross_near, partial(two.add_core, 0)],
        [partial(one.swap, 3), two.ring.relay, gt_rows, gather_gt.send_rest, gather_gt.send_cut, small.step, gather_gt.start, partial(one.add_core, 1), one.ring.send_right, partial(one.add_core, 3), one.ring.send_left, gather_out.start_far, cross_two],
        [partial(one.swap, 0)],
    )
    small.step()
    gather_out.cross_opp()
    one.ring.relay()
    gather_out.pass_far()
    one.add_core(0)
    gather_gt.pass_near()
    gather_gt.cross_near()
    gather_gt.start_far()
    small.step()
    cross_one()
    gather_gt.pass_far()
    gather_gt.cross_opp()
    near_done()
    small.step()
    rest_two()
    rest_one()
    finish_out()
    tail_v[...] = jnp.zeros_like(tail_v)
    tail_v[0:4, :HS] = steps[7, 0:4, aligned(here.mp * HS, HS)]
    tail_v[4:5, :HS] = steps[4, 4:5, aligned(here.mp * HS, HS)]
    tail_v[5:6, : 3 * HS] = steps[4, 5:6, : 3 * HS]
    tail_v[6:7, :hidden] = steps[4, 6:7, :hidden]
    tail_out = pltpu.make_async_copy(tail_v, tail, local_sems.at[0])
    tail_out.start()
    packed_out = pltpu.make_async_copy(st.at[1, pl.ds(0, packed.shape[0])], packed, local_sems.at[4])
    packed_out.start()
    wide.finish()
    one.finish()
    two.finish()
    small.finish()
    gather_gt.finish()
    for copy in gt_far:
        copy.start()
    for copy in [tail_out, packed_out, out_done] + gt_near + gt_far:
        copy.wait()


def any_space():
    return pl.BlockSpec(memory_space=pl.ANY)


def vmem_space():
    return pl.BlockSpec(memory_space=pltpu.VMEM)


def rotary_tables(rows):
    inverse = np.exp(np.arange(ROT // 2) * (-2.0 * math.log(10000.0) / ROT))
    angle = np.arange(rows)[:, None] * inverse[None, :]
    cos_of, sin_of = np.ones((rows, 128)), np.zeros((rows, 128))
    freq = np.zeros((8, 128))
    for first in (0, ROT // 2):
        part = slice(first, first + ROT // 2)
        cos_of[:, part], sin_of[:, part] = np.cos(angle), np.sin(angle)
        freq[:, part] = inverse
    return np.stack([cos_of, sin_of]).astype(np.float32), freq.astype(np.float32)


def whole(lengths, tokens, cotangent, norms, wq, bq, wo, wu, bu, wd, bb):
    rows, width = tokens.shape
    hidden = wu.shape[1]
    turn, freq = rotary_tables(rows)
    shape = jax.ShapeDtypeStruct
    wide_in, tall_out = hidden + 3 * HS, hidden + HS
    outs = (
        shape((rows, width), bf16),
        shape((rows, width), bf16),
        shape((wide_in // HS * HALF + tall_out // 2, HS), f32),
        shape((8, hidden), f32),
        pltpu.VMEM((rows, width), bf16),
        pltpu.VMEM((rows, width), bf16),
    )
    v = pltpu.VMEM
    dma = pltpu.SemaphoreType.DMA

    def sum_bufs(cut):
        return [v((6, SUB, width), bf16), v((6, SUB, cut), bf16), v((4, HALF, width - cut), bf16), v((HALF, cut), bf16)]

    def grad_bufs(*part):
        return [v((4, *part), bf16), v((6, *part), bf16), v(part, bf16)]

    return pl.pallas_call(
        whole_kernel,
        out_shape=outs,
        in_specs=[pl.BlockSpec(memory_space=pltpu.SMEM)] + [any_space()] * 15,
        out_specs=(any_space(),) * 4 + (vmem_space(),) * 2,
        scratch_shapes=[
            v((8, hidden), f32), v((rows, width), bf16), v((rows, width), bf16),
            v((width, wide_in), bf16), v((tall_out, width), bf16), v((SLOTS, width, HS), f32), v((rows, 3 * HS), bf16),
            v((rows, HS), bf16), v((rows, HS), bf16), v((2, rows, 128), f32), v((rows, 2), f32),
            v((rows, hidden), bf16), v((rows, hidden), bf16),
            v((HALF, width), bf16), v((HALF, width), bf16),
            *sum_bufs(BRANCH_CUT), *sum_bufs(NORM_CUT), *grad_bufs(HALF, wide_in), *grad_bufs(tall_out, HALF),
            v((8, 8, width), f32), v((7, 8, width), f32),
            *[v((1, width), f32)] * 4, v((8, 128), f32), v((3, HS), f32), v((1, hidden), f32), v((1, width), f32),
            dma((18,)), dma((23,)), dma((14,)), dma((2, BucketSum.LINKS)), dma((2, BucketSum.LINKS)),
            dma((2, BucketCopy.LINKS)), dma((2, BucketCopy.LINKS)), dma((2, GradSum.LINKS)), dma((2, GradSum.LINKS)),
            dma((2, 7)), pltpu.SemaphoreType.REGULAR((2,)), pltpu.SemaphoreType.REGULAR((2,)),
        ],
        compiler_params=pltpu.CompilerParams(
            collective_id=0, has_side_effects=True, vmem_limit_bytes=55 * MIB + 768 * 1024
        ),
        name="whole",
    )(lengths, tokens, cotangent, *norms, turn, freq, wq, bq, wo, wu, bu, wd, bb)


def finish_kernel(
    gathered, gathered_grad, packed, tail,
    output, grad_tokens, up, down, qkv, out, one_gain, one_bias, two_gain, two_bias, qkv_bias, up_bias, bias,
    packed_v, tail_v, in_sems, out_sems,
):
    pieces = up.shape[1] // HS
    first = (pieces + 3) * HALF
    tall = (down.shape[0] + out.shape[0]) // 2
    over = down.shape[0] - tall
    left, right = pl.ds(0, HALF), pl.ds(HALF, HALF)
    parts = gathered.shape[0] // HALF
    moves, back = [(tail, tail_v), (packed, packed_v)], []
    for src, dst in ((gathered, output), (gathered_grad, grad_tokens)):
        for k in range(parts):
            part = pl.ds(k * HALF, HALF)
            back.append((src.at[part], dst.at[part]))
    back += [(packed_v.at[pl.ds(j * HALF, HALF)], up.at[:, pl.ds(j * HS, HS)]) for j in range(pieces)]
    back += [(packed_v.at[pl.ds((pieces + j) * HALF, HALF)], qkv.at[j]) for j in range(3)]
    back += [
        (packed_v.at[pl.ds(first, tall), left], down.at[pl.ds(0, tall)]),
        (packed_v.at[pl.ds(first, over), right], down.at[pl.ds(tall, over)]),
        (packed_v.at[pl.ds(first + over, tall - over), right], out),
    ]
    loads = [pltpu.make_async_copy(src, dst, in_sems.at[i]) for i, (src, dst) in enumerate(moves)]
    stores = [pltpu.make_async_copy(src, dst, out_sems.at[i]) for i, (src, dst) in enumerate(back)]
    for copy in loads:
        copy.start()
    for store in stores[: 2 * parts]:
        store.start()
    loads[0].wait()
    for row, ref in enumerate((one_gain, one_bias, two_gain, two_bias, bias)):
        ref[...] = tail_v[row, :HS]
    for j in range(3):
        qkv_bias[j : j + 1, :] = tail_v[5:6, pl.ds(j * HS, HS)]
    up_bias[...] = tail_v[6, :]
    loads[1].wait()
    for store in stores[2 * parts :]:
        store.start()
    for store in stores:
        store.wait()


def finish(gathered, gathered_grad, packed, tail):
    rows, width = gathered.shape
    hidden = tail.shape[1]
    shape = jax.ShapeDtypeStruct
    dma = pltpu.SemaphoreType.DMA
    moves = 2 * rows // HALF
    return pl.pallas_call(
        finish_kernel,
        out_shape=(
            shape(gathered.shape, bf16), shape(gathered.shape, bf16),
            shape((HALF, hidden), f32), shape((hidden, HALF), f32), shape((3, HALF, HS), f32), shape((HS, HALF), f32),
            shape((HS,), f32), shape((HS,), f32), shape((HS,), f32), shape((HS,), f32),
            shape((3, HS), f32), shape((hidden,), f32), shape((HS,), f32),
        ),
        in_specs=[any_space()] * 4,
        out_specs=(any_space(),) * 6 + (vmem_space(),) * 7,
        scratch_shapes=[
            pltpu.VMEM(packed.shape, f32), pltpu.VMEM(tail.shape, f32),
            dma((2,)), dma((moves + hidden // HS + 6,)),
        ],
        compiler_params=pltpu.CompilerParams(vmem_limit_bytes=16 * MIB),
        name="finish",
    )(
        pltpu.with_memory_space_constraint(gathered, pltpu.VMEM),
        pltpu.with_memory_space_constraint(gathered_grad, pltpu.VMEM),
        pltpu.with_memory_space_constraint(packed, pltpu.HBM),
        pltpu.with_memory_space_constraint(tail, pltpu.HBM),
    )


def local(
    tokens, lengths, ln1_gain, ln1_bias, ln2_gain, ln2_bias, qkv_master, qkv_bias, out_master, up_master, up_bias,
    down_master, branch_bias, cotangent,
):
    norms = [vector.reshape(1, -1) for vector in (ln1_gain, ln1_bias, ln2_gain, ln2_bias)]
    w_qkv = jnp.transpose(qkv_master, (1, 0, 2))
    _, _, packed, tail, gathered_grad, gathered = whole(
        lengths, tokens, cotangent, norms, w_qkv, qkv_bias, out_master, up_master,
        up_bias.reshape(1, -1), down_master, branch_bias.reshape(1, -1),
    )
    (
        output, grad_tokens, up, down, qkv, out, one_gain, one_bias, two_gain, two_bias,
        qkv_bias_sum, up_bias_sum, bias_sum,
    ) = finish(gathered, gathered_grad, packed, tail)
    return (
        output,
        grad_tokens,
        one_gain,
        one_bias,
        two_gain,
        two_bias,
        jnp.transpose(qkv, (1, 0, 2)),
        qkv_bias_sum,
        out,
        up,
        up_bias_sum,
        down,
        bias_sum,
    )


def solution(mesh):
    placed = (
        P("dp", None),
        P("dp", None),
        P(),
        P(),
        P(),
        P(),
        P(None, None, "mp"),
        P(None, "mp"),
        P("mp", None),
        P(None, "mp"),
        P("mp"),
        P("mp", None),
        P(),
        P("dp", None),
    )
    return jax.shard_map(
        local,
        mesh=mesh,
        in_specs=placed,
        out_specs=(
            P("dp", None),
            P("dp", None),
            P("mp"),
            P("mp"),
            P("mp"),
            P("mp"),
            P("dp", None, "mp"),
            P(None, "mp"),
            P("mp", "dp"),
            P("dp", "mp"),
            P("mp"),
            P("mp", "dp"),
            P("mp"),
        ),
        check_vma=False,
    )
```

```python
import math
from functools import partial

import jax
import jax.numpy as jnp
import numpy as np
from jax import lax
from jax.experimental import pallas as pl
from jax.experimental.pallas import tpu as pltpu
from jax.sharding import PartitionSpec as P

HS = 256
ROT = 64
BLK = 256
HALF = 128
SUB = 64
SLOTS = 2
BRANCH_CUT = 1280
NORM_CUT = 1280
OUT_CUT = 1280
GRAD_CUT = 1536
MESH = pl.DeviceIdType.MESH
MIB = 2**20
norm_eps = 1e-05
masked_value = -1e30
f32 = jnp.float32
bf16 = jnp.bfloat16


def dot_nn(a, b):
    return jnp.dot(a, b, preferred_element_type=f32)


def dot_nt(a, b):
    return lax.dot_general(a, b, (((1,), (1,)), ((), ())), preferred_element_type=f32)


def dot_tn(a, b):
    return lax.dot_general(a, b, (((0,), (0,)), ((), ())), preferred_element_type=f32)


def turn_off(k):
    return (2 + 3 * k + 3 * (k * (k - 1) // 2)) % 4


def in_turn(work, *after):
    @pl.loop(0, len(after))
    def _(k):
        work(turn_off(k))
        for i, actions in enumerate(after[:-1]):
            if actions:

                @pl.when(k == i)
                def _(actions=actions):
                    for action in actions:
                        action()

    for action in after[-1]:
        action()


def aligned(start, size, unit=None):
    if isinstance(start, int):
        return pl.ds(start, size)
    return pl.ds(pl.multiple_of(start, unit or size), size)


class Place:
    def __init__(self):
        self.dp = lax.axis_index("dp")
        self.mp = lax.axis_index("mp")
        self.x_hi = self.mp // 4
        self.y = self.mp % 4
        self.x_lo = self.dp // 8
        self.z = (self.dp // 2) % 4
        self.core = self.dp % 2

    def y_at(self, off):
        return (self.y + off) % 4

    def z_at(self, off):
        return (self.z + off) % 4

    def to_y(self, y):
        return (self.dp, self.x_hi * 4 + y)

    def ring_y(self):
        right, left = self.y_at(1), self.y_at(3)
        return self.y, right, self.y_at(2), left, self.to_y(right), self.to_y(left)

    def ring_z(self):
        right, left = self.z_at(1), self.z_at(3)
        return self.z, right, self.z_at(2), left, self.to_z(right), self.to_z(left)

    def to_x_hi(self):
        return (self.dp, (1 - self.x_hi) * 4 + self.y)

    def to_z(self, z):
        return ((self.x_lo * 4 + z) * 2 + self.core, self.mp)

    def to_x_lo(self):
        return (((1 - self.x_lo) * 4 + self.z) * 2 + self.core, self.mp)

    def to_core(self):
        return ((self.x_lo * 4 + self.z) * 2 + 1 - self.core, self.mp)


def greet(targets):
    for target in targets:
        pl.semaphore_signal(pltpu.get_barrier_semaphore(), inc=1, device_id=target, device_id_type=MESH)


def await_greetings(count):
    pl.semaphore_wait(pltpu.get_barrier_semaphore(), count)


class Link:
    def __init__(self, sems, number, src, dst, target):
        self.copy = pltpu.make_async_remote_copy(
            src_ref=src,
            dst_ref=dst,
            send_sem=sems.at[0, number],
            recv_sem=sems.at[1, number],
            device_id=target,
            device_id_type=MESH,
        )

    def start(self):
        self.copy.start()

    def got(self):
        self.copy.wait_recv()

    def sent(self):
        self.copy.wait_send()


class RingSum:
    def __init__(self, ring, src, at, buf, sems, base):
        self.src, self.at, self.buf = src, at, buf
        self.own, self.right, self.opp, self.left, to_right, to_left = ring
        part = lambda place, half: src.at[at(place, half)]
        self.links = [
            Link(sems, base + 0, part(self.opp, 0), buf.at[0], to_right),
            Link(sems, base + 1, part(self.opp, 1), buf.at[1], to_left),
            Link(sems, base + 2, part(self.right, 0), buf.at[2], to_right),
            Link(sems, base + 3, part(self.right, 1), buf.at[3], to_right),
            Link(sems, base + 4, part(self.left, 1), buf.at[4], to_left),
            Link(sems, base + 5, part(self.left, 0), buf.at[5], to_left),
        ]

    def send_opp(self):
        self.links[0].start()
        self.links[1].start()

    def send_right(self):
        self.links[3].start()

    def send_left(self):
        self.links[5].start()

    def relay(self):
        for number, place, half in ((0, self.right, 0), (1, self.left, 1)):
            self.links[number].got()
            at = self.at(place, half)
            self.src[at] = (self.src[at].astype(f32) + self.buf[number].astype(f32)).astype(bf16)
            self.links[2 if number == 0 else 4].start()

    def total(self, half):
        one, two = (2, 5) if half == 0 else (4, 3)
        self.links[one].got()
        self.links[two].got()
        own = self.src[self.at(self.own, half)].astype(f32)
        return own + self.buf[one].astype(f32) + self.buf[two].astype(f32)

    def finish(self):
        for link in self.links:
            link.sent()


class BucketSum:
    LINKS = 17

    def __init__(self, here, src, buf_wide, buf_cut, buf_x, buf_far, sems, width, cut):
        self.here, self.src, self.buf_x, self.buf_far, self.width, self.at_cut = here, src, buf_x, buf_far, width, cut
        self.cut, self.rest = pl.ds(0, cut), pl.ds(cut, width - cut)
        self.first_own = lambda y: y * BLK + here.x_hi * HALF
        self.first_far = lambda y: y * BLK + (1 - here.x_hi) * HALF

        def halves(first, cols):
            return lambda y, half: (aligned(first(y) + half * SUB, SUB), cols)

        self.far = RingSum(here.ring_y(), src, halves(self.first_far, self.cut), buf_cut, sems, 0)
        self.near = RingSum(here.ring_y(), src, halves(self.first_own, pl.ds(0, width)), buf_wide, sems, 6)
        self.across = [
            Link(
                sems,
                12 + off,
                src.at[aligned(self.first_far(here.y_at(off)), HALF), self.rest],
                buf_x.at[off],
                here.to_x_hi(),
            )
            for off in range(4)
        ]
        own_far = src.at[aligned(self.first_far(here.y), HALF), self.cut]
        self.last = Link(sems, 16, own_far, buf_far, here.to_x_hi())

    def add_across(self, off):
        self.across[off].got()
        rows = aligned(self.first_own(self.here.y_at(off)), HALF)
        self.src[rows, self.rest] = (
            self.src[rows, self.rest].astype(f32) + self.buf_x[off].astype(f32)
        ).astype(bf16)

    def pass_far(self):
        for half in range(2):
            self.src[self.far.at(self.here.y, half)] = self.far.total(half).astype(bf16)
        self.last.start()

    def total(self, half):
        if half == 0:
            self.last.got()
        near = self.near.total(half)
        far = self.buf_far[pl.ds(half * SUB, SUB), :].astype(f32)
        return jnp.concatenate([near[:, : self.at_cut] + far, near[:, self.at_cut :]], axis=1)

    def finish(self):
        self.far.finish()
        self.near.finish()
        for link in self.across:
            link.sent()
        self.last.sent()


class RingCopy:
    LINKS = 6

    def __init__(self, here, own, out, first, cols, sems, base):
        self.out, self.first, self.cols = out, first, cols
        own_y, right, _, left, to_right, to_left = here.ring_y()
        part = self.part
        halves = [own.at[pl.ds(half * SUB, SUB)] for half in range(2)]
        self.links = [
            Link(sems, base + 0, halves[0], part(own_y, 0), to_right),
            Link(sems, base + 1, halves[1], part(own_y, 1), to_left),
            Link(sems, base + 2, part(left, 0), part(left, 0), to_right),
            Link(sems, base + 3, part(right, 1), part(right, 1), to_left),
            Link(sems, base + 4, halves[1], part(own_y, 1), to_right),
            Link(sems, base + 5, halves[0], part(own_y, 0), to_left),
        ]

    def part(self, y, half=None, cols=None):
        if half is None:
            rows = aligned(self.first(y), HALF)
        else:
            rows = aligned(self.first(y) + half * SUB, SUB)
        return self.out.at[rows, self.cols if cols is None else cols]

    def start(self):
        for number in (0, 1, 4, 5):
            self.links[number].start()

    def pass_on(self):
        for near, far in ((0, 2), (1, 3)):
            self.links[near].got()
            self.links[far].start()

    def rest(self):
        self.links[4].got()
        self.links[5].got()

    def opposite(self):
        self.links[2].got()
        self.links[3].got()

    def finish(self):
        for link in self.links:
            link.sent()


class BucketCopy:
    LINKS = 18

    def __init__(self, here, own, out, sems, local_sem, width, cut):
        cut, rest = pl.ds(0, cut), pl.ds(cut, width - cut)
        first_own = lambda y: y * BLK + here.x_hi * HALF
        first_far = lambda y: y * BLK + (1 - here.x_hi) * HALF
        self.near = RingCopy(here, own, out, first_own, pl.ds(0, width), sems, 0)
        far_own = out.at[aligned(first_far(here.y), HALF), cut]
        self.far = RingCopy(here, far_own, out, first_far, cut, sems, RingCopy.LINKS)
        part = self.near.part
        y, right, opp, left, _, _ = here.ring_y()
        moves = [(own.at[:, cut], part(y, cols=cut)), (own.at[:, rest], part(y, cols=rest))]
        for place, half in ((left, None), (right, None), (opp, 0), (opp, 1)):
            moves.append((part(place, half, rest), part(place, half, rest)))
        self.across = [Link(sems, 2 * RingCopy.LINKS + i, src, dst, here.to_x_hi()) for i, (src, dst) in enumerate(moves)]
        self.keep = pltpu.make_async_copy(own, part(y), local_sem)

    def start(self):
        self.near.start()
        self.keep.start()

    def send_cut(self):
        self.across[0].start()

    def send_rest(self):
        self.across[1].start()

    def start_far(self):
        self.across[0].got()
        self.far.start()

    def pass_near(self):
        self.near.pass_on()

    def cross_near(self):
        self.near.rest()
        self.across[2].start()
        self.across[3].start()

    def cross_opp(self):
        for i in range(2):
            self.near.links[2 + i].got()
            self.across[4 + i].start()

    def pass_far(self):
        self.far.pass_on()

    def arrive(self):
        self.far.rest()
        for link in self.across[1:4]:
            link.got()

    def arrive_opposite(self):
        self.far.opposite()
        for link in self.across[4:]:
            link.got()

    def finish(self):
        for link in self.across:
            link.sent()
        self.near.finish()
        self.far.finish()


class GradSum:
    ORDER = (2, 1, 3, 0)
    LINKS = 15

    def __init__(self, here, grads, at, buf_core, buf_ring, buf_last, sems, free_sems):
        self.here, self.grads, self.buf_core, self.buf_last, self.free_sems = here, grads, buf_core, buf_last, free_sems
        self.at = lambda x_lo, z, core: at((x_lo * 4 + z) * 2 + core)
        self.cores = {
            off: [
                Link(
                    sems,
                    turn * 2 + x_lo,
                    grads.at[self.at(x_lo, here.z_at(off), 1 - here.core)],
                    buf_core.at[(turn % 2) * 2 + x_lo],
                    here.to_core(),
                )
                for x_lo in range(2)
            ]
            for turn, off in enumerate(self.ORDER)
        }
        self.ring = RingSum(here.ring_z(), grads, lambda z, half: self.at(half, z, here.core), buf_ring, sems, 8)
        self.other = self.at(1 - here.x_lo, here.z, here.core)
        self.last = Link(sems, 14, grads.at[self.other], buf_last, here.to_x_lo())

    def swap(self, off):
        turn = self.ORDER.index(off)
        if turn >= 2:
            pl.semaphore_wait(self.free_sems.at[turn % 2], 1)
        for link in self.cores[off]:
            link.start()

    def add_core(self, off):
        turn = self.ORDER.index(off)
        for x_lo in range(2):
            self.cores[off][x_lo].got()
            at = self.at(x_lo, self.here.z_at(off), self.here.core)
            self.grads[at] = (
                self.grads[at].astype(f32) + self.buf_core[(turn % 2) * 2 + x_lo].astype(f32)
            ).astype(bf16)
        if turn < 2:
            pl.semaphore_signal(
                self.free_sems.at[turn], inc=1, device_id=self.here.to_core(), device_id_type=MESH
            )

    def cross(self):
        low, high = self.ring.total(0), self.ring.total(1)
        mine = self.here.x_lo == 0
        self.grads[self.other] = jnp.where(mine, high, low).astype(bf16)
        self.last.start()
        return jnp.where(mine, low, high)

    def rest(self):
        self.last.got()
        return self.buf_last[...].astype(f32)

    def finish(self):
        for links in self.cores.values():
            for link in links:
                link.sent()
        self.last.sent()
        self.ring.finish()


class Total:
    def __init__(self, here, steps, bufs, sems):
        self.steps, self.bufs, self.at = steps, bufs, 0
        z_pair, y_pair = here.z + 1 - 2 * (here.z % 2), here.y + 1 - 2 * (here.y % 2)
        targets = [
            here.to_core(), here.to_z(z_pair), here.to_z(3 - here.z), here.to_x_lo(),
            here.to_y(y_pair), here.to_y(3 - here.y), here.to_x_hi(),
        ]
        self.links = [Link(sems, i, steps.at[i], bufs.at[i], target) for i, target in enumerate(targets)]

    def start(self):
        self.links[0].start()

    def step(self):
        i = self.at
        self.links[i].got()
        self.steps[i + 1] = self.steps[i] + self.bufs[i]
        self.at = i + 1
        if self.at < len(self.links):
            self.links[self.at].start()

    def finish(self):
        for link in self.links:
            link.sent()


def gelu_parts(v):
    cdf = 0.5 * (1.0 + lax.erf(v * (1.0 / math.sqrt(2.0))))
    slope = cdf + v * (jnp.exp(-0.5 * v * v) * (1.0 / math.sqrt(2.0 * math.pi)))
    return v * cdf, slope


def row_stats(load, width):
    tiles = width // 128
    total = load(0)
    for tile in range(1, tiles):
        total = total + load(tile)
    mean = jnp.sum(total, axis=-1, keepdims=True) * (1.0 / width)
    square = jnp.zeros_like(total)
    for tile in range(tiles):
        centred = load(tile) - mean
        square = square + centred * centred
    var = jnp.sum(square, axis=-1, keepdims=True) * (1.0 / width)
    return mean, lax.rsqrt(var + norm_eps)


def whole_kernel(
    lens, tok, cot, one_gain_h, one_bias_h, two_gain_h, two_bias_h, turn, freq_h, wq, bq_h, wo, wu, bu_h, wd, bb_h,
    out, gt, packed, tail, b_v, e_v,
    tail_v, tok_v, a_v, w_in, w_out, st, qkv_v, o_v, do_v, tabs, stats, g_v, du_v, rows_own, gt_own,
    z_wide, z_cut, z_x, z_far, s_wide, s_cut, s_x, s_far,
    one_core, one_ring, one_last, two_core, two_ring, two_last, steps, step_bufs,
    one_gain, one_bias, two_gain, two_bias, freq, bq, bu, bb,
    in_sems, st_sems, local_sems, z_sems, s_sems, out_sems, gt_sems, one_sems, two_sems, vec_sems, one_free, two_free,
):
    here = Place()
    rows_all, width = tok_v.shape
    hidden = g_v.shape[1]
    blocks = rows_all // BLK
    scale = 1.0 / math.sqrt(HS)
    qkv_first = hidden

    ring, ring_z = here.ring_y(), here.ring_z()
    greet([ring[4], ring[5], here.to_x_hi(), ring_z[4], ring_z[5], here.to_core(), here.to_x_lo()])

    def block_of(i):
        return pl.ds(i * BLK, BLK)

    def column(k):
        return pl.ds(k * HS, HS)

    tok_in = [pltpu.make_async_copy(tok.at[block_of(i)], tok_v.at[block_of(i)], in_sems.at[i]) for i in range(blocks)]
    cot_in = [pltpu.make_async_copy(cot.at[block_of(i)], e_v.at[block_of(i)], in_sems.at[blocks + i]) for i in range(blocks)]
    own_first = here.y * BLK + here.x_hi * HALF
    x_in = pltpu.make_async_copy(tok.at[aligned(own_first, HALF)], gt_own, in_sems.at[2 * blocks])
    turn_in = pltpu.make_async_copy(turn, tabs, in_sems.at[2 * blocks + 1])

    pieces = [((wq.at[j], (pl.ds(0, width),)),) for j in range(3)]
    pieces += [((wu.at[:, column(k)], (pl.ds(0, width),)),) for k in range(hidden // HS)]
    pieces += [tuple((wo.at[:, column(k)], (column(k),)) for k in range(width // HS))]
    pieces += [
        tuple((wd.at[:, column(k)], (pl.ds((k % 2) * hidden, hidden),)) for k in (2 * j, 2 * j + 1))
        for j in range(width // HS // 2)
    ]
    loads, number = [], 0
    for i, piece in enumerate(pieces):
        copies = []
        for src, (rows,) in piece:
            copies.append(pltpu.make_async_copy(src, st.at[i % SLOTS, rows], st_sems.at[number]))
            number += 1
        loads.append(copies)

    def load(i):
        if i < len(loads):
            for copy in loads[i]:
                copy.start()

    def take(i):
        for copy in loads[i]:
            copy.wait()
        slot = i % SLOTS
        if i < 7:
            first = qkv_first + i * HS if i < 3 else (i - 3) * HS

            @pl.loop(0, width // BLK)
            def _(r):
                rows = aligned(r * BLK, BLK)
                w_in[rows, pl.ds(first, HS)] = st[slot, rows, :].astype(bf16)

        elif i == 7:
            for k in range(width // HS):
                w_out[hidden:, column(k)] = st[slot, column(k), :].astype(bf16)
        else:
            for k in range(2):
                cols = column(2 * (i - 8) + k)

                @pl.loop(0, hidden // BLK)
                def _(r):
                    rows = aligned(r * BLK, BLK)
                    w_out[rows, cols] = st[slot, aligned(k * hidden + r * BLK, BLK), :].astype(bf16)

        load(i + SLOTS)

    small_pairs = [
        (one_gain_h, one_gain), (one_bias_h, one_bias), (two_gain_h, two_gain), (two_bias_h, two_bias),
        (freq_h, freq), (bq_h, bq), (bu_h, bu), (bb_h, bb),
    ]
    small_in = [
        pltpu.make_async_copy(src, dst, in_sems.at[2 * blocks + 2 + i]) for i, (src, dst) in enumerate(small_pairs)
    ]
    tok_in[0].start()
    for copy in small_in:
        copy.start()
    tok_in[1].start()
    for i in range(SLOTS):
        load(i)
    tok_in[2].start()
    turn_in.start()
    tok_in[3].start()

    end = []
    for j in range(4):
        end.append(lens[0, j] + (end[-1] if j else 0))

    def first_of(t):
        low = jnp.zeros_like(t)
        for j in range(4):
            low = jnp.where(t >= end[j], end[j], low)
        return low

    steps[0] = jnp.zeros(steps.shape[1:], f32)

    chunk = 64

    def norms(i):
        rows = aligned(i * BLK, BLK)
        pltpu.make_async_copy(tok.at[rows], tok_v.at[rows], in_sems.at[i]).wait()
        for c in range(BLK // chunk):
            norm_chunk(aligned(i * BLK + c * chunk, chunk))

    def norm_chunk(rows):
        def tile_of(tile):
            return tok_v[rows, pl.ds(tile * 128, 128)].astype(f32)

        mean, rstd = row_stats(tile_of, width)
        stats[rows, 0:1] = mean
        stats[rows, 1:2] = rstd
        for tile in range(width // 128):
            cols = pl.ds(tile * 128, 128)
            normed = (tile_of(tile) - mean) * rstd
            a_v[rows, cols] = (normed * one_gain[:, cols] + one_bias[:, cols]).astype(bf16)
            b_v[rows, cols] = (normed * two_gain[:, cols] + two_bias[:, cols]).astype(bf16)

    def tables():
        starts = [jnp.int32(0)] + end[:3]
        lane_row = lax.broadcasted_iota(jnp.int32, (8, 128), 0)
        shift = jnp.zeros((8, 128), jnp.int32)
        for j in range(4):
            shift = jnp.where(lane_row == j, starts[j], shift)
        phase = shift.astype(f32) * freq[...]
        shift_cos, shift_sin = jnp.cos(phase), jnp.sin(phase)
        turn_in.wait()

        @pl.loop(0, rows_all // HALF)
        def _(i):
            rows = aligned(i * HALF, HALF)
            t = lax.broadcasted_iota(jnp.int32, (HALF, 128), 0) + i * HALF
            lane = lax.broadcasted_iota(jnp.int32, (HALF, 128), 1)
            c_of = jnp.broadcast_to(shift_cos[0:1], (HALF, 128))
            s_of = jnp.broadcast_to(shift_sin[0:1], (HALF, 128))
            for j in range(4):
                c_of = jnp.where(t >= end[j], shift_cos[j + 1 : j + 2], c_of)
                s_of = jnp.where(t >= end[j], shift_sin[j + 1 : j + 2], s_of)
            t_cos, t_sin = tabs[0, rows], tabs[1, rows]
            sin_of = t_sin * c_of - t_cos * s_of
            tabs[0, rows] = t_cos * c_of + t_sin * s_of
            tabs[1, rows] = jnp.where(lane < ROT // 2, -sin_of, sin_of)

    def turned(wide, sign, rows):
        low = wide[:, :128]
        lane = lax.broadcasted_iota(jnp.int32, low.shape, 1)
        other = jnp.where(lane < ROT // 2, pltpu.roll(low, 128 - ROT // 2, 1), pltpu.roll(low, ROT // 2, 1))
        low = low * tabs[0, rows] + sign * (other * tabs[1, rows])
        return jnp.concatenate([low, wide[:, 128:]], axis=1)

    def project(i):
        rows = aligned(i * BLK, BLK)
        mixed = dot_nn(a_v[rows, :], w_in[:, qkv_first:])
        for j in range(3):
            part = mixed[:, j * HS : (j + 1) * HS] + bq[j : j + 1, :]
            qkv_v[rows, column(j)] = (turned(part, 1.0, rows) if j < 2 else part).astype(bf16)

    def probabilities(first, seen):
        rows = aligned(first, BLK)
        t = lax.broadcasted_iota(jnp.int32, (BLK, 1), 0) + first
        key_at = lax.broadcasted_iota(jnp.int32, (BLK, seen), 1)
        scores = dot_nt(qkv_v[rows, :HS], qkv_v[:seen, HS : 2 * HS]) * scale
        scores = jnp.where((key_at >= first_of(t)) & (key_at <= t), scores, masked_value)
        weights = jnp.exp(scores - jnp.max(scores, axis=-1, keepdims=True))
        return weights * (1.0 / jnp.sum(weights, axis=-1, keepdims=True))

    def attend(off):
        first = here.y_at(off) * BLK
        probs = probabilities(first, rows_all).astype(bf16)
        o_v[aligned(first, BLK), :] = dot_nn(probs, qkv_v[:, 2 * HS :]).astype(bf16)

    def mask(i):
        rows = aligned(i * BLK, BLK)
        t = lax.broadcasted_iota(jnp.int32, (BLK, 1), 0) + i * BLK
        used = (t < end[3]).astype(f32)

        @pl.loop(0, width // 512)
        def _(c):
            cols = aligned(c * 512, 512)
            kept = e_v[rows, cols].astype(f32) * used
            e_v[rows, cols] = kept.astype(bf16)
            steps[0, 4:5, cols] += jnp.sum(kept, axis=0, keepdims=True)

    def mask_all():
        for copy in cot_in:
            copy.wait()
        pl.loop(0, blocks)(mask)

    def mixed_back():
        do_v[...] = dot_nt(e_v[...], w_out[hidden:, :]).astype(bf16)

    def attend_back(i):
        rows, seen = block_of(i), (i + 1) * BLK
        query, keys, values = qkv_v[rows, :HS], qkv_v[:seen, HS : 2 * HS], qkv_v[:seen, 2 * HS :]
        probs = probabilities(i * BLK, seen)
        grad_mixed = do_v[rows, :]
        grad_probs = dot_nt(grad_mixed, values)
        row_dot = jnp.sum(probs * grad_probs, axis=-1, keepdims=True)
        grad_scores = (probs * (grad_probs - row_dot)).astype(bf16)
        grad_query = dot_nn(grad_scores, keys) * scale
        grad_keys = dot_tn(grad_scores, query) * scale
        grad_values = dot_tn(probs.astype(bf16), grad_mixed)
        if i == blocks - 1:
            st[0, :seen] = grad_keys
            st[0, pl.ds(rows_all, seen)] = grad_values
        else:
            st[0, :seen] += grad_keys
            st[0, pl.ds(rows_all, seen)] += grad_values
        qkv_v[rows, :HS] = turned(grad_query, -1.0, rows).astype(bf16)

    def project_back():
        for i in range(blocks):
            rows = block_of(i)
            qkv_v[rows, HS : 2 * HS] = turned(st[0, rows], -1.0, rows).astype(bf16)
            qkv_v[rows, 2 * HS :] = st[0, pl.ds(rows_all + i * BLK, BLK)].astype(bf16)
            steps[0, 5:6, : 3 * HS] += jnp.sum(qkv_v[rows, :].astype(f32), axis=0, keepdims=True)

    z_v = a_v
    branch = BucketSum(here, z_v, z_wide, z_cut, z_x, z_far, z_sems, width, BRANCH_CUT)

    def feed_up(off):
        rows = aligned(here.y_at(off) * BLK, BLK)
        act, slope = gelu_parts(dot_nn(b_v[rows, :], w_in[:, :hidden]) + bu[...])
        g_v[rows, :] = act.astype(bf16)
        du_v[rows, :] = slope.astype(bf16)

    def feed_down(off):
        rows = aligned(here.y_at(off) * BLK, BLK)

        @pl.loop(0, 2)
        def _(c):
            cols = aligned(c * (width // 2), width // 2)
            z_v[rows, cols] = (
                dot_nn(o_v[rows, :], w_out[hidden:, cols]) + dot_nn(g_v[rows, :], w_out[:hidden, cols])
            ).astype(bf16)

    def out_rows():
        x_in.wait()
        t = lax.broadcasted_iota(jnp.int32, (SUB, 1), 0) + own_first
        for half in range(2):
            rows = pl.ds(half * SUB, SUB)
            used = (t + half * SUB < end[3]).astype(f32)
            rows_own[rows, :] = (used * (gt_own[rows, :].astype(f32) + branch.total(half) + bb[...])).astype(bf16)

    def attend_up(off):
        attend(off)
        feed_up(off)

    wide = BucketSum(here, tok_v, s_wide, s_cut, s_x, s_far, s_sems, width, NORM_CUT)

    def into_norms(off):
        rows = aligned(here.y_at(off) * BLK, BLK)
        grad_low = (dot_nt(e_v[rows, :], w_out[:hidden, :]) * du_v[rows, :].astype(f32)).astype(bf16)
        du_v[rows, :] = grad_low
        steps[0, 6:7, :hidden] += jnp.sum(grad_low.astype(f32), axis=0, keepdims=True)
        mean, rstd = stats[rows, 0:1], stats[rows, 1:2]

        @pl.loop(0, 4)
        def _(c):
            cols = aligned(c * (width // 4), width // 4)
            da = dot_nt(qkv_v[rows, :], w_in[cols, qkv_first:])
            db = dot_nt(du_v[rows, :], w_in[cols, :hidden])
            normed = (tok_v[rows, cols].astype(f32) - mean) * rstd
            steps[0, 0:1, cols] += jnp.sum(da * normed, axis=0, keepdims=True)
            steps[0, 1:2, cols] += jnp.sum(da, axis=0, keepdims=True)
            steps[0, 2:3, cols] += jnp.sum(db * normed, axis=0, keepdims=True)
            steps[0, 3:4, cols] += jnp.sum(db, axis=0, keepdims=True)
            tok_v[rows, cols] = (da * one_gain[:, cols] + db * two_gain[:, cols]).astype(bf16)

    def gt_rows():
        for half in range(2):
            rows = pl.ds(half * SUB, SUB)
            total = wide.total(half)
            x = gt_own[rows, :].astype(f32)
            centred = x - jnp.mean(x, axis=-1, keepdims=True)
            rstd = lax.rsqrt(jnp.mean(centred * centred, axis=-1, keepdims=True) + norm_eps)
            normed = centred * rstd
            grad = rstd * (
                total - jnp.mean(total, axis=-1, keepdims=True)
                - normed * jnp.mean(total * normed, axis=-1, keepdims=True)
            )
            gt_own[rows, :] = (e_v[aligned(own_first + half * SUB, SUB), :].astype(f32) + grad).astype(bf16)

    one = GradSum(
        here, w_in, lambda block: (aligned(block * HALF, HALF), pl.ds(0, w_in.shape[1])),
        one_core, one_ring, one_last, one_sems, one_free,
    )
    two = GradSum(
        here, w_out, lambda block: (pl.ds(0, w_out.shape[0]), aligned(block * HALF, HALF)),
        two_core, two_ring, two_last, two_sems, two_free,
    )

    def grads_one(off):
        @pl.loop(0, 2)
        def _(x_lo):
            m = aligned((x_lo * 4 + here.z_at(off)) * BLK, BLK)
            w_in[m, :hidden] = dot_tn(b_v[:, m], du_v[...]).astype(bf16)
            w_in[m, qkv_first:] = dot_tn(a_v[:, m], qkv_v[...]).astype(bf16)

    def grads_two(off):
        @pl.loop(0, 2)
        def _(x_lo):
            m = aligned((x_lo * 4 + here.z_at(off)) * BLK, BLK)
            w_out[:hidden, m] = dot_tn(g_v[...], e_v[:, m]).astype(bf16)
            w_out[hidden:, m] = dot_tn(o_v[...], e_v[:, m]).astype(bf16)

    def pack_one(part, add):
        for j in range(w_in.shape[1] // HS):
            rows = pl.ds(j * HALF, HALF)
            tile = part[:, j * HS : (j + 1) * HS]
            st[1, rows, :] = st[1, rows, :] + tile if add else tile

    def pack_two(part, add):
        tall = w_out.shape[0] // 2
        rows = pl.ds((w_in.shape[1] // HS) * HALF, tall)
        both = jnp.concatenate([part[:tall], part[tall:]], axis=1)
        st[1, rows, :] = st[1, rows, :] + both if add else both

    def cross_one():
        pack_one(one.cross(), False)

    def rest_one():
        pack_one(one.rest(), True)

    def cross_two():
        pack_two(two.cross(), False)

    def rest_two():
        pack_two(two.rest(), True)

    gather_out = BucketCopy(here, rows_own, out, out_sems, local_sems.at[1], width, OUT_CUT)
    gather_gt = BucketCopy(here, gt_own, gt, gt_sems, local_sems.at[2], width, GRAD_CUT)
    small = Total(here, steps, step_bufs, vec_sems)
    a_in = pltpu.make_async_copy(tok, a_v, local_sems.at[3])

    def renew():
        a_in.wait()

        @pl.loop(0, rows_all // chunk)
        def _(c):
            rows = aligned(c * chunk, chunk)
            mean, rstd = stats[rows, 0:1], stats[rows, 1:2]
            for tile in range(width // 128):
                cols = pl.ds(tile * 128, 128)
                normed = (a_v[rows, cols].astype(f32) - mean) * rstd
                a_v[rows, cols] = (normed * one_gain[:, cols] + one_bias[:, cols]).astype(bf16)

    for copy in small_in:
        copy.wait()

    def after_norms(i):
        if i == 1:
            tables()
        for k in ((0,), (1, 2), (3, 4), (5, 6))[i]:
            take(k)

    @pl.loop(0, blocks)
    def _(i):
        norms(i)
        for k in range(blocks):
            pl.when(i == k)(partial(after_norms, k))


    @pl.loop(0, blocks)
    def _(i):
        project(i)
        for k in range(3):
            pl.when(i == k)(partial(take, 7 + k))

    def first_feed():
        take(11)
        for copy in cot_in + [x_in]:
            copy.start()
        await_greetings(7)

    def feed(off):
        attend_up(off)
        pl.when(off == 2)(first_feed)
        feed_down(off)

    take(10)
    out_done = pltpu.make_async_copy(out, e_v, local_sems.at[5])

    def gt_copies(x_hi, first_sem):
        parts = [aligned(here.y_at(off) * BLK + x_hi * HALF, HALF) for off in range(4)]
        return [pltpu.make_async_copy(gt.at[part], b_v.at[part], local_sems.at[first_sem + i]) for i, part in enumerate(parts)]

    gt_near, gt_far = gt_copies(here.x_hi, 6), gt_copies(1 - here.x_hi, 10)

    def finish_out():
        gather_out.arrive()
        gather_out.arrive_opposite()
        gather_out.finish()
        gather_out.keep.wait()
        out_done.start()

    def near_done():
        gather_gt.keep.wait()
        for copy in gt_near:
            copy.start()

    in_turn(
        feed,
        [branch.across[2].start, branch.far.send_opp],
        [branch.across[1].start, branch.far.send_right],
        [branch.across[3].start, branch.far.send_left, branch.far.relay],
        [branch.across[0].start],
    )
    branch.add_across(2)
    branch.near.send_opp()
    mask_all()
    mixed_back()
    attend_back(3)
    branch.add_across(1)
    branch.near.send_right()
    attend_back(2)
    branch.add_across(3)
    branch.near.send_left()
    attend_back(1)
    attend_back(0)
    project_back()
    branch.pass_far()
    in_turn(
        into_norms,
        [wide.across[2].start, wide.far.send_opp, partial(branch.add_across, 0), branch.near.relay],
        [wide.across[1].start, wide.far.send_right],
        [wide.across[3].start, wide.far.send_left],
        [wide.across[0].start],
    )
    small.start()
    wide.add_across(2)
    wide.near.send_opp()
    wide.far.relay()
    in_turn(
        grads_two,
        [partial(two.swap, 2), out_rows, small.step],
        [partial(two.swap, 1), gather_out.start, gather_out.send_cut, branch.finish, a_in.start, partial(two.add_core, 2), two.ring.send_opp, partial(wide.add_across, 1), wide.near.send_right],
        [partial(two.swap, 3), partial(two.add_core, 1), two.ring.send_right, partial(wide.add_across, 3), wide.near.send_left, renew],
        [partial(two.swap, 0)],
    )
    wide.add_across(0)
    small.step()
    two.add_core(3)
    two.ring.send_left()
    wide.pass_far()
    in_turn(
        grads_one,
        [partial(one.swap, 2)],
        [partial(one.swap, 1), gather_out.send_rest, partial(one.add_core, 2), one.ring.send_opp, wide.near.relay, small.step, gather_out.pass_near, gather_out.cross_near, partial(two.add_core, 0)],
        [partial(one.swap, 3), two.ring.relay, gt_rows, gather_gt.send_rest, gather_gt.send_cut, small.step, gather_gt.start, partial(one.add_core, 1), one.ring.send_right, partial(one.add_core, 3), one.ring.send_left, gather_out.start_far, cross_two],
        [partial(one.swap, 0)],
    )
    small.step()
    gather_out.cross_opp()
    one.ring.relay()
    gather_out.pass_far()
    one.add_core(0)
    gather_gt.pass_near()
    gather_gt.cross_near()
    gather_gt.start_far()
    small.step()
    cross_one()
    gather_gt.pass_far()
    gather_gt.cross_opp()
    near_done()
    small.step()
    rest_two()
    rest_one()
    finish_out()
    tail_v[...] = jnp.zeros_like(tail_v)
    tail_v[0:4, :HS] = steps[7, 0:4, aligned(here.mp * HS, HS)]
    tail_v[4:5, :HS] = steps[4, 4:5, aligned(here.mp * HS, HS)]
    tail_v[5:6, : 3 * HS] = steps[4, 5:6, : 3 * HS]
    tail_v[6:7, :hidden] = steps[4, 6:7, :hidden]
    tail_out = pltpu.make_async_copy(tail_v, tail, local_sems.at[0])
    tail_out.start()
    packed_out = pltpu.make_async_copy(st.at[1, pl.ds(0, packed.shape[0])], packed, local_sems.at[4])
    packed_out.start()
    wide.finish()
    one.finish()
    two.finish()
    small.finish()
    gather_gt.arrive()
    for off in (0, 1, 3):
        gt_far[off].start()
    gather_gt.arrive_opposite()
    gt_far[2].start()
    gather_gt.finish()
    for copy in [tail_out, packed_out, out_done] + gt_near + gt_far:
        copy.wait()


def any_space():
    return pl.BlockSpec(memory_space=pl.ANY)


def vmem_space():
    return pl.BlockSpec(memory_space=pltpu.VMEM)


def rotary_tables(rows):
    inverse = np.exp(np.arange(ROT // 2) * (-2.0 * math.log(10000.0) / ROT))
    angle = np.arange(rows)[:, None] * inverse[None, :]
    cos_of, sin_of = np.ones((rows, 128)), np.zeros((rows, 128))
    freq = np.zeros((8, 128))
    for first in (0, ROT // 2):
        part = slice(first, first + ROT // 2)
        cos_of[:, part], sin_of[:, part] = np.cos(angle), np.sin(angle)
        freq[:, part] = inverse
    return np.stack([cos_of, sin_of]).astype(np.float32), freq.astype(np.float32)


def whole(lengths, tokens, cotangent, norms, wq, bq, wo, wu, bu, wd, bb):
    rows, width = tokens.shape
    hidden = wu.shape[1]
    turn, freq = rotary_tables(rows)
    shape = jax.ShapeDtypeStruct
    wide_in, tall_out = hidden + 3 * HS, hidden + HS
    outs = (
        shape((rows, width), bf16),
        shape((rows, width), bf16),
        shape((wide_in // HS * HALF + tall_out // 2, HS), f32),
        shape((8, hidden), f32),
        pltpu.VMEM((rows, width), bf16),
        pltpu.VMEM((rows, width), bf16),
    )
    v = pltpu.VMEM
    dma = pltpu.SemaphoreType.DMA

    def sum_bufs(cut):
        return [v((6, SUB, width), bf16), v((6, SUB, cut), bf16), v((4, HALF, width - cut), bf16), v((HALF, cut), bf16)]

    def grad_bufs(*part):
        return [v((4, *part), bf16), v((6, *part), bf16), v(part, bf16)]

    return pl.pallas_call(
        whole_kernel,
        out_shape=outs,
        in_specs=[pl.BlockSpec(memory_space=pltpu.SMEM)] + [any_space()] * 15,
        out_specs=(any_space(),) * 4 + (vmem_space(),) * 2,
        scratch_shapes=[
            v((8, hidden), f32), v((rows, width), bf16), v((rows, width), bf16),
            v((width, wide_in), bf16), v((tall_out, width), bf16), v((SLOTS, width, HS), f32), v((rows, 3 * HS), bf16),
            v((rows, HS), bf16), v((rows, HS), bf16), v((2, rows, 128), f32), v((rows, 2), f32),
            v((rows, hidden), bf16), v((rows, hidden), bf16),
            v((HALF, width), bf16), v((HALF, width), bf16),
            *sum_bufs(BRANCH_CUT), *sum_bufs(NORM_CUT), *grad_bufs(HALF, wide_in), *grad_bufs(tall_out, HALF),
            v((8, 8, width), f32), v((7, 8, width), f32),
            *[v((1, width), f32)] * 4, v((8, 128), f32), v((3, HS), f32), v((1, hidden), f32), v((1, width), f32),
            dma((18,)), dma((23,)), dma((14,)), dma((2, BucketSum.LINKS)), dma((2, BucketSum.LINKS)),
            dma((2, BucketCopy.LINKS)), dma((2, BucketCopy.LINKS)), dma((2, GradSum.LINKS)), dma((2, GradSum.LINKS)),
            dma((2, 7)), pltpu.SemaphoreType.REGULAR((2,)), pltpu.SemaphoreType.REGULAR((2,)),
        ],
        compiler_params=pltpu.CompilerParams(
            collective_id=0, has_side_effects=True, vmem_limit_bytes=55 * MIB + 768 * 1024
        ),
        name="whole",
    )(lengths, tokens, cotangent, *norms, turn, freq, wq, bq, wo, wu, bu, wd, bb)


def finish_kernel(
    gathered, gathered_grad, packed, tail,
    output, grad_tokens, up, down, qkv, out, one_gain, one_bias, two_gain, two_bias, qkv_bias, up_bias, bias,
    packed_v, tail_v, in_sems, out_sems,
):
    pieces = up.shape[1] // HS
    first = (pieces + 3) * HALF
    tall = (down.shape[0] + out.shape[0]) // 2
    over = down.shape[0] - tall
    left, right = pl.ds(0, HALF), pl.ds(HALF, HALF)
    parts = gathered.shape[0] // HALF
    moves, back = [(tail, tail_v), (packed, packed_v)], []
    for src, dst in ((gathered, output), (gathered_grad, grad_tokens)):
        for k in range(parts):
            part = pl.ds(k * HALF, HALF)
            back.append((src.at[part], dst.at[part]))
    back += [(packed_v.at[pl.ds(j * HALF, HALF)], up.at[:, pl.ds(j * HS, HS)]) for j in range(pieces)]
    back += [(packed_v.at[pl.ds((pieces + j) * HALF, HALF)], qkv.at[j]) for j in range(3)]
    back += [
        (packed_v.at[pl.ds(first, tall), left], down.at[pl.ds(0, tall)]),
        (packed_v.at[pl.ds(first, over), right], down.at[pl.ds(tall, over)]),
        (packed_v.at[pl.ds(first + over, tall - over), right], out),
    ]
    loads = [pltpu.make_async_copy(src, dst, in_sems.at[i]) for i, (src, dst) in enumerate(moves)]
    stores = [pltpu.make_async_copy(src, dst, out_sems.at[i]) for i, (src, dst) in enumerate(back)]
    for copy in loads:
        copy.start()
    for store in stores[: 2 * parts]:
        store.start()
    loads[0].wait()
    for row, ref in enumerate((one_gain, one_bias, two_gain, two_bias, bias)):
        ref[...] = tail_v[row, :HS]
    for j in range(3):
        qkv_bias[j : j + 1, :] = tail_v[5:6, pl.ds(j * HS, HS)]
    up_bias[...] = tail_v[6, :]
    loads[1].wait()
    for store in stores[2 * parts :]:
        store.start()
    for store in stores:
        store.wait()


def finish(gathered, gathered_grad, packed, tail):
    rows, width = gathered.shape
    hidden = tail.shape[1]
    shape = jax.ShapeDtypeStruct
    dma = pltpu.SemaphoreType.DMA
    moves = 2 * rows // HALF
    return pl.pallas_call(
        finish_kernel,
        out_shape=(
            shape(gathered.shape, bf16), shape(gathered.shape, bf16),
            shape((HALF, hidden), f32), shape((hidden, HALF), f32), shape((3, HALF, HS), f32), shape((HS, HALF), f32),
            shape((HS,), f32), shape((HS,), f32), shape((HS,), f32), shape((HS,), f32),
            shape((3, HS), f32), shape((hidden,), f32), shape((HS,), f32),
        ),
        in_specs=[any_space()] * 4,
        out_specs=(any_space(),) * 6 + (vmem_space(),) * 7,
        scratch_shapes=[
            pltpu.VMEM(packed.shape, f32), pltpu.VMEM(tail.shape, f32),
            dma((2,)), dma((moves + hidden // HS + 6,)),
        ],
        compiler_params=pltpu.CompilerParams(vmem_limit_bytes=16 * MIB),
        name="finish",
    )(
        pltpu.with_memory_space_constraint(gathered, pltpu.VMEM),
        pltpu.with_memory_space_constraint(gathered_grad, pltpu.VMEM),
        pltpu.with_memory_space_constraint(packed, pltpu.HBM),
        pltpu.with_memory_space_constraint(tail, pltpu.HBM),
    )


def local(
    tokens, lengths, ln1_gain, ln1_bias, ln2_gain, ln2_bias, qkv_master, qkv_bias, out_master, up_master, up_bias,
    down_master, branch_bias, cotangent,
):
    norms = [vector.reshape(1, -1) for vector in (ln1_gain, ln1_bias, ln2_gain, ln2_bias)]
    w_qkv = jnp.transpose(qkv_master, (1, 0, 2))
    _, _, packed, tail, gathered_grad, gathered = whole(
        lengths, tokens, cotangent, norms, w_qkv, qkv_bias, out_master, up_master,
        up_bias.reshape(1, -1), down_master, branch_bias.reshape(1, -1),
    )
    (
        output, grad_tokens, up, down, qkv, out, one_gain, one_bias, two_gain, two_bias,
        qkv_bias_sum, up_bias_sum, bias_sum,
    ) = finish(gathered, gathered_grad, packed, tail)
    return (
        output,
        grad_tokens,
        one_gain,
        one_bias,
        two_gain,
        two_bias,
        jnp.transpose(qkv, (1, 0, 2)),
        qkv_bias_sum,
        out,
        up,
        up_bias_sum,
        down,
        bias_sum,
    )


def solution(mesh):
    placed = (
        P("dp", None),
        P("dp", None),
        P(),
        P(),
        P(),
        P(),
        P(None, None, "mp"),
        P(None, "mp"),
        P("mp", None),
        P(None, "mp"),
        P("mp"),
        P("mp", None),
        P(),
        P("dp", None),
    )
    return jax.shard_map(
        local,
        mesh=mesh,
        in_specs=placed,
        out_specs=(
            P("dp", None),
            P("dp", None),
            P("mp"),
            P("mp"),
            P("mp"),
            P("mp"),
            P("dp", None, "mp"),
            P(None, "mp"),
            P("mp", "dp"),
            P("dp", "mp"),
            P("mp"),
            P("mp", "dp"),
            P("mp"),
        ),
        check_vma=False,
    )
```
